32 devices in a mesh: dp: 4 (over y, core), seq: 4 (over z), mp: 2 (over x).
Axes of the slice: x: 2, y: 2, z: 4, core: 2. Of those that a mesh axis runs over, the one named last changes fastest.
Arguments:
- trunk_in: bfloat16 [12, 1536, 1536], P('dp', 'seq'), may hold values from -6 to 6
- norm1_gain: float32 [1536], replicated, may hold values from 0.5 to 1.5
- norm1_bias: float32 [1536], replicated, may hold values from -1.75 to 1.75
- w_query: bfloat16 [1536, 512], P(None, 'mp'), may hold values from -0.15625 to 0.15625
- w_key: bfloat16 [1536, 512], P(None, 'mp'), may hold values from -0.15625 to 0.15625
- w_value: bfloat16 [1536, 1536], P(None, 'mp'), may hold values from -0.15625 to 0.15625
- w_rel: bfloat16 [192, 512], P(None, 'mp'), may hold values from -0.4375 to 0.4375
- content_bias: float32 [8, 64], P('mp'), may hold values from -1.25 to 1.25
- pos_bias: float32 [8, 64], P('mp'), may hold values from -1.25 to 1.25
- w_out: bfloat16 [1536, 1536], P('mp'), may hold values from -4 to 4
- b_out: float32 [1536], replicated, may hold values from -1.75 to 1.75
- norm2_gain: float32 [1536], replicated, may hold values from 0.5 to 1.5
- norm2_bias: float32 [1536], replicated, may hold values from -1.75 to 1.75
- w_in: bfloat16 [1536, 3072], P(None, 'mp'), may hold values from -0.15625 to 0.15625
- b_in: float32 [3072], P('mp'), may hold values from -1.75 to 1.75
- w_hid: bfloat16 [3072, 1536], P('mp'), may hold values from -0.109375 to 0.109375
- b_hid: float32 [1536], replicated, may hold values from -1.75 to 1.75
- head_human: bfloat16 [1536, 5313], P('mp'), may hold values from -0.15625 to 0.15625
- bias_human: float32 [5313], replicated, may hold values from -3 to 3
- head_mouse: bfloat16 [1536, 1643], P('mp'), may hold values from -0.15625 to 0.15625
- bias_mouse: float32 [1643], replicated, may hold values from -3 to 3
- species: int32 [12], P('dp'), may hold values from 0 to 1
- targets_human: int32 [12, 1536, 5313], P('dp', 'seq'), may hold values from 0 to 5
- targets_mouse: int32 [12, 1536, 1643], P('dp', 'seq'), may hold values from 0 to 5
Outputs:
- trunk_out: float32 [12, 1536, 1536], P('dp', 'seq')
- loss: float32 [], replicated
- grad_trunk_in: float32 [12, 1536, 1536], P('dp', 'seq')
- grad_norm1_gain: float32 [1536], P(('dp', 'seq'))
- grad_norm1_bias: float32 [1536], P(('dp', 'seq'))
- grad_w_query: float32 [1536, 512], P(('dp', 'seq'), 'mp')
- grad_w_key: float32 [1536, 512], P(('dp', 'seq'), 'mp')
- grad_w_value: float32 [1536, 1536], P(('dp', 'seq'), 'mp')
- grad_w_rel: float32 [192, 512], P(('dp', 'seq'), 'mp')
- grad_content_bias: float32 [8, 64], P('mp', ('dp', 'seq'))
- grad_pos_bias: float32 [8, 64], P('mp', ('dp', 'seq'))
- grad_w_out: float32 [1536, 1536], P('mp', ('dp', 'seq'))
- grad_b_out: float32 [1536], P(('dp', 'seq'))
- grad_norm2_gain: float32 [1536], P(('dp', 'seq'))
- grad_norm2_bias: float32 [1536], P(('dp', 'seq'))
- grad_w_in: float32 [1536, 3072], P(('dp', 'seq'), 'mp')
- grad_b_in: float32 [3072], P('mp')
- grad_w_hid: float32 [3072, 1536], P('mp', ('dp', 'seq'))
- grad_b_hid: float32 [1536], P(('dp', 'seq'))
- grad_head_human: float32 [1536, 5313], P('mp')
- grad_bias_human: float32 [5313], replicated
- grad_head_mouse: float32 [1536, 1643], P('mp')
- grad_bias_mouse: float32 [1643], replicated
The draws below stay inside these ranges and needn't reach their ends.
Inputs may be any that keep to these rules, and one draw needn't show every extreme that they name: `species`: 0 selects the human head, 1 the mouse head. `targets_human`: only the central 896 bins of a window are scored. `targets_mouse`: only the central 896 bins of a window are scored.
All inputs are finite; a program needn't handle non-finite values.
Results may differ from the reference program's by a relative error of at most 0.012.
The reference program's roundings to bfloat16 on the way count: a program that leaves them out, or rounds other values in their place, can miss the bound.
Values may be sent and summed in bfloat16 or wider, within the bound.
No kernel may reach another device: no remote copies, remote signals or barrier semaphores. Data moves between devices by JAX's collectives and lax.ppermute only.
A program may use at most 448 MiB of HBM per device.

```python
import math
import jax
import jax.numpy as jnp
from jax import lax

D = 1536
H = 8
KD = 64
VD = 192
FEAT = 192
FF = 3072
TH = 5313
TM = 1643
BINS = 1536
CROP = 896
WINDOWS = 12


def place_ends(values, own_key, low, top_value):
    dims = values.shape
    place = [jax.random.randint(jax.random.fold_in(own_key, axis), (), 0, dims[axis]) for axis in range(len(dims))]
    values = values.at[tuple(place)].set(low)
    longest = dims.index(max(dims))
    place[longest] = (place[longest] + 1) % dims[longest]
    return values.at[tuple(place)].set(top_value)


def levels(stream_key, dims, cuts, smallest, high):
    loudness = 1.0
    for dim, blocks in cuts:
        draws = jax.random.uniform(jax.random.fold_in(jax.random.fold_in(stream_key, 6), dim), (blocks,), jnp.float32, smallest / len(cuts), high / len(cuts))
        loudness = loudness * jnp.repeat(jnp.exp(draws), dims[dim] // blocks).reshape((-1,) + (1,) * (len(dims) - 1 - dim))
    return loudness


def normal_values(key, dims, width, bound, cuts=(), kind=jnp.bfloat16):
    array = jax.random.normal(key, dims, jnp.float32) * width
    if len(cuts) > 0:
        array = levels(key, dims, cuts, -0.22, 0.18) * array
    return jnp.clip(array, min=-bound, max=bound).astype(kind)


def setup_inputs(seed: int = 0) -> dict:
    key_list = jax.random.split(jax.random.key(seed), 25)
    trunk_in = normal_values(key_list[0], (WINDOWS, BINS, D), 1.0, 6.0, ((0, 4), (1, 4)))
    norm1_gain = jnp.clip(1.0 + 0.1 * jax.random.normal(key_list[1], (D,), jnp.float32), 0.5, 1.5)
    norm1_bias = normal_values(key_list[2], (D,), 0.3, 1.75, (), jnp.float32)
    w_query = normal_values(key_list[3], (D, H * KD), D ** -0.5, 0.15625, ((1, 2),))
    w_key = normal_values(key_list[4], (D, H * KD), D ** -0.5, 0.15625, ((1, 2),))
    w_value = normal_values(key_list[5], (D, H * VD), D ** -0.5, 0.15625, ((1, 2),))
    w_rel = normal_values(key_list[6], (FEAT, H * KD), FEAT ** -0.5, 0.4375, ((1, 2),))
    content_bias = normal_values(key_list[7], (H, KD), 0.2, 1.25, ((0, 2),), jnp.float32)
    pos_bias = normal_values(key_list[8], (H, KD), 0.2, 1.25, ((0, 2),), jnp.float32)
    w_out = normal_values(key_list[9], (H * VD, D), 2 ** -0.5, 4.0, ((0, 2),))
    b_out = normal_values(key_list[10], (D,), 0.3, 1.75, (), jnp.float32)
    norm2_gain = jnp.clip(1.0 + 0.1 * jax.random.normal(key_list[11], (D,), jnp.float32), 0.5, 1.5)
    norm2_bias = normal_values(key_list[12], (D,), 0.3, 1.75, (), jnp.float32)
    w_in = normal_values(key_list[13], (D, FF), D ** -0.5, 0.15625, ((1, 2),))
    b_in = normal_values(key_list[14], (FF,), 0.3, 1.75, ((0, 2),), jnp.float32)
    w_hid = normal_values(key_list[15], (FF, D), FF ** -0.5, 0.109375, ((0, 2),))
    b_hid = normal_values(key_list[16], (D,), 0.3, 1.75, (), jnp.float32)
    head_human = normal_values(key_list[17], (D, TH), D ** -0.5, 0.15625, ((0, 2),))
    bias_human = normal_values(key_list[18], (TH,), 0.5, 3.0, (), jnp.float32)
    head_mouse = normal_values(key_list[19], (D, TM), D ** -0.5, 0.15625, ((0, 2),))
    bias_mouse = normal_values(key_list[20], (TM,), 0.5, 3.0, (), jnp.float32)
    species = place_ends(jax.random.randint(key_list[21], (WINDOWS,), 0, 2), jax.random.fold_in(key_list[21], 1), 0, 1).astype(jnp.int32)
    targets_human = place_ends(jax.random.randint(key_list[22], (WINDOWS, BINS, TH), 0, 6), jax.random.fold_in(key_list[22], 1), 0, 5).astype(jnp.int32)
    targets_mouse = place_ends(jax.random.randint(key_list[23], (WINDOWS, BINS, TM), 0, 6), jax.random.fold_in(key_list[23], 1), 0, 5).astype(jnp.int32)
    return dict(trunk_in=trunk_in, norm1_gain=norm1_gain, norm1_bias=norm1_bias, w_query=w_query, w_key=w_key, w_value=w_value, w_rel=w_rel, content_bias=content_bias, pos_bias=pos_bias, w_out=w_out, b_out=b_out, norm2_gain=norm2_gain, norm2_bias=norm2_bias, w_in=w_in, b_in=b_in, w_hid=w_hid, b_hid=b_hid, head_human=head_human, bias_human=bias_human, head_mouse=head_mouse, bias_mouse=bias_mouse, species=species, targets_human=targets_human, targets_mouse=targets_mouse)


norm_eps = 1e-05
log_eps = 1e-07
exact_mode = lax.Precision.HIGHEST

@jax.custom_vjp
def low(v):
    return lax.optimization_barrier(v.astype(jnp.bfloat16)).astype(jnp.float32)

@jax.custom_vjp
def low_back(v):
    return v

def low_keep(v):
    return (low(v), None)

def low_pass(kept, grad):
    return (grad,)

def back_keep(v):
    return (v, None)

def back_low(kept, grad):
    return (low(grad),)
low.defvjp(low_keep, low_pass)
low_back.defvjp(back_keep, back_low)

def rel_basis():
    per_class = FEAT // 6
    distance = jnp.arange(-(BINS - 1), BINS).astype(jnp.float32)
    magnitude = jnp.abs(distance)[:, None]
    half_life = (2.0 ** jnp.linspace(3.0, math.log2(BINS), per_class)).astype(jnp.float32)
    decays = jnp.exp(-math.log(2.0) / half_life[None, :] * magnitude)
    widths = (2.0 ** jnp.arange(1, per_class + 1)).astype(jnp.float32) - 1.0
    central = (widths[None, :] > magnitude).astype(jnp.float32)
    spread = BINS / (2.0 * per_class)
    centre = jnp.linspace(BINS / per_class, BINS, per_class).astype(jnp.float32)
    concentration = (centre / spread) ** 2
    rate_param = centre / spread ** 2
    peak_at = (concentration - 1.0) / rate_param
    log_ratio = (concentration - 1.0) * (jnp.log(jnp.maximum(magnitude, 1e-20)) - jnp.log(peak_at)) - rate_param * (magnitude - peak_at)
    density = jnp.exp(log_ratio)
    gammas = density / lax.optimization_barrier(jnp.max(density, axis=0, keepdims=True))
    symmetric = jnp.concatenate([decays, central, gammas], axis=1)
    return jnp.concatenate([symmetric, jnp.sign(distance)[:, None] * symmetric], axis=1)

def rel_shift(logits, key_count):
    query_count = logits.shape[-2]
    span_width = logits.shape[-1]
    leading = logits.shape[:-2]
    padded = jnp.pad(logits, [(0, 0)] * len(leading) + [(0, 0), (0, 1)])
    flattened = padded.reshape(leading + (query_count * (span_width + 1),))
    flattened = flattened[..., query_count - 1:query_count - 1 + query_count * span_width]
    return flattened.reshape(leading + (query_count, span_width))[..., :key_count]

def layer_norm(values, norm_gain, norm_bias):
    centred = values - lax.optimization_barrier(jnp.mean(values, axis=-1, keepdims=True))
    variance = lax.optimization_barrier(jnp.mean(centred * centred, axis=-1, keepdims=True))
    return centred * lax.rsqrt(variance + norm_eps) * norm_gain + norm_bias

def soft_plus(logits):
    return jnp.maximum(logits, 0.0) + jnp.log1p(jnp.exp(-jnp.abs(logits)))

def reference(trunk_in, norm1_gain, norm1_bias, w_query, w_key, w_value, w_rel, content_bias, pos_bias, w_out, b_out, norm2_gain, norm2_bias, w_in, b_in, w_hid, b_hid, head_human, bias_human, head_mouse, bias_mouse, species, targets_human, targets_mouse):
    floats = tuple((item.astype(jnp.float32) for item in (trunk_in, norm1_gain, norm1_bias, w_query, w_key, w_value, w_rel, content_bias, pos_bias, w_out, b_out, norm2_gain, norm2_bias, w_in, b_in, w_hid, b_hid, head_human, bias_human, head_mouse, bias_mouse)))
    basis = rel_basis()
    crop_start = (BINS - CROP) // 2
    loss_scale = 1.0 / math.sqrt(WINDOWS * CROP)
    key_scale = KD ** (-0.5)

    def forward(trunk, gain_one, offset_one, wquery, wkey, wvalue, wrel, cbias, pbias, wout, bout, gain_two, offset_two, weight_in, bias_in, weight_hid, bias_hid, whead_h, bhead_h, whead_m, bhead_m):
        relative = low(jnp.dot(basis, wrel, precision=exact_mode)).reshape(2 * BINS - 1, H, KD)

        def one_window(total, inputs):
            window_x, kind_id, target_h, target_m = inputs
            normed = low(layer_norm(window_x, gain_one, offset_one))
            query_raw = low_back(jnp.dot(normed, wquery, precision=exact_mode))
            keys = low(low_back(jnp.dot(normed, wkey, precision=exact_mode))).reshape(BINS, H, KD)
            values = low(low_back(jnp.dot(normed, wvalue, precision=exact_mode))).reshape(BINS, H, VD)
            query_scaled = query_raw.reshape(BINS, H, KD) * key_scale
            query_content = low(query_scaled + cbias)
            query_pos = low(query_scaled + pbias)
            content = jnp.einsum('qhd,khd->hqk', query_content, keys, precision=exact_mode)
            position = jnp.einsum('qhd,rhd->hqr', query_pos, relative, precision=exact_mode)
            scores = low_back(content + rel_shift(position, BINS))
            weights = jnp.exp(scores - lax.optimization_barrier(jnp.max(scores, axis=-1, keepdims=True)))
            probs = weights / lax.optimization_barrier(jnp.sum(weights, axis=-1, keepdims=True))
            attended = jnp.einsum('hqk,khd->qhd', low(probs), values, precision=exact_mode).reshape(BINS, H * VD)
            attended = low(low_back(attended))
            branch = low_back(jnp.dot(attended, wout, precision=exact_mode)) + bout
            mid = window_x + branch
            normed_two = low(layer_norm(mid, gain_two, offset_two))
            preact = low_back(jnp.dot(normed_two, weight_in, precision=exact_mode)) + bias_in
            active = low(jnp.maximum(preact, 0.0))
            mlp_out = low_back(jnp.dot(active, weight_hid, precision=exact_mode)) + bias_hid
            output = mid + mlp_out
            cropped = low(output[crop_start:crop_start + CROP])
            logit_h = low_back(jnp.dot(cropped, whead_h, precision=exact_mode)) + bhead_h
            logit_m = low_back(jnp.dot(cropped, whead_m, precision=exact_mode)) + bhead_m
            pred_h = soft_plus(logit_h)
            pred_m = soft_plus(logit_m)
            count_h = target_h[crop_start:crop_start + CROP].astype(jnp.float32)
            count_m = target_m[crop_start:crop_start + CROP].astype(jnp.float32)
            loss_h = jnp.sum(pred_h - count_h * jnp.log(pred_h + log_eps))
            loss_m = jnp.sum(pred_m - count_m * jnp.log(pred_m + log_eps))
            window_loss = jnp.where(kind_id == 0, loss_h, loss_m) * loss_scale
            return (total + window_loss, output)
        loss_total, outputs = lax.scan(jax.checkpoint(one_window), jnp.zeros((), jnp.float32), (trunk, species, targets_human, targets_mouse))
        return (loss_total, outputs)
    loss_value, pullback, trunk_out = jax.vjp(forward, *floats, has_aux=True)
    grads = pullback(jnp.ones((), jnp.float32))
    return (trunk_out, loss_value, grads[0], grads[1], grads[2], grads[3], grads[4], grads[5], grads[6], grads[7], grads[8], grads[9], grads[10], grads[11], grads[12], grads[13], grads[14], grads[15], grads[16], grads[17], grads[18], grads[19], grads[20])
```

```python
import math

import jax
import jax.numpy as jnp
from jax import lax
from jax.experimental import pallas as pl
from jax.experimental.pallas import tpu as pltpu
from jax.sharding import PartitionSpec as P

KD = 64
VD = 192
FEAT = 192
BINS = 1536
CROP = 896


norm_eps = 1e-05
log_eps = 1e-07
exact_mode = lax.Precision.HIGHEST


def rel_basis():
    per_class = FEAT // 6
    distance = jnp.arange(-(BINS - 1), BINS).astype(jnp.float32)
    magnitude = jnp.abs(distance)[:, None]
    half_life = (2.0 ** jnp.linspace(3.0, math.log2(BINS), per_class)).astype(jnp.float32)
    decays = jnp.exp(-math.log(2.0) / half_life[None, :] * magnitude)
    widths = (2.0 ** jnp.arange(1, per_class + 1)).astype(jnp.float32) - 1.0
    central = (widths[None, :] > magnitude).astype(jnp.float32)
    spread = BINS / (2.0 * per_class)
    centre = jnp.linspace(BINS / per_class, BINS, per_class).astype(jnp.float32)
    concentration = (centre / spread) ** 2
    rate_param = centre / spread**2
    peak_at = (concentration - 1.0) / rate_param
    log_ratio = (concentration - 1.0) * (
        jnp.log(jnp.maximum(magnitude, 1e-20)) - jnp.log(peak_at)
    ) - rate_param * (magnitude - peak_at)
    density = jnp.exp(log_ratio)
    gammas = density / jnp.max(density, axis=0, keepdims=True)
    symmetric = jnp.concatenate([decays, central, gammas], axis=1)
    return jnp.concatenate([symmetric, jnp.sign(distance)[:, None] * symmetric], axis=1)


PACK = VD + 3 * KD
GRAD_PACK = VD + 2 * KD
TILE = 896
NN = (((1,), (0,)), ((), ()))
NT = (((1,), (1,)), ((), ()))
TN = (((0,), (0,)), ((), ()))


def mxu(left_arr, right_arr, dims, precision=None):
    return lax.dot_general(
        left_arr, right_arr, dims, precision=precision, preferred_element_type=jnp.float32
    )


def query_block(bins):
    for block in (384, 256, 128):
        if bins % block == 0:
            return block
    return bins


def attend_forward_kernel(block, bins, pack_ref, rel_ref, out_ref, probs_ref):
    step = pl.program_id(0)
    span = bins + block
    query = pack_ref[pl.ds(pl.multiple_of(step * block, block), block), VD + KD :]
    base = pl.multiple_of(bins - block - step * block, block)
    content = mxu(query[:, :KD], pack_ref[:, VD : VD + KD], NT)
    position = mxu(query[:, KD:], rel_ref[pl.ds(base, span), :], NT)
    position = pltpu.roll(position, span - (block - 1), 1, stride=1, stride_axis=0)
    scores = content + position[:, :bins]
    exps = jnp.exp(scores - jnp.max(scores, axis=1, keepdims=True))
    probs = (exps * (1.0 / jnp.sum(exps, axis=1, keepdims=True))).astype(jnp.bfloat16)
    probs_ref[...] = probs
    out_ref[0] = mxu(probs, pack_ref[:, :VD], NN).T.astype(jnp.bfloat16)


def attend_forward(pack, rel):
    bins = pack.shape[0]
    block = query_block(bins)
    steps = bins // block
    return pl.pallas_call(
        lambda *refs: attend_forward_kernel(block, bins, *refs),
        grid=(steps,),
        in_specs=[
            pl.BlockSpec((bins, PACK), lambda i: (0, 0)),
            pl.BlockSpec((2 * bins, KD), lambda i: (0, 0)),
        ],
        out_specs=[
            pl.BlockSpec((1, VD, block), lambda i: (i, 0, 0)),
            pl.BlockSpec((block, bins), lambda i: (i, 0)),
        ],
        out_shape=[
            jax.ShapeDtypeStruct((steps, VD, block), jnp.bfloat16),
            jax.ShapeDtypeStruct((bins, bins), jnp.bfloat16),
        ],
        compiler_params=pltpu.CompilerParams(vmem_limit_bytes=48 << 20),
        cost_estimate=pl.CostEstimate(
            flops=2 * bins * bins * 1024, bytes_accessed=2 * bins * bins, transcendentals=bins * bins
        ),
        name="attend_forward",
    )(pack, rel)


def attend_backward_kernel(
    block, bins, pack_ref, rel_ref, probs_ref, grad_ref, out_ref, drel_ref, stat_ref, acc_ref
):
    step = pl.program_id(0)
    steps = bins // block
    span = bins + block

    @pl.when(step == 0)
    def _():
        acc_ref[...] = jnp.zeros_like(acc_ref)
        drel_ref[...] = jnp.zeros_like(drel_ref)
        stat_ref[...] = jnp.zeros_like(stat_ref)

    query = pack_ref[pl.ds(pl.multiple_of(step * block, block), block), VD + KD :]
    base = pl.multiple_of(bins - block - step * block, block)
    grad_t = grad_ref[0]
    probs = probs_ref[...]
    acc_ref[:VD, :] += mxu(grad_t, probs, NN)
    grad_probs = mxu(grad_t.T, pack_ref[:, :VD], NT)
    wide = probs.astype(jnp.float32)
    scaled = wide * grad_probs
    delta = jnp.sum(scaled, axis=1, keepdims=True)
    grad_scores = (scaled - wide * delta).astype(jnp.bfloat16)
    grad_qc = mxu(grad_scores, pack_ref[:, VD : VD + KD], NN)
    query_t = query.T
    acc_ref[VD:, :] += mxu(query_t[:KD], grad_scores, NN)
    row = lax.broadcasted_iota(jnp.int32, (block, block), 0)
    col = lax.broadcasted_iota(jnp.int32, (block, block), 1)
    flip = (row + col == block - 1).astype(jnp.bfloat16)
    turned = mxu(flip, grad_scores, NN)
    turned = jnp.concatenate([turned, jnp.zeros((block, block), jnp.float32)], axis=1)
    turned = pltpu.roll(turned, 0, 1, stride=1, stride_axis=0).astype(jnp.bfloat16)
    grad_qp = mxu(
        flip.astype(jnp.float32),
        mxu(turned, rel_ref[pl.ds(base, span), :], NN),
        NN,
        exact_mode,
    )
    pos_turned = mxu(query_t[KD:], flip, NN).astype(jnp.bfloat16)
    drel_ref[:, pl.ds(base, span)] += mxu(pos_turned, turned, NN)
    stat_ref[0:1, :KD] += jnp.sum(grad_qc, axis=0, keepdims=True)
    stat_ref[1:2, :KD] += jnp.sum(grad_qp, axis=0, keepdims=True)
    out_ref[pl.ds(step, 1), VD + KD :, :] = (
        ((grad_qc + grad_qp) * (KD**-0.5)).T.astype(jnp.bfloat16)[None]
    )

    @pl.when(step == steps - 1)
    def _():
        for part in range(steps):
            out_ref[part, : VD + KD, :] = acc_ref[:, part * block : (part + 1) * block].astype(
                jnp.bfloat16
            )


def attend_backward(pack, rel, probs, grad):
    bins = pack.shape[0]
    block = query_block(bins)
    steps = bins // block
    return pl.pallas_call(
        lambda *refs: attend_backward_kernel(block, bins, *refs),
        grid=(steps,),
        in_specs=[
            pl.BlockSpec((bins, PACK), lambda i: (0, 0)),
            pl.BlockSpec((2 * bins, KD), lambda i: (0, 0)),
            pl.BlockSpec((block, bins), lambda i: (i, 0)),
            pl.BlockSpec((1, VD, block), lambda i: (i, 0, 0)),
        ],
        out_specs=[
            pl.BlockSpec((steps, GRAD_PACK, block), lambda i: (0, 0, 0)),
            pl.BlockSpec((KD, 2 * bins), lambda i: (0, 0)),
            pl.BlockSpec((8, 128), lambda i: (0, 0)),
        ],
        out_shape=[
            jax.ShapeDtypeStruct((steps, GRAD_PACK, block), jnp.bfloat16),
            jax.ShapeDtypeStruct((KD, 2 * bins), jnp.float32),
            jax.ShapeDtypeStruct((8, 128), jnp.float32),
        ],
        scratch_shapes=[pltpu.VMEM((VD + KD, bins), jnp.float32)],
        compiler_params=pltpu.CompilerParams(vmem_limit_bytes=48 << 20),
        cost_estimate=pl.CostEstimate(
            flops=2 * bins * bins * 2048, bytes_accessed=2 * bins * bins, transcendentals=0
        ),
        name="attend_backward",
    )(pack, rel, probs, grad)


def heads_kernel(
    track_human,
    track_mouse,
    tiles_human,
    pick_ref,
    rows_ref,
    weight_ref,
    human_own_ref,
    human_oth_ref,
    mouse_own_ref,
    mouse_oth_ref,
    bias_ref,
    count_human_ref,
    count_mouse_ref,
    grad_ref,
    dtrunk_ref,
    dbias_ref,
    loss_ref,
):
    step = pl.program_id(0)
    kind = pick_ref[0]
    swapped = pick_ref[1] == 1
    on_human = jnp.logical_and(step < tiles_human, kind == 0)
    on_mouse = jnp.logical_and(step >= tiles_human, kind == 1)

    @pl.when(step == 0)
    def _():
        dtrunk_ref[...] = jnp.zeros_like(dtrunk_ref)
        loss_ref[...] = jnp.zeros_like(loss_ref)

    def score(own_ref, oth_ref, count_ref, first, tracks):
        track = lax.broadcasted_iota(jnp.int32, (TILE, 1), 0) + first * TILE
        valid = track < tracks
        own = jnp.where(valid, own_ref[...], 0.0).astype(jnp.bfloat16)
        oth = jnp.where(valid, oth_ref[...], 0.0).astype(jnp.bfloat16)
        head = jnp.concatenate(
            [jnp.where(swapped, oth, own), jnp.where(swapped, own, oth)], axis=1
        )
        logits = mxu(head, rows_ref[...], NT) + bias_ref[...]
        counts = count_ref[0].astype(jnp.float32)
        small = jnp.exp(-jnp.abs(logits))
        above = 1.0 + small
        log_above = jnp.log(above) + (small - (above - 1.0)) / above
        shifted = jnp.maximum(logits, 0.0) + log_above
        predicted = shifted
        shifted = shifted + log_eps
        sigma = jnp.where(logits >= 0.0, 1.0, small) / above
        weight = weight_ref[0:1, :]
        rows_loss = weight * (predicted - counts * jnp.log(shifted))
        grad = weight * (sigma - counts * sigma / shifted)
        rows_loss = jnp.where(valid, rows_loss, 0.0)
        grad = jnp.where(valid, grad, 0.0)
        loss_ref[...] += jnp.sum(rows_loss.reshape(TILE // 8, 8, -1), axis=0)
        dbias_ref[...] = jnp.sum(grad, axis=1, keepdims=True)
        grad_low = grad.astype(jnp.bfloat16)
        grad_ref[...] = grad_low
        dtrunk_ref[...] += mxu(grad_low.T, head, NN)

    @pl.when(on_human)
    def _():
        score(human_own_ref, human_oth_ref, count_human_ref, step, track_human)

    @pl.when(on_mouse)
    def _():
        score(mouse_own_ref, mouse_oth_ref, count_mouse_ref, step - tiles_human, track_mouse)

    @pl.when(jnp.logical_not(jnp.logical_or(on_human, on_mouse)))
    def _():
        dbias_ref[...] = jnp.zeros_like(dbias_ref)


def score_heads(window, pick, rows, weight, human, mouse, bias, count_human, count_mouse):
    bins, width = rows.shape
    share = human[0].shape[1]
    rest = width - share
    track_human, track_mouse = count_human.shape[1], count_mouse.shape[1]
    tiles_human, tiles_mouse = pl.cdiv(track_human, TILE), pl.cdiv(track_mouse, TILE)
    tiles = tiles_human + tiles_mouse

    def human_tile(t, p):
        return jnp.where(p[0] == 0, jnp.minimum(t, tiles_human - 1), 0)

    def mouse_tile(t, p):
        return jnp.where(p[0] == 1, jnp.maximum(t - tiles_human, 0), 0)

    whole = lambda t, p: (0, 0)
    along = lambda t, p: (t, 0)
    return pl.pallas_call(
        lambda *refs: heads_kernel(track_human, track_mouse, tiles_human, *refs),
        grid_spec=pltpu.PrefetchScalarGridSpec(
            num_scalar_prefetch=1,
            grid=(tiles,),
            in_specs=[
                pl.BlockSpec((bins, width), whole),
                pl.BlockSpec((8, bins), whole),
                pl.BlockSpec((TILE, share), lambda t, p: (human_tile(t, p), 0)),
                pl.BlockSpec((TILE, rest), lambda t, p: (human_tile(t, p), 0)),
                pl.BlockSpec((TILE, share), lambda t, p: (mouse_tile(t, p), 0)),
                pl.BlockSpec((TILE, rest), lambda t, p: (mouse_tile(t, p), 0)),
                pl.BlockSpec((TILE, 1), along),
                pl.BlockSpec((1, TILE, bins), lambda t, p: (window, human_tile(t, p), 0)),
                pl.BlockSpec((1, TILE, bins), lambda t, p: (window, mouse_tile(t, p), 0)),
            ],
            out_specs=[
                pl.BlockSpec((TILE, bins), along),
                pl.BlockSpec((bins, width), whole),
                pl.BlockSpec((TILE, 1), along),
                pl.BlockSpec((8, bins), whole),
            ],
        ),
        out_shape=[
            jax.ShapeDtypeStruct((tiles * TILE, bins), jnp.bfloat16),
            jax.ShapeDtypeStruct((bins, width), jnp.float32),
            jax.ShapeDtypeStruct((tiles * TILE, 1), jnp.float32),
            jax.ShapeDtypeStruct((8, bins), jnp.float32),
        ],
        compiler_params=pltpu.CompilerParams(vmem_limit_bytes=56 << 20),
        cost_estimate=pl.CostEstimate(
            flops=4 * bins * width * track_human,
            bytes_accessed=4 * width * track_human,
            transcendentals=4 * bins * track_human,
        ),
        name="score_heads",
    )(pick, rows, weight, *human, *mouse, bias, count_human, count_mouse)


def head_grads_kernel(windows, tiles_human, pick_ref, *refs):
    grads, rows, out_ref, acc_ref = refs[:windows], refs[windows], refs[windows + 1], refs[-1]
    step = pl.program_id(0)
    mine = jnp.where(step < tiles_human, 0, 1)
    acc_ref[...] = jnp.zeros_like(acc_ref)
    for window in range(windows):

        @pl.when(pick_ref[window] == mine)
        def _():
            acc_ref[...] += mxu(grads[window][...], rows[window], NN)

    out_ref[...] = acc_ref[...].astype(jnp.bfloat16)


def head_grads(pick, grads, rows, tiles_human):
    windows, bins, share = rows.shape
    tiles = grads[0].shape[0] // TILE

    def tile_of(window):
        def index(t, p):
            first = jnp.where(p[window] == 0, jnp.minimum(t, tiles_human - 1), 0)
            return (jnp.where(p[window] == 1, jnp.maximum(t, tiles_human), first), 0)

        return index

    return pl.pallas_call(
        lambda *refs: head_grads_kernel(windows, tiles_human, *refs),
        grid_spec=pltpu.PrefetchScalarGridSpec(
            num_scalar_prefetch=1,
            grid=(tiles,),
            in_specs=[pl.BlockSpec((TILE, bins), tile_of(w)) for w in range(windows)]
            + [pl.BlockSpec((windows, bins, share), lambda t, p: (0, 0, 0))],
            out_specs=pl.BlockSpec((TILE, share), lambda t, p: (t, 0)),
            scratch_shapes=[pltpu.VMEM((TILE, share), jnp.float32)],
        ),
        out_shape=jax.ShapeDtypeStruct((tiles * TILE, share), jnp.bfloat16),
        compiler_params=pltpu.CompilerParams(vmem_limit_bytes=40 << 20),
        cost_estimate=pl.CostEstimate(
            flops=2 * windows * bins * share * tiles * TILE,
            bytes_accessed=4 * tiles * TILE * share,
            transcendentals=0,
        ),
        name="head_grads",
    )(pick, *grads, rows)


def norm_stats(values):
    mean = jnp.mean(values, axis=-1, keepdims=True)
    centred = values - mean
    inverse = lax.rsqrt(jnp.mean(centred * centred, axis=-1, keepdims=True) + norm_eps)
    return mean, inverse


def norm_backward(grad_output, scaled, inverse, norm_gain):
    grad_scaled = grad_output * norm_gain
    mean_grad = jnp.mean(grad_scaled, axis=-1, keepdims=True)
    mean_proj = jnp.mean(grad_scaled * scaled, axis=-1, keepdims=True)
    grad_input = inverse * (grad_scaled - mean_grad - scaled * mean_proj)
    return (grad_input, jnp.sum(grad_output * scaled, axis=0), jnp.sum(grad_output, axis=0))


def sum_over_model(partial):
    low = partial.astype(jnp.bfloat16)
    if lax.axis_size("mp") == 2:
        other = lax.ppermute(low, "mp", [(0, 1), (1, 0)])
        return low.astype(jnp.float32) + other.astype(jnp.float32)
    return lax.psum(low, "mp").astype(jnp.float32)


def in_model_order(own, dim):
    if lax.axis_size("mp") == 2:
        first = lax.axis_index("mp") == 0
        other = lax.ppermute(own, "mp", [(0, 1), (1, 0)])
        return jnp.concatenate(
            [jnp.where(first, own, other), jnp.where(first, other, own)], axis=dim
        )
    return lax.all_gather(own, "mp", axis=dim, tiled=True)


def other_rows(own, chunk):
    count = lax.axis_size("dp") * lax.axis_size("seq")
    place = lax.axis_index("dp") * lax.axis_size("seq") + lax.axis_index("seq")
    rows = own.shape[0]
    start = jnp.minimum(place * chunk, rows - chunk)
    part = lax.dynamic_slice_in_dim(own, start, chunk, 0)
    if count * chunk != rows:
        part = lax.dynamic_slice_in_dim(
            jnp.concatenate([part, part], axis=0),
            jnp.minimum(place * chunk - start, chunk),
            chunk,
            0,
        )
    part = lax.ppermute(part, "mp", [(0, 1), (1, 0)])
    return lax.all_gather(part, ("dp", "seq"), axis=0, tiled=True)


def swap_pairs(axis, step):
    return [(i, i ^ step) for i in range(lax.axis_size(axis))]


def sum_everywhere(vector):
    for axis in ("dp", "seq"):
        step = 1
        while step < lax.axis_size(axis):
            vector = vector + lax.ppermute(vector, axis, swap_pairs(axis, step))
            step *= 2
    return vector


def scatter_sum(full):
    dp_size, seq_size = lax.axis_size("dp"), lax.axis_size("seq")
    dp_index, seq_index = lax.axis_index("dp"), lax.axis_index("seq")
    rows = full.shape[0] // (dp_size * seq_size)
    cols = full.shape[1]
    kept = full.astype(jnp.bfloat16)
    step = 1
    while step < dp_size:
        bit = (dp_index // step) % 2
        split = kept.reshape(-1, 2, seq_size * rows, cols)
        mine = lax.dynamic_index_in_dim(split, bit, 1, keepdims=False)
        theirs = lax.dynamic_index_in_dim(split, 1 - bit, 1, keepdims=False)
        got = lax.ppermute(theirs, "dp", swap_pairs("dp", step))
        kept = (mine.astype(jnp.float32) + got.astype(jnp.float32)).astype(jnp.bfloat16)
        step *= 2
    parts = kept.reshape(seq_size, rows, cols)

    def part(index):
        return lax.dynamic_index_in_dim(parts, index % seq_size, 0, keepdims=False)

    ring = [(i, (i + 1) % seq_size) for i in range(seq_size)]
    moving = part(seq_index - 1 + seq_size)
    for step in range(seq_size - 1):
        got = lax.ppermute(moving, "seq", ring)
        total = got.astype(jnp.float32) + part(seq_index - 2 - step + 2 * seq_size).astype(
            jnp.float32
        )
        moving = total.astype(jnp.bfloat16)
    return total


def on_device(
    trunk_in,
    norm1_gain,
    norm1_bias,
    w_query,
    w_key,
    w_value,
    w_rel,
    content_bias,
    pos_bias,
    w_out,
    b_out,
    norm2_gain,
    norm2_bias,
    w_in,
    b_in,
    w_hid,
    b_hid,
    head_human,
    bias_human,
    head_mouse,
    bias_mouse,
    species,
    targets_human,
    targets_mouse,
):
    windows, bins, width = trunk_in.shape
    heads = content_bias.shape[0]
    dp_size, seq_size, mp_size = (lax.axis_size(axis) for axis in ("dp", "seq", "mp"))
    seq_index, mp_index = lax.axis_index("seq"), lax.axis_index("mp")
    place = lax.axis_index("dp") * seq_size + seq_index
    places = dp_size * seq_size
    all_bins = bins * seq_size
    block = query_block(all_bins)
    query_start = seq_index * bins
    key_scale = KD ** (-0.5)
    loss_scale = 1.0 / math.sqrt(windows * dp_size * CROP)
    crop_start = (all_bins - CROP) // 2
    bf16 = jnp.bfloat16

    if heads % seq_size == 0:
        groups = [[w] for w in range(windows)]
    else:
        groups = [list(range(windows))]
    group_size = len(groups[0])
    pairs = heads * group_size
    pairs_here = -(-pairs // seq_size)
    pair_heads = [
        jnp.minimum((seq_index * pairs_here + j) // group_size, heads - 1)
        for j in range(pairs_here)
    ]

    def spread(array):
        short = seq_size * pairs_here - pairs
        if short:
            array = jnp.pad(array, [(0, short)] + [(0, 0)] * (array.ndim - 1))
        return exchange(array.reshape((seq_size, pairs_here) + array.shape[1:]))

    def exchange(array):
        return lax.all_to_all(array, "seq", split_axis=0, concat_axis=0, tiled=True)

    def bins_last(array):
        if bins == block:
            return array
        depth = array.shape[1]
        array = array.transpose(1, 0, 2).reshape(depth, all_bins // block, block)
        return array.transpose(1, 0, 2)

    def owners_first(array):
        if bins == block:
            return array
        depth = array.shape[1]
        array = array.transpose(1, 0, 2).reshape(depth, seq_size, bins)
        return array.transpose(1, 0, 2)

    def collect(arrays):
        depth = arrays[0].shape[1]
        stacked = jnp.stack([owners_first(a) for a in arrays], axis=1)
        stacked = exchange(stacked).reshape(seq_size * pairs_here, depth, bins)[:pairs]
        stacked = stacked.reshape(heads, group_size, depth, bins).transpose(0, 2, 1, 3)
        return stacked.reshape(heads, depth, group_size * bins)

    def all_rows(own, chunk):
        if mp_size != 2:
            full = lax.all_gather(own, "mp", axis=1, tiled=True)
            half = full.shape[1] // 2
            return (full[:, :half], full[:, half:])
        return (own, other_rows(own, chunk))

    def chunk_of(rows):
        return -(-rows // (places * 16)) * 16

    if mp_size == 2:
        out_oth = other_rows(w_out, w_out.shape[0] // places)
        first = mp_index == 0
        w_out_all = jnp.concatenate(
            [jnp.where(first, w_out, out_oth), jnp.where(first, out_oth, w_out)], axis=0
        )
    else:
        w_out_all = lax.all_gather(w_out, "mp", axis=0, tiled=True)
    track_human, track_mouse = head_human.shape[1], head_mouse.shape[1]
    human = all_rows(head_human.T, chunk_of(track_human))
    mouse = all_rows(head_mouse.T, chunk_of(track_mouse))

    def per_head(weight, size):
        return weight.reshape(width, heads, size)

    value_w, key_w, query_w = per_head(w_value, VD), per_head(w_key, KD), per_head(w_query, KD)
    w_pack = jnp.concatenate([value_w, key_w, query_w, query_w], axis=2).reshape(
        width, heads * PACK
    )
    w_grad = jnp.concatenate([value_w, key_w, query_w], axis=2).reshape(width, heads * GRAD_PACK)
    pack_scale = jnp.concatenate(
        [jnp.ones((VD + KD,), jnp.float32), jnp.full((2 * KD,), key_scale, jnp.float32)]
    )
    pack_scale = jnp.tile(pack_scale, heads)
    pack_bias = jnp.concatenate(
        [jnp.zeros((heads, VD + KD), jnp.float32), content_bias, pos_bias], axis=1
    ).reshape(-1)

    basis = jnp.pad(rel_basis(), [(0, 1), (0, 0)])
    w_rel_heads = w_rel.reshape(FEAT, heads, KD)
    rels = [
        mxu(
            basis,
            lax.dynamic_index_in_dim(w_rel_heads, head, 1, keepdims=False).astype(jnp.float32),
            NN,
            exact_mode,
        ).astype(bf16)
        for head in pair_heads
    ]

    trunk, stats1, normed1, packs = [], [], [], []
    for group in groups:
        rows = group_size * bins
        values = trunk_in[group[0] : group[-1] + 1].reshape(rows, width).astype(jnp.float32)
        mean, inverse = norm_stats(values)
        normed = ((values - mean) * inverse * norm1_gain + norm1_bias).astype(bf16)
        pack = (mxu(normed, w_pack, NN) * pack_scale + pack_bias).astype(bf16)
        pack = pack.reshape(group_size, bins, heads, PACK).transpose(2, 0, 1, 3)
        pack = spread(pack.reshape(pairs, bins, PACK))
        trunk.append(values)
        stats1.append((mean, inverse))
        normed1.append(normed)
        packs.append([pack[:, j].reshape(all_bins, PACK) for j in range(pairs_here)])

    probs, attended, mids, stats2, normed2, preacts, actives, trunk_out, trunk_low = (
        [] for _ in range(9)
    )
    for g, group in enumerate(groups):
        outs, kept = [], []
        for j in range(pairs_here):
            out, prob = attend_forward(packs[g][j], rels[j])
            outs.append(out)
            kept.append(prob)
        probs.append(kept)
        att = collect(outs).reshape(heads * VD, group_size * bins)
        attended.append(att)
        att_all = in_model_order(att, 0)
        mid = trunk[g] + mxu(att_all, w_out_all, TN) + b_out
        mean, inverse = norm_stats(mid)
        normed = ((mid - mean) * inverse * norm2_gain + norm2_bias).astype(bf16)
        preact = mxu(normed, w_in, NN) + b_in
        active = jnp.maximum(preact, 0.0).astype(bf16)
        out = mid + (sum_over_model(mxu(active, w_hid, NN)) + b_hid)
        mids.append(mid)
        stats2.append((mean, inverse))
        normed2.append(normed)
        preacts.append(preact > 0.0)
        actives.append(active)
        trunk_out.append(out)
        trunk_low.append(out.astype(bf16))

    bin_place = query_start + jnp.arange(bins)
    in_crop = ((bin_place >= crop_start) & (bin_place < crop_start + CROP)).astype(jnp.float32)
    weight = jnp.broadcast_to((in_crop * loss_scale)[None, :], (8, bins))
    has_crop = (query_start + bins > crop_start) & (query_start < crop_start + CROP)
    picks = jnp.where(has_crop, species, 2)
    count_human = targets_human.transpose(0, 2, 1)
    count_mouse = targets_mouse.transpose(0, 2, 1)
    tiles_human, tiles_mouse = pl.cdiv(track_human, TILE), pl.cdiv(track_mouse, TILE)
    bias_all = jnp.concatenate(
        [
            jnp.pad(bias_human, (0, tiles_human * TILE - track_human)),
            jnp.pad(bias_mouse, (0, tiles_mouse * TILE - track_mouse)),
        ]
    )[:, None]
    order = mp_index if mp_size == 2 else 0
    grad_rows, logit_grads, track_sums, losses = [], [], [], []
    low_windows = [
        trunk_low[g][i * bins : (i + 1) * bins] for g in range(len(groups)) for i in range(group_size)
    ]
    for window in range(windows):
        pick = jnp.stack([picks[window], jnp.int32(0) + order])
        grad_low, grad_out, track_sum, loss = score_heads(
            window, pick, low_windows[window], weight, human, mouse, bias_all, count_human, count_mouse
        )
        logit_grads.append(grad_low)
        grad_rows.append(grad_out)
        track_sums.append(track_sum)
        losses.append(jnp.sum(loss))
    share = head_human.shape[0]
    own_rows = jnp.stack(
        [lax.dynamic_slice_in_dim(rows, mp_index * share, share, 1) for rows in low_windows]
    )
    dheads = head_grads(picks, logit_grads, own_rows, tiles_human)
    dheads = lax.psum(dheads, ("dp", "seq")).astype(jnp.float32)
    dtracks = sum(track_sums)[:, 0]

    grad_mids, grad_outs, grad_pres, grad_mid_lows, packed_grads = [], [], [], [], []
    sums = [0.0] * 5
    drels = [0.0] * pairs_here
    dstats = [0.0] * pairs_here
    for g, group in enumerate(groups):
        grad_trunk = jnp.concatenate([grad_rows[w] for w in group], axis=0)
        grad_out = grad_trunk.astype(bf16)
        grad_preact = jnp.where(preacts[g], mxu(grad_out, w_hid, NT), 0.0)
        grad_pre = grad_preact.astype(bf16)
        grad_normed = sum_over_model(mxu(grad_pre, w_in, NT))
        mean, inverse = stats2[g]
        grad_norm, dgain, dbias = norm_backward(
            grad_normed, (mids[g] - mean) * inverse, inverse, norm2_gain
        )
        grad_mid = grad_trunk + grad_norm
        grad_mid_low = grad_mid.astype(bf16)
        parts = (
            dgain,
            dbias,
            jnp.sum(grad_mid, axis=0),
            jnp.sum(grad_trunk, axis=0),
            jnp.sum(grad_preact, axis=0),
        )
        sums = [old + new for old, new in zip(sums, parts)]
        grad_outs.append(grad_out)
        grad_pres.append(grad_pre)
        grad_mids.append(grad_mid)
        grad_mid_lows.append(grad_mid_low)
        grad_att = mxu(w_out, grad_mid_low, NT).astype(bf16)
        grad_att = grad_att.reshape(heads, VD, group_size, bins).transpose(0, 2, 1, 3)
        grad_att = spread(grad_att.reshape(pairs, VD, bins))
        outs = []
        for j in range(pairs_here):
            out, drel, stat = attend_backward(
                packs[g][j], rels[j], probs[g][j], bins_last(grad_att[:, j])
            )
            outs.append(out)
            drels[j] = drels[j] + drel
            dstats[j] = dstats[j] + stat
        packed_grads.append(collect(outs).reshape(heads * GRAD_PACK, group_size * bins))

    join = lambda arrays: jnp.concatenate(arrays, axis=0)
    dtrunk_weights = jnp.concatenate(
        [
            mxu(join(normed2), join(grad_pres), TN).astype(bf16),
            mxu(join(grad_outs), join(actives), TN).astype(bf16),
            lax.dot_general(
                join(grad_mid_lows),
                jnp.concatenate(attended, axis=1),
                (((0,), (1,)), ((), ())),
                preferred_element_type=jnp.float32,
            ).astype(bf16),
        ],
        axis=1,
    )
    trunk_summed = scatter_sum(dtrunk_weights)

    grad_inputs = []
    sums1 = [0.0, 0.0]
    for g, group in enumerate(groups):
        grad_normed = sum_over_model(
            lax.dot_general(
                packed_grads[g],
                w_grad,
                (((0,), (1,)), ((), ())),
                preferred_element_type=jnp.float32,
            )
        )
        mean, inverse = stats1[g]
        grad_norm, dgain, dbias = norm_backward(
            grad_normed, (trunk[g] - mean) * inverse, inverse, norm1_gain
        )
        sums1 = [sums1[0] + dgain, sums1[1] + dbias]
        grad_inputs.append((grad_mids[g] + grad_norm).reshape(group_size, bins, width))
    dpack = lax.dot_general(
        join(normed1),
        jnp.concatenate(packed_grads, axis=1),
        (((0,), (1,)), ((), ())),
        preferred_element_type=jnp.float32,
    ).astype(bf16)
    pack_summed = scatter_sum(dpack).reshape(-1, heads, GRAD_PACK)

    dw_rel = jnp.zeros((heads, FEAT, KD), jnp.float32)
    dstat = jnp.zeros((heads, 2, KD), jnp.float32)
    for j, head in enumerate(pair_heads):
        mine = (jnp.arange(heads) == head).astype(jnp.float32)[:, None, None]
        part = lax.dot_general(
            basis,
            drels[j],
            (((0,), (1,)), ((), ())),
            precision=exact_mode,
            preferred_element_type=jnp.float32,
        )
        dw_rel = dw_rel + mine * part
        dstat = dstat + mine * dstats[j][None, :2, :KD]

    def sum_parts(parts):
        sizes = [part.size for part in parts]
        flat = [part.reshape(-1) for part in parts]
        flat = [jnp.pad(part, (0, -part.size % 128)) for part in flat]
        total = sum_everywhere(jnp.concatenate(flat).reshape(-1, 128)).reshape(-1)
        results, start = [], 0
        for part, size in zip(parts, sizes):
            results.append(total[start : start + size].reshape(part.shape))
            start += -(-size // 128) * 128
        return results

    dgain2, dbias2, db_out, db_hid, db_in, dtracks, loss = sum_parts(
        list(sums) + [dtracks, sum(losses)[None]]
    )
    dgain1, dbias1, dstat, dw_rel = sum_parts(list(sums1) + [dstat, dw_rel])

    def own(array, dim=0):
        size = array.shape[dim] // places
        return lax.dynamic_slice_in_dim(array, place * size, size, dim)

    rel_rows = own(dw_rel, 1).transpose(1, 0, 2).reshape(-1, heads * KD)
    hidden = w_in.shape[1]
    pack_rows = pack_summed.shape[0]
    shape3 = (windows, bins, width)
    return (
        join(trunk_out).reshape(shape3),
        loss[0],
        join(grad_inputs).reshape(shape3),
        own(dgain1),
        own(dbias1),
        pack_summed[:, :, VD + KD :].reshape(pack_rows, heads * KD),
        pack_summed[:, :, VD : VD + KD].reshape(pack_rows, heads * KD),
        pack_summed[:, :, :VD].reshape(pack_rows, heads * VD),
        rel_rows,
        own(dstat[:, 0], 1),
        own(dstat[:, 1], 1),
        trunk_summed[:, 2 * hidden :].T,
        own(db_out),
        own(dgain2),
        own(dbias2),
        trunk_summed[:, :hidden],
        db_in,
        trunk_summed[:, hidden : 2 * hidden].T,
        own(db_hid),
        dheads[:track_human].T,
        dtracks[:track_human],
        dheads[tiles_human * TILE : tiles_human * TILE + track_mouse].T,
        dtracks[tiles_human * TILE : tiles_human * TILE + track_mouse],
    )


def solution(mesh):
    in_specs = (
        P("dp", "seq", None),
        P(),
        P(),
        P(None, "mp"),
        P(None, "mp"),
        P(None, "mp"),
        P(None, "mp"),
        P("mp", None),
        P("mp", None),
        P("mp", None),
        P(),
        P(),
        P(),
        P(None, "mp"),
        P("mp"),
        P("mp", None),
        P(),
        P("mp", None),
        P(),
        P("mp", None),
        P(),
        P("dp"),
        P("dp", "seq", None),
        P("dp", "seq", None),
    )
    out_specs = (
        P("dp", "seq", None),
        P(),
        P("dp", "seq", None),
        P(("dp", "seq")),
        P(("dp", "seq")),
        P(("dp", "seq"), "mp"),
        P(("dp", "seq"), "mp"),
        P(("dp", "seq"), "mp"),
        P(("dp", "seq"), "mp"),
        P("mp", ("dp", "seq")),
        P("mp", ("dp", "seq")),
        P("mp", ("dp", "seq")),
        P(("dp", "seq")),
        P(("dp", "seq")),
        P(("dp", "seq")),
        P(("dp", "seq"), "mp"),
        P("mp"),
        P("mp", ("dp", "seq")),
        P(("dp", "seq")),
        P("mp", None),
        P(),
        P("mp", None),
        P(),
    )
    return jax.shard_map(
        on_device, mesh=mesh, in_specs=in_specs, out_specs=out_specs, check_vma=False
    )
```

```python
import math

import jax
import jax.numpy as jnp
from jax import lax
from jax.experimental import pallas as pl
from jax.experimental.pallas import tpu as pltpu
from jax.sharding import PartitionSpec as P

KD = 64
VD = 192
FEAT = 192
BINS = 1536
CROP = 896


norm_eps = 1e-05
log_eps = 1e-07
exact_mode = lax.Precision.HIGHEST


def rel_basis():
    per_class = FEAT // 6
    distance = jnp.arange(-(BINS - 1), BINS).astype(jnp.float32)
    magnitude = jnp.abs(distance)[:, None]
    half_life = (2.0 ** jnp.linspace(3.0, math.log2(BINS), per_class)).astype(jnp.float32)
    decays = jnp.exp(-math.log(2.0) / half_life[None, :] * magnitude)
    widths = (2.0 ** jnp.arange(1, per_class + 1)).astype(jnp.float32) - 1.0
    central = (widths[None, :] > magnitude).astype(jnp.float32)
    spread = BINS / (2.0 * per_class)
    centre = jnp.linspace(BINS / per_class, BINS, per_class).astype(jnp.float32)
    concentration = (centre / spread) ** 2
    rate_param = centre / spread**2
    peak_at = (concentration - 1.0) / rate_param
    log_ratio = (concentration - 1.0) * (
        jnp.log(jnp.maximum(magnitude, 1e-20)) - jnp.log(peak_at)
    ) - rate_param * (magnitude - peak_at)
    density = jnp.exp(log_ratio)
    gammas = density / jnp.max(density, axis=0, keepdims=True)
    symmetric = jnp.concatenate([decays, central, gammas], axis=1)
    return jnp.concatenate([symmetric, jnp.sign(distance)[:, None] * symmetric], axis=1)


PACK = VD + 3 * KD
GRAD_PACK = VD + 2 * KD
TILE = 896
NN = (((1,), (0,)), ((), ()))
NT = (((1,), (1,)), ((), ()))
TN = (((0,), (0,)), ((), ()))


def mxu(left_arr, right_arr, dims, precision=None):
    return lax.dot_general(
        left_arr, right_arr, dims, precision=precision, preferred_element_type=jnp.float32
    )


def query_block(bins):
    for block in (384, 256, 128):
        if bins % block == 0:
            return block
    return bins


def attend_forward_kernel(block, bins, pack_ref, rel_ref, out_ref, probs_ref):
    step = pl.program_id(0)
    span = bins + block
    query = pack_ref[pl.ds(pl.multiple_of(step * block, block), block), VD + KD :]
    base = pl.multiple_of(bins - block - step * block, block)
    content = mxu(query[:, :KD], pack_ref[:, VD : VD + KD], NT)
    position = mxu(query[:, KD:], rel_ref[pl.ds(base, span), :], NT)
    position = pltpu.roll(position, span - (block - 1), 1, stride=1, stride_axis=0)
    scores = content + position[:, :bins]
    exps = jnp.exp(scores - jnp.max(scores, axis=1, keepdims=True))
    probs = (exps * (1.0 / jnp.sum(exps, axis=1, keepdims=True))).astype(jnp.bfloat16)
    probs_ref[...] = probs
    out_ref[0] = mxu(probs, pack_ref[:, :VD], NN).T.astype(jnp.bfloat16)


def attend_forward(pack, rel):
    bins = pack.shape[0]
    block = query_block(bins)
    steps = bins // block
    return pl.pallas_call(
        lambda *refs: attend_forward_kernel(block, bins, *refs),
        grid=(steps,),
        in_specs=[
            pl.BlockSpec((bins, PACK), lambda i: (0, 0)),
            pl.BlockSpec((2 * bins, KD), lambda i: (0, 0)),
        ],
        out_specs=[
            pl.BlockSpec((1, VD, block), lambda i: (i, 0, 0)),
            pl.BlockSpec((block, bins), lambda i: (i, 0)),
        ],
        out_shape=[
            jax.ShapeDtypeStruct((steps, VD, block), jnp.bfloat16),
            jax.ShapeDtypeStruct((bins, bins), jnp.bfloat16),
        ],
        compiler_params=pltpu.CompilerParams(vmem_limit_bytes=48 << 20),
        cost_estimate=pl.CostEstimate(
            flops=2 * bins * bins * 1024, bytes_accessed=2 * bins * bins, transcendentals=bins * bins
        ),
        name="attend_forward",
    )(pack, rel)


def attend_backward_kernel(
    block, bins, pack_ref, rel_ref, probs_ref, grad_ref, out_ref, drel_ref, stat_ref, acc_ref
):
    step = pl.program_id(0)
    steps = bins // block
    span = bins + block

    @pl.when(step == 0)
    def _():
        acc_ref[...] = jnp.zeros_like(acc_ref)
        drel_ref[...] = jnp.zeros_like(drel_ref)
        stat_ref[...] = jnp.zeros_like(stat_ref)

    query = pack_ref[pl.ds(pl.multiple_of(step * block, block), block), VD + KD :]
    base = pl.multiple_of(bins - block - step * block, block)
    grad_t = grad_ref[0]
    probs = probs_ref[...]
    acc_ref[:VD, :] += mxu(grad_t, probs, NN)
    grad_probs = mxu(grad_t.T, pack_ref[:, :VD], NT)
    wide = probs.astype(jnp.float32)
    scaled = wide * grad_probs
    delta = jnp.sum(scaled, axis=1, keepdims=True)
    grad_scores = (scaled - wide * delta).astype(jnp.bfloat16)
    grad_qc = mxu(grad_scores, pack_ref[:, VD : VD + KD], NN)
    query_t = query.T
    acc_ref[VD:, :] += mxu(query_t[:KD], grad_scores, NN)
    row = lax.broadcasted_iota(jnp.int32, (block, block), 0)
    col = lax.broadcasted_iota(jnp.int32, (block, block), 1)
    flip = (row + col == block - 1).astype(jnp.bfloat16)
    turned = mxu(flip, grad_scores, NN)
    turned = jnp.concatenate([turned, jnp.zeros((block, block), jnp.float32)], axis=1)
    turned = pltpu.roll(turned, 0, 1, stride=1, stride_axis=0).astype(jnp.bfloat16)
    grad_qp = mxu(
        flip.astype(jnp.float32),
        mxu(turned, rel_ref[pl.ds(base, span), :], NN),
        NN,
        exact_mode,
    )
    pos_turned = mxu(query_t[KD:], flip, NN).astype(jnp.bfloat16)
    drel_ref[:, pl.ds(base, span)] += mxu(pos_turned, turned, NN)
    stat_ref[0:1, :KD] += jnp.sum(grad_qc, axis=0, keepdims=True)
    stat_ref[1:2, :KD] += jnp.sum(grad_qp, axis=0, keepdims=True)
    out_ref[pl.ds(step, 1), VD + KD :, :] = (
        ((grad_qc + grad_qp) * (KD**-0.5)).T.astype(jnp.bfloat16)[None]
    )

    @pl.when(step == steps - 1)
    def _():
        for part in range(steps):
            out_ref[part, : VD + KD, :] = acc_ref[:, part * block : (part + 1) * block].astype(
                jnp.bfloat16
            )


def attend_backward(pack, rel, probs, grad):
    bins = pack.shape[0]
    block = query_block(bins)
    steps = bins // block
    return pl.pallas_call(
        lambda *refs: attend_backward_kernel(block, bins, *refs),
        grid=(steps,),
        in_specs=[
            pl.BlockSpec((bins, PACK), lambda i: (0, 0)),
            pl.BlockSpec((2 * bins, KD), lambda i: (0, 0)),
            pl.BlockSpec((block, bins), lambda i: (i, 0)),
            pl.BlockSpec((1, VD, block), lambda i: (i, 0, 0)),
        ],
        out_specs=[
            pl.BlockSpec((steps, GRAD_PACK, block), lambda i: (0, 0, 0)),
            pl.BlockSpec((KD, 2 * bins), lambda i: (0, 0)),
            pl.BlockSpec((8, 128), lambda i: (0, 0)),
        ],
        out_shape=[
            jax.ShapeDtypeStruct((steps, GRAD_PACK, block), jnp.bfloat16),
            jax.ShapeDtypeStruct((KD, 2 * bins), jnp.float32),
            jax.ShapeDtypeStruct((8, 128), jnp.float32),
        ],
        scratch_shapes=[pltpu.VMEM((VD + KD, bins), jnp.float32)],
        compiler_params=pltpu.CompilerParams(vmem_limit_bytes=48 << 20),
        cost_estimate=pl.CostEstimate(
            flops=2 * bins * bins * 2048, bytes_accessed=2 * bins * bins, transcendentals=0
        ),
        name="attend_backward",
    )(pack, rel, probs, grad)


def heads_kernel(
    track_human,
    track_mouse,
    tiles_human,
    pick_ref,
    rows_ref,
    weight_ref,
    human_own_ref,
    human_oth_ref,
    mouse_own_ref,
    mouse_oth_ref,
    bias_ref,
    count_human_ref,
    count_mouse_ref,
    grad_ref,
    dtrunk_ref,
    dbias_ref,
    loss_ref,
):
    step = pl.program_id(0)
    kind = pick_ref[0]
    swapped = pick_ref[1] == 1
    on_human = jnp.logical_and(step < tiles_human, kind == 0)
    on_mouse = jnp.logical_and(step >= tiles_human, kind == 1)

    @pl.when(step == 0)
    def _():
        dtrunk_ref[...] = jnp.zeros_like(dtrunk_ref)
        loss_ref[...] = jnp.zeros_like(loss_ref)

    def score(own_ref, oth_ref, count_ref, first, tracks):
        track = lax.broadcasted_iota(jnp.int32, (TILE, 1), 0) + first * TILE
        valid = track < tracks
        own = jnp.where(valid, own_ref[...], 0.0).astype(jnp.bfloat16)
        oth = jnp.where(valid, oth_ref[...], 0.0).astype(jnp.bfloat16)
        head = jnp.concatenate(
            [jnp.where(swapped, oth, own), jnp.where(swapped, own, oth)], axis=1
        )
        logits = mxu(head, rows_ref[...], NT) + bias_ref[...]
        counts = count_ref[0].astype(jnp.float32)
        small = jnp.exp(-jnp.abs(logits))
        above = 1.0 + small
        log_above = jnp.log(above) + (small - (above - 1.0)) / above
        shifted = jnp.maximum(logits, 0.0) + log_above
        predicted = shifted
        shifted = shifted + log_eps
        sigma = jnp.where(logits >= 0.0, 1.0, small) / above
        weight = weight_ref[0:1, :]
        rows_loss = weight * (predicted - counts * jnp.log(shifted))
        grad = weight * (sigma - counts * sigma / shifted)
        rows_loss = jnp.where(valid, rows_loss, 0.0)
        grad = jnp.where(valid, grad, 0.0)
        loss_ref[...] += jnp.sum(rows_loss.reshape(TILE // 8, 8, -1), axis=0)
        dbias_ref[...] = jnp.sum(grad, axis=1, keepdims=True)
        grad_low = grad.astype(jnp.bfloat16)
        grad_ref[...] = grad_low
        dtrunk_ref[...] += mxu(grad_low.T, head, NN)

    @pl.when(on_human)
    def _():
        score(human_own_ref, human_oth_ref, count_human_ref, step, track_human)

    @pl.when(on_mouse)
    def _():
        score(mouse_own_ref, mouse_oth_ref, count_mouse_ref, step - tiles_human, track_mouse)

    @pl.when(jnp.logical_not(jnp.logical_or(on_human, on_mouse)))
    def _():
        dbias_ref[...] = jnp.zeros_like(dbias_ref)


def score_heads(window, pick, rows, weight, human, mouse, bias, count_human, count_mouse):
    bins, width = rows.shape
    share = human[0].shape[1]
    rest = width - share
    track_human, track_mouse = count_human.shape[1], count_mouse.shape[1]
    tiles_human, tiles_mouse = pl.cdiv(track_human, TILE), pl.cdiv(track_mouse, TILE)
    tiles = tiles_human + tiles_mouse

    def human_tile(t, p):
        return jnp.where(p[0] == 0, jnp.minimum(t, tiles_human - 1), 0)

    def mouse_tile(t, p):
        return jnp.where(p[0] == 1, jnp.maximum(t - tiles_human, 0), 0)

    whole = lambda t, p: (0, 0)
    along = lambda t, p: (t, 0)
    return pl.pallas_call(
        lambda *refs: heads_kernel(track_human, track_mouse, tiles_human, *refs),
        grid_spec=pltpu.PrefetchScalarGridSpec(
            num_scalar_prefetch=1,
            grid=(tiles,),
            in_specs=[
                pl.BlockSpec((bins, width), whole),
                pl.BlockSpec((8, bins), whole),
                pl.BlockSpec((TILE, share), lambda t, p: (human_tile(t, p), 0)),
                pl.BlockSpec((TILE, rest), lambda t, p: (human_tile(t, p), 0)),
                pl.BlockSpec((TILE, share), lambda t, p: (mouse_tile(t, p), 0)),
                pl.BlockSpec((TILE, rest), lambda t, p: (mouse_tile(t, p), 0)),
                pl.BlockSpec((TILE, 1), along),
                pl.BlockSpec((1, TILE, bins), lambda t, p: (window, human_tile(t, p), 0)),
                pl.BlockSpec((1, TILE, bins), lambda t, p: (window, mouse_tile(t, p), 0)),
            ],
            out_specs=[
                pl.BlockSpec((TILE, bins), along),
                pl.BlockSpec((bins, width), whole),
                pl.BlockSpec((TILE, 1), along),
                pl.BlockSpec((8, bins), whole),
            ],
        ),
        out_shape=[
            jax.ShapeDtypeStruct((tiles * TILE, bins), jnp.bfloat16),
            jax.ShapeDtypeStruct((bins, width), jnp.float32),
            jax.ShapeDtypeStruct((tiles * TILE, 1), jnp.float32),
            jax.ShapeDtypeStruct((8, bins), jnp.float32),
        ],
        compiler_params=pltpu.CompilerParams(vmem_limit_bytes=56 << 20),
        cost_estimate=pl.CostEstimate(
            flops=4 * bins * width * track_human,
            bytes_accessed=4 * width * track_human,
            transcendentals=4 * bins * track_human,
        ),
        name="score_heads",
    )(pick, rows, weight, *human, *mouse, bias, count_human, count_mouse)


def head_grads_kernel(windows, tiles_human, pick_ref, *refs):
    grads, rows, out_ref, acc_ref = refs[:windows], refs[windows], refs[windows + 1], refs[-1]
    step = pl.program_id(0)
    mine = jnp.where(step < tiles_human, 0, 1)
    acc_ref[...] = jnp.zeros_like(acc_ref)
    for window in range(windows):

        @pl.when(pick_ref[window] == mine)
        def _():
            acc_ref[...] += mxu(grads[window][...], rows[window], NN)

    out_ref[...] = acc_ref[...].astype(jnp.bfloat16)


def head_grads(pick, grads, rows, tiles_human):
    windows, bins, share = rows.shape
    tiles = grads[0].shape[0] // TILE

    def tile_of(window):
        def index(t, p):
            first = jnp.where(p[window] == 0, jnp.minimum(t, tiles_human - 1), 0)
            return (jnp.where(p[window] == 1, jnp.maximum(t, tiles_human), first), 0)

        return index

    return pl.pallas_call(
        lambda *refs: head_grads_kernel(windows, tiles_human, *refs),
        grid_spec=pltpu.PrefetchScalarGridSpec(
            num_scalar_prefetch=1,
            grid=(tiles,),
            in_specs=[pl.BlockSpec((TILE, bins), tile_of(w)) for w in range(windows)]
            + [pl.BlockSpec((windows, bins, share), lambda t, p: (0, 0, 0))],
            out_specs=pl.BlockSpec((TILE, share), lambda t, p: (t, 0)),
            scratch_shapes=[pltpu.VMEM((TILE, share), jnp.float32)],
        ),
        out_shape=jax.ShapeDtypeStruct((tiles * TILE, share), jnp.bfloat16),
        compiler_params=pltpu.CompilerParams(vmem_limit_bytes=40 << 20),
        cost_estimate=pl.CostEstimate(
            flops=2 * windows * bins * share * tiles * TILE,
            bytes_accessed=4 * tiles * TILE * share,
            transcendentals=0,
        ),
        name="head_grads",
    )(pick, *grads, rows)


def norm_stats(values):
    mean = jnp.mean(values, axis=-1, keepdims=True)
    centred = values - mean
    inverse = lax.rsqrt(jnp.mean(centred * centred, axis=-1, keepdims=True) + norm_eps)
    return mean, inverse


def norm_backward(grad_output, scaled, inverse, norm_gain):
    grad_scaled = grad_output * norm_gain
    mean_grad = jnp.mean(grad_scaled, axis=-1, keepdims=True)
    mean_proj = jnp.mean(grad_scaled * scaled, axis=-1, keepdims=True)
    grad_input = inverse * (grad_scaled - mean_grad - scaled * mean_proj)
    return (grad_input, jnp.sum(grad_output * scaled, axis=0), jnp.sum(grad_output, axis=0))


def sum_over_model(partial):
    low = partial.astype(jnp.bfloat16)
    if lax.axis_size("mp") == 2:
        other = lax.ppermute(low, "mp", [(0, 1), (1, 0)])
        return low.astype(jnp.float32) + other.astype(jnp.float32)
    return lax.psum(low, "mp").astype(jnp.float32)


def in_model_order(own, dim):
    if lax.axis_size("mp") == 2:
        first = lax.axis_index("mp") == 0
        other = lax.ppermute(own, "mp", [(0, 1), (1, 0)])
        return jnp.concatenate(
            [jnp.where(first, own, other), jnp.where(first, other, own)], axis=dim
        )
    return lax.all_gather(own, "mp", axis=dim, tiled=True)


def other_rows(own, chunk):
    count = lax.axis_size("dp") * lax.axis_size("seq")
    place = lax.axis_index("dp") * lax.axis_size("seq") + lax.axis_index("seq")
    rows = own.shape[0]
    start = jnp.minimum(place * chunk, rows - chunk)
    part = lax.dynamic_slice_in_dim(own, start, chunk, 0)
    if count * chunk != rows:
        part = lax.dynamic_slice_in_dim(
            jnp.concatenate([part, part], axis=0),
            jnp.minimum(place * chunk - start, chunk),
            chunk,
            0,
        )
    part = lax.ppermute(part, "mp", [(0, 1), (1, 0)])
    return lax.all_gather(part, ("dp", "seq"), axis=0, tiled=True)


def swap_pairs(axis, step):
    return [(i, i ^ step) for i in range(lax.axis_size(axis))]


def sum_everywhere(vector):
    for axis in ("dp", "seq"):
        step = 1
        while step < lax.axis_size(axis):
            vector = vector + lax.ppermute(vector, axis, swap_pairs(axis, step))
            step *= 2
    return vector


def scatter_product(left, right):
    dp_size, seq_size = lax.axis_size("dp"), lax.axis_size("seq")
    dp_index, seq_index = lax.axis_index("dp"), lax.axis_index("seq")
    width = left.shape[1]
    slab = width // dp_size
    rows = slab // seq_size

    def half(parity):
        return jnp.concatenate(
            [left[:, i * slab : (i + 1) * slab] for i in range(parity, dp_size, 2)], axis=1
        )

    even = dp_index % 2 == 0
    kept, sent = jnp.where(even, half(0), half(1)), jnp.where(even, half(1), half(0))
    got = lax.ppermute(mxu(sent, right, TN).astype(jnp.bfloat16), "dp", swap_pairs("dp", 1))
    kept = mxu(kept, right, TN) + got.astype(jnp.float32)
    step = dp_size
    while step > 2:
        step //= 2
        size = kept.shape[0] // 2
        upper = (dp_index // step) % 2 == 1
        low, high = kept[:size], kept[size:]
        got = lax.ppermute(
            jnp.where(upper, low, high).astype(jnp.bfloat16), "dp", swap_pairs("dp", step)
        )
        kept = jnp.where(upper, high, low) + got.astype(jnp.float32)
    parts = kept.astype(jnp.bfloat16).reshape(seq_size, rows, -1)
    total = lax.dynamic_index_in_dim(parts, seq_index, 0, keepdims=False).astype(jnp.float32)
    for step in range(1, seq_size):
        other = seq_index ^ step
        got = lax.ppermute(
            lax.dynamic_index_in_dim(parts, other, 0, keepdims=False), "seq", swap_pairs("seq", step)
        )
        total = total + got.astype(jnp.float32)
    return total


def on_device(
    trunk_in,
    norm1_gain,
    norm1_bias,
    w_query,
    w_key,
    w_value,
    w_rel,
    content_bias,
    pos_bias,
    w_out,
    b_out,
    norm2_gain,
    norm2_bias,
    w_in,
    b_in,
    w_hid,
    b_hid,
    head_human,
    bias_human,
    head_mouse,
    bias_mouse,
    species,
    targets_human,
    targets_mouse,
):
    windows, bins, width = trunk_in.shape
    heads = content_bias.shape[0]
    dp_size, seq_size, mp_size = (lax.axis_size(axis) for axis in ("dp", "seq", "mp"))
    seq_index, mp_index = lax.axis_index("seq"), lax.axis_index("mp")
    place = lax.axis_index("dp") * seq_size + seq_index
    places = dp_size * seq_size
    all_bins = bins * seq_size
    block = query_block(all_bins)
    query_start = seq_index * bins
    key_scale = KD ** (-0.5)
    loss_scale = 1.0 / math.sqrt(windows * dp_size * CROP)
    crop_start = (all_bins - CROP) // 2
    bf16 = jnp.bfloat16

    if heads % seq_size == 0:
        groups = [[w] for w in range(windows)]
    else:
        groups = [list(range(windows))]
    group_size = len(groups[0])
    pairs = heads * group_size
    pairs_here = -(-pairs // seq_size)
    pair_heads = [
        jnp.minimum((seq_index * pairs_here + j) // group_size, heads - 1)
        for j in range(pairs_here)
    ]

    def spread(array):
        short = seq_size * pairs_here - pairs
        if short:
            array = jnp.pad(array, [(0, short)] + [(0, 0)] * (array.ndim - 1))
        return exchange(array.reshape((seq_size, pairs_here) + array.shape[1:]))

    def exchange(array):
        result = array
        for step in range(1, seq_size):
            other = seq_index ^ step
            block_out = lax.dynamic_index_in_dim(array, other, 0, keepdims=True)
            block_in = lax.ppermute(block_out, "seq", swap_pairs("seq", step))
            result = lax.dynamic_update_slice_in_dim(result, block_in, other, 0)
        return result

    def bins_last(array):
        if bins == block:
            return array
        depth = array.shape[1]
        array = array.transpose(1, 0, 2).reshape(depth, all_bins // block, block)
        return array.transpose(1, 0, 2)

    def owners_first(array):
        if bins == block:
            return array
        depth = array.shape[1]
        array = array.transpose(1, 0, 2).reshape(depth, seq_size, bins)
        return array.transpose(1, 0, 2)

    def collect(arrays):
        depth = arrays[0].shape[1]
        stacked = jnp.stack([owners_first(a) for a in arrays], axis=1)
        stacked = exchange(stacked).reshape(seq_size * pairs_here, depth, bins)[:pairs]
        stacked = stacked.reshape(heads, group_size, depth, bins).transpose(0, 2, 1, 3)
        return stacked.reshape(heads, depth, group_size * bins)

    def all_rows(own, chunk):
        if mp_size != 2:
            full = lax.all_gather(own, "mp", axis=1, tiled=True)
            half = full.shape[1] // 2
            return (full[:, :half], full[:, half:])
        return (own, other_rows(own, chunk))

    def chunk_of(rows):
        return -(-rows // (places * 16)) * 16

    if mp_size == 2:
        out_oth = other_rows(w_out, w_out.shape[0] // places)
        first = mp_index == 0
        w_out_all = jnp.concatenate(
            [jnp.where(first, w_out, out_oth), jnp.where(first, out_oth, w_out)], axis=0
        )
    else:
        w_out_all = lax.all_gather(w_out, "mp", axis=0, tiled=True)
    track_human, track_mouse = head_human.shape[1], head_mouse.shape[1]
    human = all_rows(head_human.T, chunk_of(track_human))
    mouse = all_rows(head_mouse.T, chunk_of(track_mouse))

    def per_head(weight, size):
        return weight.reshape(width, heads, size)

    value_w, key_w, query_w = per_head(w_value, VD), per_head(w_key, KD), per_head(w_query, KD)
    w_pack = jnp.concatenate([value_w, key_w, query_w, query_w], axis=2).reshape(
        width, heads * PACK
    )
    w_grad = jnp.concatenate([value_w, key_w, query_w], axis=2).reshape(width, heads * GRAD_PACK)
    pack_scale = jnp.concatenate(
        [jnp.ones((VD + KD,), jnp.float32), jnp.full((2 * KD,), key_scale, jnp.float32)]
    )
    pack_scale = jnp.tile(pack_scale, heads)
    pack_bias = jnp.concatenate(
        [jnp.zeros((heads, VD + KD), jnp.float32), content_bias, pos_bias], axis=1
    ).reshape(-1)

    basis = jnp.pad(rel_basis(), [(0, 1), (0, 0)])
    w_rel_heads = w_rel.reshape(FEAT, heads, KD)
    rels = [
        mxu(
            basis,
            lax.dynamic_index_in_dim(w_rel_heads, head, 1, keepdims=False).astype(jnp.float32),
            NN,
            exact_mode,
        ).astype(bf16)
        for head in pair_heads
    ]

    trunk, stats1, normed1, packs = [], [], [], []
    for group in groups:
        rows = group_size * bins
        values = trunk_in[group[0] : group[-1] + 1].reshape(rows, width).astype(jnp.float32)
        mean, inverse = norm_stats(values)
        normed = ((values - mean) * inverse * norm1_gain + norm1_bias).astype(bf16)
        pack = (mxu(normed, w_pack, NN) * pack_scale + pack_bias).astype(bf16)
        pack = pack.reshape(group_size, bins, heads, PACK).transpose(2, 0, 1, 3)
        pack = spread(pack.reshape(pairs, bins, PACK))
        trunk.append(values)
        stats1.append((mean, inverse))
        normed1.append(normed)
        packs.append([pack[:, j].reshape(all_bins, PACK) for j in range(pairs_here)])

    probs, attended, mids, stats2, normed2, preacts, actives, trunk_out, trunk_low = (
        [] for _ in range(9)
    )
    for g, group in enumerate(groups):
        outs, kept = [], []
        for j in range(pairs_here):
            out, prob = attend_forward(packs[g][j], rels[j])
            outs.append(out)
            kept.append(prob)
        probs.append(kept)
        att = collect(outs).reshape(heads * VD, group_size * bins)
        attended.append(att)
        att_all = in_model_order(att, 0)
        mid = trunk[g] + mxu(att_all, w_out_all, TN) + b_out
        mean, inverse = norm_stats(mid)
        normed = ((mid - mean) * inverse * norm2_gain + norm2_bias).astype(bf16)
        preact = mxu(normed, w_in, NN) + b_in
        active = jnp.maximum(preact, 0.0).astype(bf16)
        out = mid + (sum_over_model(mxu(active, w_hid, NN)) + b_hid)
        mids.append(mid)
        stats2.append((mean, inverse))
        normed2.append(normed)
        preacts.append(preact > 0.0)
        actives.append(active)
        trunk_out.append(out)
        trunk_low.append(out.astype(bf16))

    bin_place = query_start + jnp.arange(bins)
    in_crop = ((bin_place >= crop_start) & (bin_place < crop_start + CROP)).astype(jnp.float32)
    weight = jnp.broadcast_to((in_crop * loss_scale)[None, :], (8, bins))
    has_crop = (query_start + bins > crop_start) & (query_start < crop_start + CROP)
    picks = jnp.where(has_crop, species, 2)
    count_human = targets_human.transpose(0, 2, 1)
    count_mouse = targets_mouse.transpose(0, 2, 1)
    tiles_human, tiles_mouse = pl.cdiv(track_human, TILE), pl.cdiv(track_mouse, TILE)
    bias_all = jnp.concatenate(
        [
            jnp.pad(bias_human, (0, tiles_human * TILE - track_human)),
            jnp.pad(bias_mouse, (0, tiles_mouse * TILE - track_mouse)),
        ]
    )[:, None]
    order = mp_index if mp_size == 2 else 0
    grad_rows, logit_grads, track_sums, losses = [], [], [], []
    low_windows = [
        trunk_low[g][i * bins : (i + 1) * bins] for g in range(len(groups)) for i in range(group_size)
    ]
    for window in range(windows):
        pick = jnp.stack([picks[window], jnp.int32(0) + order])
        grad_low, grad_out, track_sum, loss = score_heads(
            window, pick, low_windows[window], weight, human, mouse, bias_all, count_human, count_mouse
        )
        logit_grads.append(grad_low)
        grad_rows.append(grad_out)
        track_sums.append(track_sum)
        losses.append(jnp.sum(loss))
    share = head_human.shape[0]
    own_rows = jnp.stack(
        [lax.dynamic_slice_in_dim(rows, mp_index * share, share, 1) for rows in low_windows]
    )
    dheads = head_grads(picks, logit_grads, own_rows, tiles_human)
    dheads = lax.psum(dheads, ("dp", "seq"))
    dtracks = sum(track_sums)[:, 0]

    grad_mids, grad_outs, grad_pres, grad_mid_lows, packed_grads = [], [], [], [], []
    sums = [0.0] * 5
    drels = [0.0] * pairs_here
    dstats = [0.0] * pairs_here
    for g, group in enumerate(groups):
        grad_trunk = jnp.concatenate([grad_rows[w] for w in group], axis=0)
        grad_out = grad_trunk.astype(bf16)
        grad_preact = jnp.where(preacts[g], mxu(grad_out, w_hid, NT), 0.0)
        grad_pre = grad_preact.astype(bf16)
        grad_normed = sum_over_model(mxu(grad_pre, w_in, NT))
        mean, inverse = stats2[g]
        grad_norm, dgain, dbias = norm_backward(
            grad_normed, (mids[g] - mean) * inverse, inverse, norm2_gain
        )
        grad_mid = grad_trunk + grad_norm
        grad_mid_low = grad_mid.astype(bf16)
        parts = (
            dgain,
            dbias,
            jnp.sum(grad_mid, axis=0),
            jnp.sum(grad_trunk, axis=0),
            jnp.sum(grad_preact, axis=0),
        )
        sums = [old + new for old, new in zip(sums, parts)]
        grad_outs.append(grad_out)
        grad_pres.append(grad_pre)
        grad_mids.append(grad_mid)
        grad_mid_lows.append(grad_mid_low)
        grad_att = mxu(w_out, grad_mid_low, NT).astype(bf16)
        grad_att = grad_att.reshape(heads, VD, group_size, bins).transpose(0, 2, 1, 3)
        grad_att = spread(grad_att.reshape(pairs, VD, bins))
        outs = []
        for j in range(pairs_here):
            out, drel, stat = attend_backward(
                packs[g][j], rels[j], probs[g][j], bins_last(grad_att[:, j])
            )
            outs.append(out)
            drels[j] = drels[j] + drel
            dstats[j] = dstats[j] + stat
        packed_grads.append(collect(outs).reshape(heads * GRAD_PACK, group_size * bins))

    join = lambda arrays: jnp.concatenate(arrays, axis=0)
    dw_in = scatter_product(join(normed2), join(grad_pres))
    dw_hid = scatter_product(join(grad_outs), join(actives))
    dw_out = scatter_product(join(grad_mid_lows), jnp.concatenate(attended, axis=1).T)

    grad_inputs = []
    sums1 = [0.0, 0.0]
    for g, group in enumerate(groups):
        grad_normed = sum_over_model(
            lax.dot_general(
                packed_grads[g],
                w_grad,
                (((0,), (1,)), ((), ())),
                preferred_element_type=jnp.float32,
            )
        )
        mean, inverse = stats1[g]
        grad_norm, dgain, dbias = norm_backward(
            grad_normed, (trunk[g] - mean) * inverse, inverse, norm1_gain
        )
        sums1 = [sums1[0] + dgain, sums1[1] + dbias]
        grad_inputs.append((grad_mids[g] + grad_norm).reshape(group_size, bins, width))
    pack_summed = scatter_product(join(normed1), jnp.concatenate(packed_grads, axis=1).T)
    pack_summed = pack_summed.reshape(-1, heads, GRAD_PACK)

    dw_rel = jnp.zeros((heads, FEAT, KD), jnp.float32)
    dstat = jnp.zeros((heads, 2, KD), jnp.float32)
    for j, head in enumerate(pair_heads):
        mine = (jnp.arange(heads) == head).astype(jnp.float32)[:, None, None]
        part = lax.dot_general(
            basis,
            drels[j],
            (((0,), (1,)), ((), ())),
            precision=exact_mode,
            preferred_element_type=jnp.float32,
        )
        dw_rel = dw_rel + mine * part
        dstat = dstat + mine * dstats[j][None, :2, :KD]

    def sum_parts(parts):
        sizes = [part.size for part in parts]
        flat = [part.reshape(-1) for part in parts]
        flat = [jnp.pad(part, (0, -part.size % 128)) for part in flat]
        total = sum_everywhere(jnp.concatenate(flat).reshape(-1, 128)).reshape(-1)
        results, start = [], 0
        for part, size in zip(parts, sizes):
            results.append(total[start : start + size].reshape(part.shape))
            start += -(-size // 128) * 128
        return results

    dgain2, dbias2, db_out, db_hid, db_in, dtracks, loss = sum_parts(
        list(sums) + [dtracks, sum(losses)[None]]
    )
    dgain1, dbias1, dstat, dw_rel = sum_parts(list(sums1) + [dstat, dw_rel])

    def own(array, dim=0):
        size = array.shape[dim] // places
        return lax.dynamic_slice_in_dim(array, place * size, size, dim)

    rel_rows = own(dw_rel, 1).transpose(1, 0, 2).reshape(-1, heads * KD)
    pack_rows = pack_summed.shape[0]
    mouse_start = tiles_human * TILE
    shape3 = (windows, bins, width)
    return (
        join(trunk_out).reshape(shape3),
        loss[0],
        join(grad_inputs).reshape(shape3),
        own(dgain1),
        own(dbias1),
        pack_summed[:, :, VD + KD :].reshape(pack_rows, heads * KD),
        pack_summed[:, :, VD : VD + KD].reshape(pack_rows, heads * KD),
        pack_summed[:, :, :VD].reshape(pack_rows, heads * VD),
        rel_rows,
        own(dstat[:, 0], 1),
        own(dstat[:, 1], 1),
        dw_out.T,
        own(db_out),
        own(dgain2),
        own(dbias2),
        dw_in,
        db_in,
        dw_hid.T,
        own(db_hid),
        dheads[:track_human].astype(jnp.float32).T,
        dtracks[:track_human],
        dheads[mouse_start : mouse_start + track_mouse].astype(jnp.float32).T,
        dtracks[mouse_start : mouse_start + track_mouse],
    )


def solution(mesh):
    in_specs = (
        P("dp", "seq", None),
        P(),
        P(),
        P(None, "mp"),
        P(None, "mp"),
        P(None, "mp"),
        P(None, "mp"),
        P("mp", None),
        P("mp", None),
        P("mp", None),
        P(),
        P(),
        P(),
        P(None, "mp"),
        P("mp"),
        P("mp", None),
        P(),
        P("mp", None),
        P(),
        P("mp", None),
        P(),
        P("dp"),
        P("dp", "seq", None),
        P("dp", "seq", None),
    )
    out_specs = (
        P("dp", "seq", None),
        P(),
        P("dp", "seq", None),
        P(("dp", "seq")),
        P(("dp", "seq")),
        P(("dp", "seq"), "mp"),
        P(("dp", "seq"), "mp"),
        P(("dp", "seq"), "mp"),
        P(("dp", "seq"), "mp"),
        P("mp", ("dp", "seq")),
        P("mp", ("dp", "seq")),
        P("mp", ("dp", "seq")),
        P(("dp", "seq")),
        P(("dp", "seq")),
        P(("dp", "seq")),
        P(("dp", "seq"), "mp"),
        P("mp"),
        P("mp", ("dp", "seq")),
        P(("dp", "seq")),
        P("mp", None),
        P(),
        P("mp", None),
        P(),
    )
    return jax.shard_map(
        on_device, mesh=mesh, in_specs=in_specs, out_specs=out_specs, check_vma=False
    )
```

```python
import math

import jax
import jax.numpy as jnp
from jax import lax
from jax.experimental import pallas as pl
from jax.experimental.pallas import tpu as pltpu
from jax.sharding import PartitionSpec as P

KD = 64
VD = 192
FEAT = 192
BINS = 1536
CROP = 896


norm_eps = 1e-05
log_eps = 1e-07
exact_mode = lax.Precision.HIGHEST


def rel_basis():
    per_class = FEAT // 6
    distance = jnp.arange(-(BINS - 1), BINS).astype(jnp.float32)
    magnitude = jnp.abs(distance)[:, None]
    half_life = (2.0 ** jnp.linspace(3.0, math.log2(BINS), per_class)).astype(jnp.float32)
    decays = jnp.exp(-math.log(2.0) / half_life[None, :] * magnitude)
    widths = (2.0 ** jnp.arange(1, per_class + 1)).astype(jnp.float32) - 1.0
    central = (widths[None, :] > magnitude).astype(jnp.float32)
    spread = BINS / (2.0 * per_class)
    centre = jnp.linspace(BINS / per_class, BINS, per_class).astype(jnp.float32)
    concentration = (centre / spread) ** 2
    rate_param = centre / spread**2
    peak_at = (concentration - 1.0) / rate_param
    log_ratio = (concentration - 1.0) * (
        jnp.log(jnp.maximum(magnitude, 1e-20)) - jnp.log(peak_at)
    ) - rate_param * (magnitude - peak_at)
    density = jnp.exp(log_ratio)
    gammas = density / jnp.max(density, axis=0, keepdims=True)
    symmetric = jnp.concatenate([decays, central, gammas], axis=1)
    return jnp.concatenate([symmetric, jnp.sign(distance)[:, None] * symmetric], axis=1)


PACK = VD + 3 * KD
GRAD_PACK = VD + 2 * KD
TILE = 896
NN = (((1,), (0,)), ((), ()))
NT = (((1,), (1,)), ((), ()))
TN = (((0,), (0,)), ((), ()))


def mxu(left_arr, right_arr, dims, precision=None):
    return lax.dot_general(
        left_arr, right_arr, dims, precision=precision, preferred_element_type=jnp.float32
    )


def query_block(bins):
    for block in (384, 256, 128):
        if bins % block == 0:
            return block
    return bins


def attend_forward_kernel(block, bins, pack_ref, rel_ref, out_ref, probs_ref):
    step = pl.program_id(0)
    span = bins + block
    query = pack_ref[pl.ds(pl.multiple_of(step * block, block), block), VD + KD :]
    base = pl.multiple_of(bins - block - step * block, block)
    content = mxu(query[:, :KD], pack_ref[:, VD : VD + KD], NT)
    position = mxu(query[:, KD:], rel_ref[pl.ds(base, span), :], NT)
    position = pltpu.roll(position, span - (block - 1), 1, stride=1, stride_axis=0)
    scores = content + position[:, :bins]
    exps = jnp.exp(scores - jnp.max(scores, axis=1, keepdims=True))
    probs = (exps * (1.0 / jnp.sum(exps, axis=1, keepdims=True))).astype(jnp.bfloat16)
    probs_ref[...] = probs
    out_ref[0] = mxu(probs, pack_ref[:, :VD], NN).T.astype(jnp.bfloat16)


def attend_forward(pack, rel):
    bins = pack.shape[0]
    block = query_block(bins)
    steps = bins // block
    return pl.pallas_call(
        lambda *refs: attend_forward_kernel(block, bins, *refs),
        grid=(steps,),
        in_specs=[
            pl.BlockSpec((bins, PACK), lambda i: (0, 0)),
            pl.BlockSpec((2 * bins, KD), lambda i: (0, 0)),
        ],
        out_specs=[
            pl.BlockSpec((1, VD, block), lambda i: (i, 0, 0)),
            pl.BlockSpec((block, bins), lambda i: (i, 0)),
        ],
        out_shape=[
            jax.ShapeDtypeStruct((steps, VD, block), jnp.bfloat16),
            jax.ShapeDtypeStruct((bins, bins), jnp.bfloat16),
        ],
        compiler_params=pltpu.CompilerParams(vmem_limit_bytes=48 << 20),
        cost_estimate=pl.CostEstimate(
            flops=2 * bins * bins * 1024, bytes_accessed=2 * bins * bins, transcendentals=bins * bins
        ),
        name="attend_forward",
    )(pack, rel)


def attend_backward_kernel(
    block, bins, pack_ref, rel_ref, probs_ref, grad_ref, out_ref, drel_ref, stat_ref, acc_ref
):
    step = pl.program_id(0)
    steps = bins // block
    span = bins + block

    @pl.when(step == 0)
    def _():
        acc_ref[...] = jnp.zeros_like(acc_ref)
        drel_ref[...] = jnp.zeros_like(drel_ref)
        stat_ref[...] = jnp.zeros_like(stat_ref)

    query = pack_ref[pl.ds(pl.multiple_of(step * block, block), block), VD + KD :]
    base = pl.multiple_of(bins - block - step * block, block)
    grad_t = grad_ref[0]
    probs = probs_ref[...]
    acc_ref[:VD, :] += mxu(grad_t, probs, NN)
    grad_probs = mxu(grad_t.T, pack_ref[:, :VD], NT)
    wide = probs.astype(jnp.float32)
    scaled = wide * grad_probs
    delta = jnp.sum(scaled, axis=1, keepdims=True)
    grad_scores = (scaled - wide * delta).astype(jnp.bfloat16)
    grad_qc = mxu(grad_scores, pack_ref[:, VD : VD + KD], NN)
    query_t = query.T
    acc_ref[VD:, :] += mxu(query_t[:KD], grad_scores, NN)
    row = lax.broadcasted_iota(jnp.int32, (block, block), 0)
    col = lax.broadcasted_iota(jnp.int32, (block, block), 1)
    flip = (row + col == block - 1).astype(jnp.bfloat16)
    turned = mxu(flip, grad_scores, NN)
    turned = jnp.concatenate([turned, jnp.zeros((block, block), jnp.float32)], axis=1)
    turned = pltpu.roll(turned, 0, 1, stride=1, stride_axis=0).astype(jnp.bfloat16)
    grad_qp = mxu(
        flip.astype(jnp.float32),
        mxu(turned, rel_ref[pl.ds(base, span), :], NN),
        NN,
        exact_mode,
    )
    pos_turned = mxu(query_t[KD:], flip, NN).astype(jnp.bfloat16)
    drel_ref[:, pl.ds(base, span)] += mxu(pos_turned, turned, NN)
    stat_ref[0:1, :KD] += jnp.sum(grad_qc, axis=0, keepdims=True)
    stat_ref[1:2, :KD] += jnp.sum(grad_qp, axis=0, keepdims=True)
    out_ref[pl.ds(step, 1), VD + KD :, :] = (
        ((grad_qc + grad_qp) * (KD**-0.5)).T.astype(jnp.bfloat16)[None]
    )

    @pl.when(step == steps - 1)
    def _():
        for part in range(steps):
            out_ref[part, : VD + KD, :] = acc_ref[:, part * block : (part + 1) * block].astype(
                jnp.bfloat16
            )


def attend_backward(pack, rel, probs, grad):
    bins = pack.shape[0]
    block = query_block(bins)
    steps = bins // block
    return pl.pallas_call(
        lambda *refs: attend_backward_kernel(block, bins, *refs),
        grid=(steps,),
        in_specs=[
            pl.BlockSpec((bins, PACK), lambda i: (0, 0)),
            pl.BlockSpec((2 * bins, KD), lambda i: (0, 0)),
            pl.BlockSpec((block, bins), lambda i: (i, 0)),
            pl.BlockSpec((1, VD, block), lambda i: (i, 0, 0)),
        ],
        out_specs=[
            pl.BlockSpec((steps, GRAD_PACK, block), lambda i: (0, 0, 0)),
            pl.BlockSpec((KD, 2 * bins), lambda i: (0, 0)),
            pl.BlockSpec((8, 128), lambda i: (0, 0)),
        ],
        out_shape=[
            jax.ShapeDtypeStruct((steps, GRAD_PACK, block), jnp.bfloat16),
            jax.ShapeDtypeStruct((KD, 2 * bins), jnp.float32),
            jax.ShapeDtypeStruct((8, 128), jnp.float32),
        ],
        scratch_shapes=[pltpu.VMEM((VD + KD, bins), jnp.float32)],
        compiler_params=pltpu.CompilerParams(vmem_limit_bytes=48 << 20),
        cost_estimate=pl.CostEstimate(
            flops=2 * bins * bins * 2048, bytes_accessed=2 * bins * bins, transcendentals=0
        ),
        name="attend_backward",
    )(pack, rel, probs, grad)


def heads_kernel(
    track_human,
    track_mouse,
    pick_ref,
    rows_ref,
    weight_ref,
    human_ref,
    mouse_ref,
    human_other_ref,
    mouse_other_ref,
    bias_ref,
    count_human_ref,
    count_mouse_ref,
    grad_ref,
    dtrunk_ref,
    dbias_ref,
    loss_ref,
):
    step = pl.program_id(0)
    kind, swapped = pick_ref[0], pick_ref[1] == 1

    @pl.when(step == 0)
    def _():
        dtrunk_ref[...] = jnp.zeros_like(dtrunk_ref)
        loss_ref[...] = jnp.zeros_like(loss_ref)

    def score(own_ref, other_ref, count_ref, tracks):
        valid = lax.broadcasted_iota(jnp.int32, (TILE, 1), 0) + step * TILE < tracks
        own = jnp.where(valid, own_ref[...], 0.0).astype(jnp.bfloat16)
        oth = jnp.where(valid, other_ref[...], 0.0).astype(jnp.bfloat16)
        head = jnp.concatenate(
            [jnp.where(swapped, oth, own), jnp.where(swapped, own, oth)], axis=1
        )
        logits = mxu(head, rows_ref[...], NT) + bias_ref[:, 0:1]
        counts = count_ref[0].astype(jnp.float32)
        small = jnp.exp(-jnp.abs(logits))
        inverse = 1.0 / (1.0 + small)
        predicted = jnp.maximum(logits, 0.0) + jnp.log1p(small)
        shifted = predicted + log_eps
        sigma = jnp.where(logits >= 0.0, 1.0, small) * inverse
        weight = jnp.where(valid, weight_ref[0:1, :], 0.0)
        rows_loss = weight * (predicted - counts * jnp.log(shifted))
        grad = weight * (sigma - counts * sigma / shifted)
        loss_ref[...] += jnp.sum(rows_loss.reshape(TILE // 8, 8, -1), axis=0)
        bins = grad.shape[1]
        if bins % 128 == 0:
            folded = sum(grad[:, i : i + 128] for i in range(0, bins, 128))
        else:
            folded = jnp.broadcast_to(jnp.sum(grad, axis=1, keepdims=True) / 128, (TILE, 128))
        dbias_ref[...] = jnp.sum(folded.T.reshape(16, 8, TILE), axis=0)
        grad_low = grad.astype(jnp.bfloat16)
        grad_ref[...] = grad_low
        dtrunk_ref[...] += mxu(grad_low.T, head, NN)

    @pl.when(jnp.logical_and(kind == 0, step < pl.cdiv(track_human, TILE)))
    def _():
        score(human_ref, human_other_ref, count_human_ref, track_human)

    @pl.when(jnp.logical_and(kind == 1, step < pl.cdiv(track_mouse, TILE)))
    def _():
        score(mouse_ref, mouse_other_ref, count_mouse_ref, track_mouse)


def score_heads(window, pick, rows, weight, own, others, bias, count_human, count_mouse):
    bins, width = rows.shape
    share = own[0].shape[1]
    rest = width - share
    track_human, track_mouse = count_human.shape[1], count_mouse.shape[1]
    tiles_human, tiles_mouse = pl.cdiv(track_human, TILE), pl.cdiv(track_mouse, TILE)

    def tile(kind, tiles):
        return lambda t, p: jnp.where(p[0] == kind, jnp.minimum(t, tiles - 1), 0)

    human_tile, mouse_tile = tile(0, tiles_human), tile(1, tiles_mouse)

    def out_tile(t, p):
        mine = jnp.where(p[0] == 0, jnp.minimum(t, tiles_human - 1), 0)
        return jnp.where(p[0] == 1, tiles_human + jnp.minimum(t, tiles_mouse - 1), mine)

    whole = lambda t, p: (0, 0)
    tracks = (tiles_human + tiles_mouse) * TILE
    return pl.pallas_call(
        lambda *refs: heads_kernel(track_human, track_mouse, *refs),
        grid_spec=pltpu.PrefetchScalarGridSpec(
            num_scalar_prefetch=1,
            grid=(max(tiles_human, tiles_mouse),),
            in_specs=[
                pl.BlockSpec((bins, width), whole),
                pl.BlockSpec((8, bins), whole),
                pl.BlockSpec((TILE, share), lambda t, p: (human_tile(t, p), 0)),
                pl.BlockSpec((TILE, share), lambda t, p: (mouse_tile(t, p), 0)),
                pl.BlockSpec((TILE, rest), lambda t, p: (human_tile(t, p), 0)),
                pl.BlockSpec((TILE, rest), lambda t, p: (mouse_tile(t, p), 0)),
                pl.BlockSpec((TILE, 128), lambda t, p: (out_tile(t, p), 0)),
                pl.BlockSpec((1, TILE, bins), lambda t, p: (window, human_tile(t, p), 0)),
                pl.BlockSpec((1, TILE, bins), lambda t, p: (window, mouse_tile(t, p), 0)),
            ],
            out_specs=[
                pl.BlockSpec((TILE, bins), lambda t, p: (out_tile(t, p), 0)),
                pl.BlockSpec((bins, width), whole),
                pl.BlockSpec((8, TILE), lambda t, p: (0, out_tile(t, p))),
                pl.BlockSpec((8, bins), whole),
            ],
        ),
        out_shape=[
            jax.ShapeDtypeStruct((tracks, bins), jnp.bfloat16),
            jax.ShapeDtypeStruct((bins, width), jnp.float32),
            jax.ShapeDtypeStruct((8, tracks), jnp.float32),
            jax.ShapeDtypeStruct((8, bins), jnp.float32),
        ],
        compiler_params=pltpu.CompilerParams(vmem_limit_bytes=56 << 20),
        cost_estimate=pl.CostEstimate(
            flops=4 * bins * width * track_human,
            bytes_accessed=4 * width * track_human,
            transcendentals=4 * bins * track_human,
        ),
        name="score_heads",
    )(pick, rows, weight, *own, *others, bias, count_human, count_mouse)


def head_tile(step, parity, quarter):
    upper = jnp.where(step >= quarter, 1, 0)
    return upper * quarter + parity * quarter + step


def head_grads_kernel(windows, tiles_human, quarter, has_more, pick_ref, *refs):
    grads, rows, out_ref, acc_ref = refs[:windows], refs[windows], refs[-2], refs[-1]
    tile = head_tile(pl.program_id(0), pick_ref[windows], quarter)
    mine = jnp.where(tile < tiles_human, 0, 1)
    acc_ref[...] = refs[windows + 1][...].astype(jnp.float32) if has_more else jnp.zeros_like(acc_ref)
    for window in range(windows):

        @pl.when(pick_ref[window] == mine)
        def _():
            acc_ref[...] += mxu(grads[window][...], rows[window], NN)

    out_ref[...] = acc_ref[...].astype(jnp.bfloat16)


def head_grads(pick, grads, rows, tiles_human, tiles, more=None):
    windows, bins, share = rows.shape
    last = grads[0].shape[0] // TILE - 1

    def tile_of(window):
        def index(t, p):
            tile = head_tile(t, p[windows], tiles // 2)
            kept = jnp.where(p[window] == 0, jnp.minimum(tile, tiles_human - 1), 0)
            kept = jnp.where(p[window] == 1, jnp.maximum(tile, tiles_human), kept)
            return (jnp.minimum(kept, last), 0)

        return index

    extra = [] if more is None else [more]
    return pl.pallas_call(
        lambda *refs: head_grads_kernel(
            windows, tiles_human, tiles // 2, more is not None, *refs
        ),
        grid_spec=pltpu.PrefetchScalarGridSpec(
            num_scalar_prefetch=1,
            grid=(tiles,),
            in_specs=[pl.BlockSpec((TILE, bins), tile_of(w)) for w in range(windows)]
            + [pl.BlockSpec((windows, bins, share), lambda t, p: (0, 0, 0))]
            + [pl.BlockSpec((TILE, share), lambda t, p: (t, 0))] * len(extra),
            out_specs=pl.BlockSpec((TILE, share), lambda t, p: (t, 0)),
            scratch_shapes=[pltpu.VMEM((TILE, share), jnp.float32)],
        ),
        out_shape=jax.ShapeDtypeStruct((tiles * TILE, share), jnp.bfloat16),
        compiler_params=pltpu.CompilerParams(vmem_limit_bytes=40 << 20),
        cost_estimate=pl.CostEstimate(
            flops=2 * windows * bins * share * tiles * TILE,
            bytes_accessed=4 * tiles * TILE * share,
            transcendentals=0,
        ),
        name="head_grads",
    )(pick, *grads, rows, *extra)


def half_product_kernel(windows, turned, has_more, pick_ref, *refs):
    lefts, rights, out_ref = refs[:windows], refs[windows : 2 * windows], refs[-1]
    total = None
    for left, right in zip(lefts, rights):
        if turned:
            term = mxu(right[...], left[...], NN)
        else:
            term = mxu(left[...], right[...], TN)
        total = term if total is None else total + term
    if turned:
        total = total.T
    if has_more:
        total = total + refs[2 * windows][...].astype(jnp.float32)
    out_ref[...] = total.astype(jnp.bfloat16)


def half_product(half, lefts, rights, slabs, turned, more=None):
    windows = len(lefts)
    rows, width = lefts[0].shape
    slab = width // slabs
    cols = rights[0].shape[0 if turned else 1]
    step = cols
    while step > 768 and step % 256 == 0:
        step //= 2
    left_spec = pl.BlockSpec((rows, slab), lambda u, j, p: (0, 2 * u + p[0]))
    if turned:
        right_spec = pl.BlockSpec((step, rows), lambda u, j, p: (j, 0))
    else:
        right_spec = pl.BlockSpec((rows, step), lambda u, j, p: (0, j))
    out_spec = pl.BlockSpec((slab, step), lambda u, j, p: (u, j))
    extra = [] if more is None else [more]
    return pl.pallas_call(
        lambda *refs: half_product_kernel(windows, turned, more is not None, *refs),
        grid_spec=pltpu.PrefetchScalarGridSpec(
            num_scalar_prefetch=1,
            grid=(slabs // 2, cols // step),
            in_specs=[left_spec] * windows + [right_spec] * windows + [out_spec] * len(extra),
            out_specs=out_spec,
        ),
        out_shape=jax.ShapeDtypeStruct((width // 2, cols), jnp.bfloat16),
        compiler_params=pltpu.CompilerParams(vmem_limit_bytes=48 << 20),
        cost_estimate=pl.CostEstimate(
            flops=windows * rows * width * cols,
            bytes_accessed=windows * rows * (width + 2 * cols),
            transcendentals=0,
        ),
        name="half_product",
    )(half, *lefts, *rights, *extra)


def norm_stats(values):
    mean = jnp.mean(values, axis=-1, keepdims=True)
    centred = values - mean
    inverse = lax.rsqrt(jnp.mean(centred * centred, axis=-1, keepdims=True) + norm_eps)
    return mean, inverse


def norm_backward(grad_output, scaled, inverse, norm_gain):
    grad_scaled = grad_output * norm_gain
    mean_grad = jnp.mean(grad_scaled, axis=-1, keepdims=True)
    mean_proj = jnp.mean(grad_scaled * scaled, axis=-1, keepdims=True)
    grad_input = inverse * (grad_scaled - mean_grad - scaled * mean_proj)
    return (grad_input, jnp.sum(grad_output * scaled, axis=0), jnp.sum(grad_output, axis=0))


def sum_over_model(partial, done, after_line):
    low = done(partial.astype(jnp.bfloat16))
    if lax.axis_size("mp") == 2:
        other = lax.ppermute(low, "mp", [(0, 1), (1, 0)])
        return lambda: low.astype(jnp.float32) + after_line(other).astype(jnp.float32)
    total = lax.psum(low, "mp")
    return lambda: after_line(total).astype(jnp.float32)


def in_model_order(own, dim, after_line):
    if lax.axis_size("mp") == 2:
        first = lax.axis_index("mp") == 0
        other = lax.ppermute(own, "mp", [(0, 1), (1, 0)])

        def ordered():
            got = after_line(other)
            return jnp.concatenate(
                [jnp.where(first, own, got), jnp.where(first, got, own)], axis=dim
            )

        return ordered
    full = lax.all_gather(own, "mp", axis=dim, tiled=True)
    return lambda: after_line(full)


class OtherRows:
    def __init__(self, own, tile, after_line, done):
        self.after_line, self.done = after_line, done
        count = lax.axis_size("dp")
        size = -(-own.shape[0] // tile) * tile // count
        part = None
        for place in range(count - 1, -1, -1):
            piece = own[place * size : (place + 1) * size]
            piece = jnp.pad(piece, [(0, size - piece.shape[0]), (0, 0)])
            here = lax.axis_index("dp") == place
            part = piece if part is None else jnp.where(here, piece, part)
        self.mine = lax.ppermute(done(part), "mp", [(0, 1), (1, 0)])

    def share(self):
        self.full = lax.all_gather(
            self.done(self.after_line(self.mine)), "dp", axis=0, tiled=True
        )

    def finish(self):
        return self.after_line(self.full)


def swap_pairs(axis, step):
    return [(i, i ^ step) for i in range(lax.axis_size(axis))]


class SmallSums:
    def __init__(self, parts, axes, after_line, done):
        self.parts, self.after_line, self.done = parts, after_line, done
        padded = [jnp.pad(x.reshape(-1), (0, -x.size % 128)) for x in parts]
        self.total = jnp.concatenate(padded).reshape(-1, 128)
        self.moves = [
            (axis, 1 << bit)
            for axis in axes
            for bit in range(lax.axis_size(axis).bit_length() - 1)
        ]
        self.got = None
        self.step()

    def step(self):
        if self.got is not None:
            self.total, self.got = self.total + self.after_line(self.got), None
        if self.moves:
            axis, step = self.moves.pop(0)
            self.total = self.done(self.total)
            self.got = lax.ppermute(self.total, axis, swap_pairs(axis, step))

    def finish(self):
        while self.got is not None:
            self.step()
        results, start, total = [], 0, self.total.reshape(-1)
        for x in self.parts:
            results.append(total[start : start + x.size].reshape(x.shape))
            start += -(-x.size // 128) * 128
        return results


class SeqSum:
    def __init__(self, parts, done):
        self.got = lax.all_to_all(done(parts), "seq", split_axis=0, concat_axis=0, tiled=True)

    def arrive(self, after_line):
        self.got = after_line(self.got)

    def finish(self, after_line, done):
        return done(jnp.sum(after_line(self.got).astype(jnp.float32), axis=0))


class ScatterProduct:
    def __init__(self, lefts, rights, after_line, done, turned=False):
        self.after_line, self.done, self.turned = after_line, done, turned
        self.lefts, self.rights = lefts, rights
        lefts = [after_line(lefts[0])] + lefts[1:]
        self.got = lax.ppermute(done(self.half(1, lefts)), "dp", swap_pairs("dp", 1))

    def half(self, other, lefts, more=None):
        pick = jnp.reshape((lax.axis_index("dp") + other) % 2, (1,)).astype(jnp.int32)
        return half_product(pick, lefts, self.rights, lax.axis_size("dp"), self.turned, more)

    def keep(self):
        self.kept = self.done(self.half(0, self.lefts, self.after_line(self.got)))
        return self


class ScatterRest:
    def __init__(self, kept, after_line, done):
        self.after_line, self.done = after_line, done
        size = kept.shape[0] // 2
        upper = lax.axis_index("dp") // 2 == 1
        low, high = kept[:size], kept[size:]
        self.mine = jnp.where(upper, high, low)
        self.got = lax.ppermute(done(jnp.where(upper, low, high)), "dp", swap_pairs("dp", 2))

    def along_seq(self):
        got = self.after_line(self.got).astype(jnp.float32)
        total = (self.mine.astype(jnp.float32) + got).astype(jnp.bfloat16)
        parts = total.reshape(lax.axis_size("seq"), -1, total.shape[1])
        self.sum = SeqSum(parts, self.done)

    def arrive(self):
        self.sum.arrive(self.after_line)

    def finish(self):
        return self.sum.finish(self.after_line, self.done)


def on_device(
    trunk_in,
    norm1_gain,
    norm1_bias,
    w_query,
    w_key,
    w_value,
    w_rel,
    content_bias,
    pos_bias,
    w_out,
    b_out,
    norm2_gain,
    norm2_bias,
    w_in,
    b_in,
    w_hid,
    b_hid,
    head_human,
    bias_human,
    head_mouse,
    bias_mouse,
    species,
    targets_human,
    targets_mouse,
):
    windows, bins, width = trunk_in.shape
    heads = content_bias.shape[0]
    dp_size, seq_size, mp_size = (lax.axis_size(axis) for axis in ("dp", "seq", "mp"))
    seq_index, mp_index = lax.axis_index("seq"), lax.axis_index("mp")
    place = lax.axis_index("dp") * seq_size + seq_index
    places = dp_size * seq_size
    all_bins = bins * seq_size
    query_start = seq_index * bins
    key_scale = KD ** (-0.5)
    loss_scale = 1.0 / math.sqrt(windows * dp_size * CROP)
    crop_start = (all_bins - CROP) // 2
    bf16 = jnp.bfloat16
    me = jnp.reshape(seq_index, (1,)).astype(jnp.int32)

    groups = [[w] for w in range(windows)] if heads % seq_size == 0 else [list(range(windows))]
    group_size = len(groups[0])
    pairs = heads * group_size
    pairs_here = -(-pairs // seq_size)
    block = query_block(all_bins)
    pair_heads = [
        jnp.minimum((seq_index * pairs_here + j) // group_size, heads - 1)
        for j in range(pairs_here)
    ]

    tokens = [jnp.zeros((8, 128), jnp.float32)]

    def after_line(array):
        array, token = lax.optimization_barrier((array, tokens[-1]))
        tokens.append(token)
        return array

    done = after_line

    def exchange(array):
        return lax.all_to_all(array, "seq", split_axis=0, concat_axis=0, tiled=True)

    def spread(array):
        short = seq_size * pairs_here - pairs
        if short:
            array = jnp.pad(array, [(0, short)] + [(0, 0)] * (array.ndim - 1))
        return exchange(array.reshape((seq_size, pairs_here) + array.shape[1:]))

    def regroup(array, size):
        if array.shape[2] == size:
            return array
        depth = array.shape[1]
        array = array.transpose(1, 0, 2).reshape(depth, all_bins // size, size)
        return array.transpose(1, 0, 2)

    def to_owners(arrays):
        return exchange(jnp.stack([regroup(a, bins) for a in arrays], axis=1))

    def by_head(array):
        depth = array.shape[2]
        array = array.reshape(seq_size * pairs_here, depth, bins)[:pairs]
        array = array.reshape(heads, group_size, depth, bins).transpose(0, 2, 1, 3)
        return array.reshape(heads * depth, group_size * bins)

    track_human, track_mouse = head_human.shape[1], head_mouse.shape[1]
    own_heads = (head_human.T, head_mouse.T)
    parts = {}

    def fetch_out(_):
        if mp_size == 2:
            parts["out"] = OtherRows(w_out, w_out.shape[0], after_line, done)

    def fetch_out_share(_):
        if mp_size == 2:
            parts["out"].share()

    def fetch_out_end(_):
        if mp_size != 2:
            parts["w_out"] = lax.all_gather(w_out, "mp", axis=0, tiled=True)
            return
        other, first = parts["out"].finish(), mp_index == 0
        parts["w_out"] = done(
            jnp.concatenate(
                [jnp.where(first, w_out, other), jnp.where(first, other, w_out)], axis=0
            )
        )

    def fetch_heads(_):
        if mp_size == 2:
            parts["heads"] = [OtherRows(own, TILE, after_line, done) for own in own_heads]

    def fetch_heads_share(_):
        if mp_size == 2:
            for part in parts["heads"]:
                part.share()

    def fetch_heads_end(_):
        if mp_size == 2:
            parts["others"] = [part.finish() for part in parts["heads"]]
            parts["own"] = own_heads
            return
        full = [lax.all_gather(own, "mp", axis=1, tiled=True) for own in own_heads]
        parts["own"] = [x[:, : width // 2] for x in full]
        parts["others"] = [x[:, width // 2 :] for x in full]

    def of_head(weight, size, h):
        return weight[:, h * size : (h + 1) * size]

    w_packs = [
        jnp.concatenate(
            [of_head(w_value, VD, h), of_head(w_key, KD, h)] + [of_head(w_query, KD, h)] * 2, axis=1
        )
        for h in range(heads)
    ]
    w_grad = jnp.concatenate([w[:, :GRAD_PACK] for w in w_packs], axis=1)
    pack_scale = jnp.concatenate(
        [jnp.ones((VD + KD,), jnp.float32), jnp.full((2 * KD,), key_scale, jnp.float32)]
    )
    pack_biases = [
        jnp.concatenate([jnp.zeros((VD + KD,), jnp.float32), content_bias[h], pos_bias[h]])
        for h in range(heads)
    ]

    basis = jnp.pad(rel_basis(), [(0, 1), (0, 0)])
    w_rel_heads = w_rel.reshape(FEAT, heads, KD)
    rels = [
        mxu(
            basis,
            lax.dynamic_index_in_dim(w_rel_heads, head, 1, keepdims=False).astype(jnp.float32),
            NN,
            exact_mode,
        ).astype(bf16)
        for head in pair_heads
    ]

    count = len(groups)
    many = lambda: [None] * count
    trunk, stats1, normed1, packs, probs, attended = many(), many(), many(), many(), many(), many()
    mids, stats2, normed2, preacts, actives = many(), many(), many(), many(), many()
    trunk_out, grad_trunks, grad_outs, grad_pres = many(), many(), many(), many()
    grad_mids, grad_mid_lows, packed_grads, grad_inputs = many(), many(), many(), many()
    moving, grad_att, own_rows = many(), many(), [None] * windows
    logit_grads, track_sums, losses = [None] * windows, [], []
    sums = [0.0] * 5
    sums1 = [0.0, 0.0]
    drels = [0.0] * pairs_here
    dstats = [0.0] * pairs_here

    def project(g):
        rows = group_size * bins
        values = trunk_in[groups[g][0] : groups[g][-1] + 1].reshape(rows, width).astype(jnp.float32)
        mean, inverse = norm_stats(values)
        normed = ((values - mean) * inverse * norm1_gain + norm1_bias).astype(bf16)
        normed = after_line(normed)
        trunk[g], stats1[g], normed1[g] = values, (mean, inverse), normed
        parts = []
        for h in range(heads):
            pack = (mxu(normed, w_packs[h], NN) * pack_scale + pack_biases[h]).astype(bf16)
            parts.append(pack.reshape(group_size, bins, PACK))
        pack = spread(done(jnp.concatenate(parts, axis=0)))
        packs[g] = pack

    def arrive(g):
        packs[g] = after_line(packs[g])

    def arrive_out(g):
        moving[g] = after_line(moving[g])

    def arrive_grad(g):
        grad_att[g] = after_line(grad_att[g])

    def arrive_packed(g):
        packed_grads[g] = by_head(after_line(packed_grads[g]))

    def attend(g):
        outs, kept = [], []
        pack = after_line(packs[g])
        packs[g] = [pack[:, j].reshape(all_bins, PACK) for j in range(pairs_here)]
        for j in range(pairs_here):
            out, prob = attend_forward(packs[g][j], rels[j])
            outs.append(done(out))
            kept.append(prob)
        probs[g] = kept
        moving[g] = to_owners(outs)

    def attend_swap(g):
        attended[g] = done(by_head(after_line(moving[g])))
        moving[g] = in_model_order(attended[g], 0, after_line)

    def feed_forward(g):
        mid = trunk[g] + mxu(moving[g](), parts["w_out"], TN) + b_out
        mean, inverse = norm_stats(mid)
        normed = ((mid - mean) * inverse * norm2_gain + norm2_bias).astype(bf16)
        preact = mxu(normed, w_in, NN) + b_in
        active = jnp.maximum(preact, 0.0).astype(bf16)
        mids[g], stats2[g], normed2[g], actives[g] = mid, (mean, inverse), normed, active
        moving[g] = sum_over_model(mxu(active, w_hid, NN), done, after_line)

    def score(g):
        out = mids[g] + (moving[g]() + b_hid)
        trunk_out[g] = out
        low = out.astype(bf16)
        grads = []
        for i, window in enumerate(groups[g]):
            rows = low[i * bins : (i + 1) * bins]
            own_rows[window] = lax.dynamic_slice_in_dim(rows, mp_index * share, share, 1)
            pick = jnp.stack([picks[window], jnp.int32(0) + order])
            logit_grads[window], grad_out, track_sum, loss = score_heads(
                window, pick, rows, weight, parts["own"], parts["others"], bias_rows[0], count_human, count_mouse
            )
            track = jnp.sum(track_sum, axis=0)
            scored = jnp.arange(track.size) < tiles_human * TILE
            scored = scored == (picks[window] == 0)
            track_sums.append(jnp.where(scored & (picks[window] < 2), track, 0.0))
            losses.append(jnp.sum(loss))
            grads.append(grad_out)
        grad_trunks[g] = done(jnp.concatenate(grads, axis=0))

    def back_hidden(g):
        grad_out = after_line(grad_trunks[g].astype(bf16))
        grad_preact = jnp.where(actives[g] > 0, mxu(grad_out, w_hid, NT), 0.0)
        grad_pre = grad_preact.astype(bf16)
        grad_outs[g], grad_pres[g] = grad_out, grad_pre
        sums[3] = sums[3] + jnp.sum(grad_trunks[g], axis=0)
        sums[4] = sums[4] + jnp.sum(grad_preact, axis=0)
        moving[g] = sum_over_model(mxu(grad_pre, w_in, NT), done, after_line)

    def back_mid(g):
        mean, inverse = stats2[g]
        grad_normed = moving[g]()
        grad_norm, dgain, dbias = norm_backward(
            grad_normed, (mids[g] - mean) * inverse, inverse, norm2_gain
        )
        grad_mids[g] = grad_trunks[g] + grad_norm
        grad_mid_lows[g] = grad_mids[g].astype(bf16)
        sums[0] = sums[0] + dgain
        sums[1] = sums[1] + dbias
        sums[2] = sums[2] + jnp.sum(grad_mids[g], axis=0)
        grad = done(mxu(w_out, grad_mid_lows[g], NT).astype(bf16))
        grad = grad.reshape(heads, VD, group_size, bins).transpose(0, 2, 1, 3)
        grad_att[g] = spread(grad.reshape(pairs, VD, bins))

    def back_attend(g):
        outs = []
        grad = after_line(grad_att[g])
        for j in range(pairs_here):
            out, drel, stat = attend_backward(
                packs[g][j], rels[j], probs[g][j], regroup(grad[:, j], block)
            )
            outs.append(done(out))
            drels[j] = drels[j] + drel
            dstats[j] = dstats[j] + stat
        packed_grads[g] = to_owners(outs)

    def back_project(g):
        packed_grads[g] = after_line(packed_grads[g])
        product = lax.dot_general(
            packed_grads[g],
            w_grad,
            (((0,), (1,)), ((), ())),
            preferred_element_type=jnp.float32,
        )
        moving[g] = sum_over_model(product, done, after_line)

    def back_input(g):
        mean, inverse = stats1[g]
        grad_norm, dgain, dbias = norm_backward(
            moving[g](), (trunk[g] - mean) * inverse, inverse, norm1_gain
        )
        sums1[0] = sums1[0] + dgain
        sums1[1] = sums1[1] + dbias
        grad_inputs[g] = (grad_mids[g] + grad_norm).reshape(group_size, bins, width)

    bin_place = query_start + jnp.arange(bins)
    in_crop = ((bin_place >= crop_start) & (bin_place < crop_start + CROP)).astype(jnp.float32)
    weight = jnp.broadcast_to((in_crop * loss_scale)[None, :], (8, bins))
    has_crop = (query_start + bins > crop_start) & (query_start < crop_start + CROP)
    picks = jnp.where(has_crop, species, 2)
    count_human = targets_human.transpose(0, 2, 1)
    count_mouse = targets_mouse.transpose(0, 2, 1)
    tiles_human, tiles_mouse = pl.cdiv(track_human, TILE), pl.cdiv(track_mouse, TILE)
    half_tiles = (tiles_human + tiles_mouse) // 2
    bias_all = jnp.concatenate(
        [
            jnp.pad(bias_human, (0, tiles_human * TILE - track_human)),
            jnp.pad(bias_mouse, (0, tiles_mouse * TILE - track_mouse)),
        ]
    )
    bias_rows = []

    def spread_bias(_):
        wide = jnp.broadcast_to(after_line(bias_all)[:, None], (bias_all.size, 128))
        bias_rows.append(done(wide))

    order = mp_index if mp_size == 2 else 0
    share = head_human.shape[0]
    join = lambda arrays: jnp.concatenate(arrays, axis=0)
    results = {}
    width_out = heads * VD

    def pick_half(half):
        return jnp.concatenate([picks, jnp.reshape(half, (1,)).astype(jnp.int32)])

    def grads_heads(_):
        parity = lax.axis_index("dp") % 2
        rows = jnp.stack(own_rows)
        grads = [after_line(logit_grads[0])] + logit_grads[1:]
        sent = head_grads(pick_half(1 - parity), grads, rows, tiles_human, half_tiles)
        got = lax.ppermute(done(sent), "dp", swap_pairs("dp", 1))
        results["heads"] = (grads, rows, got, parity)

    def grads_heads_keep(_):
        grads, rows, got, parity = results["heads"]
        kept = done(
            head_grads(pick_half(parity), grads, rows, tiles_human, half_tiles, after_line(got))
        )
        results["heads"] = ScatterRest(kept, after_line, done)

    def grads_heads_seq(_):
        results["heads"].along_seq()

    def heads_arrive(_):
        results["heads"].arrive()

    def wide_arrive(_):
        results["wide"].arrive()

    def grads_heads_end(_):
        total = results["heads"].finish().astype(bf16)
        results["heads"] = lax.all_gather(total, ("dp", "seq"), axis=0, tiled=True)

    def grads_in(_):
        results["in"] = ScatterProduct(normed2, grad_pres, after_line, done)

    def grads_hid(_):
        results["hid"] = ScatterProduct(grad_outs, actives, after_line, done)

    def grads_in_keep(_):
        results["in"].keep()

    def grads_hid_keep(_):
        results["hid"].keep()
        kept = jnp.concatenate([results["in"].kept, results["hid"].kept], axis=1)
        results["wide"] = ScatterRest(kept, after_line, done)

    def grads_wide_seq(_):
        results["wide"].along_seq()

    def grads_wide_end(_):
        results["wide"] = results["wide"].finish()

    def grads_out(_):
        results["out"] = ScatterProduct(grad_mid_lows, attended, after_line, done, True)

    def grads_out_keep(_):
        results["out"].keep()

    def grads_pack(_):
        results["pack"] = ScatterProduct(normed1, packed_grads, after_line, done, True)

    def grads_pack_keep(_):
        kept = jnp.concatenate([results["out"].kept, results["pack"].keep().kept], axis=1)
        results["late_rows"] = ScatterRest(kept, after_line, done)

    def grads_pack_seq(_):
        results["late_rows"].along_seq()

    def grads_pack_end(_):
        late = results["late_rows"].finish()
        results["out"], results["pack"] = late[:, :width_out], late[:, width_out:]

    def sums_early(_):
        values = list(sums) + [sum(track_sums), sum(losses)[None]]
        results["early"] = SmallSums(values, ("seq", "dp"), after_line, done)

    def sums_heads(_):
        dw_rel = jnp.zeros((heads, FEAT, KD), jnp.float32)
        dstat = jnp.zeros((heads, 2, KD), jnp.float32)
        for j, head in enumerate(pair_heads):
            part = lax.dot_general(
                basis,
                drels[j],
                (((0,), (1,)), ((), ())),
                precision=exact_mode,
                preferred_element_type=jnp.float32,
            )
            mine = (jnp.arange(heads) == head).astype(jnp.float32)[:, None, None]
            dw_rel = dw_rel + mine * part
            dstat = dstat + mine * dstats[j][None, :2, :KD]
        values = [part, dstats[0]] if heads == seq_size else [dstat, dw_rel]
        axes = ("dp",) if heads == seq_size else ("dp", "seq")
        results["own_head"] = SmallSums(values, axes, after_line, done)

    def sums_late(_):
        results["late"] = SmallSums(list(sums1), ("dp", "seq"), after_line, done)

    def step_early(_):
        results["early"].step()

    def step_heads(_):
        results["own_head"].step()

    def step_late(_):
        results["late"].step()

    def heads_out(_):
        full = after_line(results["heads"])
        first = tiles_human * TILE
        results["human"] = done(full[:track_human].astype(jnp.float32))
        results["mouse"] = done(full[first : first + track_mouse].astype(jnp.float32))

    def each(stage):
        return [(stage, g) for g in range(count)]

    def one(*stages):
        return [(stage, -1) for stage in stages]

    if count == 3:
        plan = one(fetch_out) + [(project, 0)] + one(fetch_out_share, fetch_heads)
        plan += [(project, 1), (project, 2)] + one(spread_bias) + [(attend, 0), (attend, 1)]
        plan += one(fetch_heads_share) + [(attend_swap, 0)] + one(fetch_out_end)
        plan += [(feed_forward, 0), (attend, 2), (attend_swap, 1), (feed_forward, 1)]
        plan += [(attend_swap, 2)] + one(fetch_heads_end)
        plan += [(score, 0), (feed_forward, 2), (back_hidden, 0)]
        plan += [(score, 1), (back_hidden, 1), (back_mid, 0), (score, 2)]
        plan += one(grads_heads) + [(arrive_grad, 0), (back_attend, 0), (back_hidden, 2)]
        plan += one(grads_heads_keep) + [(back_mid, 1), (arrive_packed, 0)] + one(grads_in)
        plan += [(arrive_grad, 1), (back_attend, 1)] + one(grads_in_keep) + [(back_mid, 2)]
        plan += one(sums_early) + [(back_project, 0), (arrive_packed, 1)] + one(step_early, grads_hid)
        plan += [(arrive_grad, 2)] + one(step_early, grads_heads_seq) + [(back_attend, 2)]
        plan += one(grads_hid_keep, step_early) + [(back_project, 1), (back_input, 0)]
        plan += one(grads_out, step_early, sums_heads, grads_out_keep, step_heads)
        plan += one(heads_arrive, grads_heads_end) + [(back_input, 1), (arrive_packed, 2)]
        plan += one(grads_pack) + [(back_project, 2)]
        plan += one(grads_wide_seq, step_heads, grads_pack_keep) + [(back_input, 2)]
        plan += one(sums_late, wide_arrive, step_late, grads_pack_seq, step_late, heads_out)
        plan += one(grads_wide_end, step_late, grads_pack_end, step_late)
    else:
        plan = one(fetch_out, fetch_out_share, fetch_out_end, spread_bias)
        plan += one(fetch_heads, fetch_heads_share, fetch_heads_end)
        plan += each(project) + each(attend) + each(attend_swap) + each(feed_forward) + each(score)
        plan += each(back_hidden) + each(back_mid)
        plan += one(grads_heads, grads_heads_keep, grads_heads_seq, grads_heads_end)
        plan += each(back_attend) + one(grads_in, grads_in_keep, grads_hid, grads_hid_keep)
        plan += one(grads_wide_seq, grads_wide_end, grads_out, grads_out_keep)
        plan += each(arrive_packed) + each(back_project) + one(grads_pack, grads_pack_keep)
        plan += one(grads_pack_seq, grads_pack_end) + each(back_input)
        plan += one(sums_early, sums_heads, sums_late, heads_out)
    for stage, g in plan:
        stage(g)
    dgain2, dbias2, db_out, db_hid, db_in, dtracks, loss = results["early"].finish()
    dgain1, dbias1 = results["late"].finish()
    mids_sum = results["own_head"].finish()
    if heads == seq_size:
        share_rel, share_stat = FEAT // places, KD // places
        own_rel = mids_sum[0].reshape(dp_size, seq_size, share_rel * KD)
        own_stat = mids_sum[1][:2, :KD].reshape(2, dp_size, seq_size, share_stat)
        dp_here = lax.axis_index("dp")
        own_rel = lax.dynamic_index_in_dim(own_rel, dp_here, 0, keepdims=False)
        own_stat = lax.dynamic_index_in_dim(own_stat, dp_here, 1, keepdims=False)
        own_stat = own_stat.transpose(1, 0, 2).reshape(seq_size, 2 * share_stat)
        small = jnp.concatenate([own_rel, own_stat], axis=1)
        small = jnp.pad(small, [(0, 0), (0, -small.shape[1] % 128)])
        small = lax.all_to_all(small[:, None], "seq", split_axis=0, concat_axis=0, tiled=True)[:, 0]
        rel_rows = small[:, : share_rel * KD].reshape(heads, share_rel, KD)
        rel_rows = rel_rows.transpose(1, 0, 2).reshape(share_rel, heads * KD)
        stats = small[:, share_rel * KD : share_rel * KD + 2 * share_stat]
        dstat = stats.reshape(heads, 2, share_stat)
        dcontent, dposition = dstat[:, 0], dstat[:, 1]
    else:
        dstat, dw_rel = mids_sum
    dw_out = results["out"]
    dw_in, dw_hid = jnp.split(results["wide"], 2, axis=1)
    pack_summed = results["pack"].reshape(-1, heads, GRAD_PACK)
    def own(array, dim=0):
        size = array.shape[dim] // places
        return lax.dynamic_slice_in_dim(array, place * size, size, dim)

    if heads != seq_size:
        rel_rows = own(dw_rel, 1).transpose(1, 0, 2).reshape(-1, heads * KD)
        dcontent, dposition = own(dstat[:, 0], 1), own(dstat[:, 1], 1)
    pack_rows = pack_summed.shape[0]
    mouse_start = tiles_human * TILE
    shape3 = (windows, bins, width)
    return (
        join(trunk_out).reshape(shape3),
        loss[0] + tokens[-1][0, 0],
        join(grad_inputs).reshape(shape3),
        own(dgain1),
        own(dbias1),
        pack_summed[:, :, VD + KD :].reshape(pack_rows, heads * KD),
        pack_summed[:, :, VD : VD + KD].reshape(pack_rows, heads * KD),
        pack_summed[:, :, :VD].reshape(pack_rows, heads * VD),
        rel_rows,
        dcontent,
        dposition,
        dw_out.T,
        own(db_out),
        own(dgain2),
        own(dbias2),
        dw_in,
        db_in,
        dw_hid.T,
        own(db_hid),
        results["human"].T,
        dtracks[:track_human],
        results["mouse"].T,
        dtracks[mouse_start : mouse_start + track_mouse],
    )


def solution(mesh):
    in_specs = (
        P("dp", "seq", None),
        P(),
        P(),
        P(None, "mp"),
        P(None, "mp"),
        P(None, "mp"),
        P(None, "mp"),
        P("mp", None),
        P("mp", None),
        P("mp", None),
        P(),
        P(),
        P(),
        P(None, "mp"),
        P("mp"),
        P("mp", None),
        P(),
        P("mp", None),
        P(),
        P("mp", None),
        P(),
        P("dp"),
        P("dp", "seq", None),
        P("dp", "seq", None),
    )
    out_specs = (
        P("dp", "seq", None),
        P(),
        P("dp", "seq", None),
        P(("dp", "seq")),
        P(("dp", "seq")),
        P(("dp", "seq"), "mp"),
        P(("dp", "seq"), "mp"),
        P(("dp", "seq"), "mp"),
        P(("dp", "seq"), "mp"),
        P("mp", ("dp", "seq")),
        P("mp", ("dp", "seq")),
        P("mp", ("dp", "seq")),
        P(("dp", "seq")),
        P(("dp", "seq")),
        P(("dp", "seq")),
        P(("dp", "seq"), "mp"),
        P("mp"),
        P("mp", ("dp", "seq")),
        P(("dp", "seq")),
        P("mp", None),
        P(),
        P("mp", None),
        P(),
    )
    return jax.shard_map(
        on_device, mesh=mesh, in_specs=in_specs, out_specs=out_specs, check_vma=False
    )
```

```python
import math

import jax
import jax.numpy as jnp
from jax import lax
from jax.experimental import pallas as pl
from jax.experimental.pallas import tpu as pltpu
from jax.sharding import PartitionSpec as P

KD = 64
VD = 192
FEAT = 192
BINS = 1536
CROP = 896


norm_eps = 1e-05
log_eps = 1e-07
exact_mode = lax.Precision.HIGHEST


def rel_basis():
    per_class = FEAT // 6
    distance = jnp.arange(-(BINS - 1), BINS).astype(jnp.float32)
    magnitude = jnp.abs(distance)[:, None]
    half_life = (2.0 ** jnp.linspace(3.0, math.log2(BINS), per_class)).astype(jnp.float32)
    decays = jnp.exp(-math.log(2.0) / half_life[None, :] * magnitude)
    widths = (2.0 ** jnp.arange(1, per_class + 1)).astype(jnp.float32) - 1.0
    central = (widths[None, :] > magnitude).astype(jnp.float32)
    spread = BINS / (2.0 * per_class)
    centre = jnp.linspace(BINS / per_class, BINS, per_class).astype(jnp.float32)
    concentration = (centre / spread) ** 2
    rate_param = centre / spread**2
    peak_at = (concentration - 1.0) / rate_param
    log_ratio = (concentration - 1.0) * (
        jnp.log(jnp.maximum(magnitude, 1e-20)) - jnp.log(peak_at)
    ) - rate_param * (magnitude - peak_at)
    density = jnp.exp(log_ratio)
    gammas = density / jnp.max(density, axis=0, keepdims=True)
    symmetric = jnp.concatenate([decays, central, gammas], axis=1)
    return jnp.concatenate([symmetric, jnp.sign(distance)[:, None] * symmetric], axis=1)


PACK = VD + 3 * KD
GRAD_PACK = VD + 2 * KD
TILE = 896
NN = (((1,), (0,)), ((), ()))
NT = (((1,), (1,)), ((), ()))
TN = (((0,), (0,)), ((), ()))


def mxu(left_arr, right_arr, dims, precision=None):
    return lax.dot_general(
        left_arr, right_arr, dims, precision=precision, preferred_element_type=jnp.float32
    )


def query_block(bins):
    for block in (384, 256, 128):
        if bins % block == 0:
            return block
    return bins


def attend_forward_kernel(block, bins, pack_ref, rel_ref, out_ref, probs_ref):
    step = pl.program_id(0)
    span = bins + block
    query = pack_ref[pl.ds(pl.multiple_of(step * block, block), block), VD + KD :]
    base = pl.multiple_of(bins - block - step * block, block)
    content = mxu(query[:, :KD], pack_ref[:, VD : VD + KD], NT)
    position = mxu(query[:, KD:], rel_ref[pl.ds(base, span), :], NT)
    position = pltpu.roll(position, span - (block - 1), 1, stride=1, stride_axis=0)
    scores = content + position[:, :bins]
    exps = jnp.exp(scores - jnp.max(scores, axis=1, keepdims=True))
    probs = (exps * (1.0 / jnp.sum(exps, axis=1, keepdims=True))).astype(jnp.bfloat16)
    probs_ref[...] = probs
    out_ref[0] = mxu(probs, pack_ref[:, :VD], NN).T.astype(jnp.bfloat16)


def attend_forward(pack, rel):
    bins = pack.shape[0]
    block = query_block(bins)
    steps = bins // block
    return pl.pallas_call(
        lambda *refs: attend_forward_kernel(block, bins, *refs),
        grid=(steps,),
        in_specs=[
            pl.BlockSpec((bins, PACK), lambda i: (0, 0)),
            pl.BlockSpec((2 * bins, KD), lambda i: (0, 0)),
        ],
        out_specs=[
            pl.BlockSpec((1, VD, block), lambda i: (i, 0, 0)),
            pl.BlockSpec((block, bins), lambda i: (i, 0)),
        ],
        out_shape=[
            jax.ShapeDtypeStruct((steps, VD, block), jnp.bfloat16),
            jax.ShapeDtypeStruct((bins, bins), jnp.bfloat16),
        ],
        compiler_params=pltpu.CompilerParams(vmem_limit_bytes=48 << 20),
        cost_estimate=pl.CostEstimate(flops=1, bytes_accessed=1, transcendentals=0),
        name="attend_forward",
    )(pack, rel)


def attend_backward_kernel(
    block, bins, pack_ref, rel_ref, probs_ref, grad_ref, out_ref, drel_ref, stat_ref, acc_ref
):
    step = pl.program_id(0)
    steps = bins // block
    span = bins + block

    @pl.when(step == 0)
    def _():
        acc_ref[...] = jnp.zeros_like(acc_ref)
        drel_ref[...] = jnp.zeros_like(drel_ref)
        stat_ref[...] = jnp.zeros_like(stat_ref)

    query = pack_ref[pl.ds(pl.multiple_of(step * block, block), block), VD + KD :]
    base = pl.multiple_of(bins - block - step * block, block)
    grad_t = grad_ref[0]
    probs = probs_ref[...]
    acc_ref[:VD, :] += mxu(grad_t, probs, NN)
    grad_probs = mxu(grad_t.T, pack_ref[:, :VD], NT)
    wide = probs.astype(jnp.float32)
    scaled = wide * grad_probs
    delta = jnp.sum(scaled, axis=1, keepdims=True)
    grad_scores = (scaled - wide * delta).astype(jnp.bfloat16)
    grad_qc = mxu(grad_scores, pack_ref[:, VD : VD + KD], NN)
    query_t = query.T
    acc_ref[VD:, :] += mxu(query_t[:KD], grad_scores, NN)
    row = lax.broadcasted_iota(jnp.int32, (block, block), 0)
    col = lax.broadcasted_iota(jnp.int32, (block, block), 1)
    flip = (row + col == block - 1).astype(jnp.bfloat16)
    turned = mxu(flip, grad_scores, NN)
    turned = jnp.concatenate([turned, jnp.zeros((block, block), jnp.float32)], axis=1)
    turned = pltpu.roll(turned, 0, 1, stride=1, stride_axis=0).astype(jnp.bfloat16)
    grad_qp = mxu(
        flip.astype(jnp.float32),
        mxu(turned, rel_ref[pl.ds(base, span), :], NN),
        NN,
        exact_mode,
    )
    pos_turned = mxu(query_t[KD:], flip, NN).astype(jnp.bfloat16)
    drel_ref[:, pl.ds(base, span)] += mxu(pos_turned, turned, NN)
    stat_ref[0:1, :KD] += jnp.sum(grad_qc, axis=0, keepdims=True)
    stat_ref[1:2, :KD] += jnp.sum(grad_qp, axis=0, keepdims=True)
    out_ref[pl.ds(step, 1), VD + KD :, :] = (
        ((grad_qc + grad_qp) * (KD**-0.5)).T.astype(jnp.bfloat16)[None]
    )

    @pl.when(step == steps - 1)
    def _():
        for part in range(steps):
            out_ref[part, : VD + KD, :] = acc_ref[:, part * block : (part + 1) * block].astype(
                jnp.bfloat16
            )


def attend_backward(pack, rel, probs, grad):
    bins = pack.shape[0]
    block = query_block(bins)
    steps = bins // block
    return pl.pallas_call(
        lambda *refs: attend_backward_kernel(block, bins, *refs),
        grid=(steps,),
        in_specs=[
            pl.BlockSpec((bins, PACK), lambda i: (0, 0)),
            pl.BlockSpec((2 * bins, KD), lambda i: (0, 0)),
            pl.BlockSpec((block, bins), lambda i: (i, 0)),
            pl.BlockSpec((1, VD, block), lambda i: (i, 0, 0)),
        ],
        out_specs=[
            pl.BlockSpec((steps, GRAD_PACK, block), lambda i: (0, 0, 0)),
            pl.BlockSpec((KD, 2 * bins), lambda i: (0, 0)),
            pl.BlockSpec((8, 128), lambda i: (0, 0)),
        ],
        out_shape=[
            jax.ShapeDtypeStruct((steps, GRAD_PACK, block), jnp.bfloat16),
            jax.ShapeDtypeStruct((KD, 2 * bins), jnp.float32),
            jax.ShapeDtypeStruct((8, 128), jnp.float32),
        ],
        scratch_shapes=[pltpu.VMEM((VD + KD, bins), jnp.float32)],
        compiler_params=pltpu.CompilerParams(vmem_limit_bytes=48 << 20),
        cost_estimate=pl.CostEstimate(flops=1, bytes_accessed=1, transcendentals=0),
        name="attend_backward",
    )(pack, rel, probs, grad)


def heads_kernel(
    track_human,
    track_mouse,
    pick_ref,
    rows_ref,
    weight_ref,
    human_ref,
    mouse_ref,
    human_other_ref,
    mouse_other_ref,
    bias_ref,
    count_human_ref,
    count_mouse_ref,
    grad_ref,
    dtrunk_ref,
    dbias_ref,
    loss_ref,
):
    step = pl.program_id(0)
    kind, swapped = pick_ref[0], pick_ref[1] == 1

    @pl.when(step == 0)
    def _():
        dtrunk_ref[...] = jnp.zeros_like(dtrunk_ref)
        loss_ref[...] = jnp.zeros_like(loss_ref)

    def score(own_ref, other_ref, count_ref, tracks):
        valid = lax.broadcasted_iota(jnp.int32, (TILE, 1), 0) + step * TILE < tracks
        own = jnp.where(valid, own_ref[...], 0.0).astype(jnp.bfloat16)
        oth = jnp.where(valid, other_ref[...], 0.0).astype(jnp.bfloat16)
        head = jnp.concatenate(
            [jnp.where(swapped, oth, own), jnp.where(swapped, own, oth)], axis=1
        )
        logits = mxu(head, rows_ref[...], NT) + bias_ref[:, 0:1]
        counts = count_ref[0].astype(jnp.float32)
        small = jnp.exp(-jnp.abs(logits))
        inverse = 1.0 / (1.0 + small)
        predicted = jnp.maximum(logits, 0.0) + jnp.log1p(small)
        shifted = predicted + log_eps
        sigma = jnp.where(logits >= 0.0, 1.0, small) * inverse
        weight = jnp.where(valid, weight_ref[0:1, :], 0.0)
        rows_loss = weight * (predicted - counts * jnp.log(shifted))
        grad = weight * (sigma - counts * sigma / shifted)
        loss_ref[...] += jnp.sum(rows_loss.reshape(TILE // 8, 8, -1), axis=0)
        bins = grad.shape[1]
        if bins % 128 == 0:
            folded = sum(grad[:, i : i + 128] for i in range(0, bins, 128))
        else:
            folded = jnp.broadcast_to(jnp.sum(grad, axis=1, keepdims=True) / 128, (TILE, 128))
        dbias_ref[...] = jnp.sum(folded.T.reshape(16, 8, TILE), axis=0)
        grad_low = grad.astype(jnp.bfloat16)
        grad_ref[...] = grad_low
        dtrunk_ref[...] += mxu(grad_low.T, head, NN)

    @pl.when(jnp.logical_and(kind == 0, step < pl.cdiv(track_human, TILE)))
    def _():
        score(human_ref, human_other_ref, count_human_ref, track_human)

    @pl.when(jnp.logical_and(kind == 1, step < pl.cdiv(track_mouse, TILE)))
    def _():
        score(mouse_ref, mouse_other_ref, count_mouse_ref, track_mouse)


def score_heads(window, pick, rows, weight, own, others, bias, count_human, count_mouse):
    bins, width = rows.shape
    share = own[0].shape[1]
    rest = width - share
    track_human, track_mouse = count_human.shape[1], count_mouse.shape[1]
    tiles_human, tiles_mouse = pl.cdiv(track_human, TILE), pl.cdiv(track_mouse, TILE)

    def tile(kind, tiles):
        return lambda t, p: jnp.where(p[0] == kind, jnp.minimum(t, tiles - 1), 0)

    human_tile, mouse_tile = tile(0, tiles_human), tile(1, tiles_mouse)

    def out_tile(t, p):
        mine = jnp.where(p[0] == 0, jnp.minimum(t, tiles_human - 1), 0)
        return jnp.where(p[0] == 1, tiles_human + jnp.minimum(t, tiles_mouse - 1), mine)

    whole = lambda t, p: (0, 0)
    tracks = (tiles_human + tiles_mouse) * TILE
    return pl.pallas_call(
        lambda *refs: heads_kernel(track_human, track_mouse, *refs),
        grid_spec=pltpu.PrefetchScalarGridSpec(
            num_scalar_prefetch=1,
            grid=(max(tiles_human, tiles_mouse),),
            in_specs=[
                pl.BlockSpec((bins, width), whole),
                pl.BlockSpec((8, bins), whole),
                pl.BlockSpec((TILE, share), lambda t, p: (human_tile(t, p), 0)),
                pl.BlockSpec((TILE, share), lambda t, p: (mouse_tile(t, p), 0)),
                pl.BlockSpec((TILE, rest), lambda t, p: (human_tile(t, p), 0)),
                pl.BlockSpec((TILE, rest), lambda t, p: (mouse_tile(t, p), 0)),
                pl.BlockSpec((TILE, 128), lambda t, p: (out_tile(t, p), 0)),
                pl.BlockSpec((1, TILE, bins), lambda t, p: (window, human_tile(t, p), 0)),
                pl.BlockSpec((1, TILE, bins), lambda t, p: (window, mouse_tile(t, p), 0)),
            ],
            out_specs=[
                pl.BlockSpec((TILE, bins), lambda t, p: (out_tile(t, p), 0)),
                pl.BlockSpec((bins, width), whole),
                pl.BlockSpec((8, TILE), lambda t, p: (0, out_tile(t, p))),
                pl.BlockSpec((8, bins), whole),
            ],
        ),
        out_shape=[
            jax.ShapeDtypeStruct((tracks, bins), jnp.bfloat16),
            jax.ShapeDtypeStruct((bins, width), jnp.float32),
            jax.ShapeDtypeStruct((8, tracks), jnp.float32),
            jax.ShapeDtypeStruct((8, bins), jnp.float32),
        ],
        compiler_params=pltpu.CompilerParams(vmem_limit_bytes=56 << 20),
        cost_estimate=pl.CostEstimate(flops=1, bytes_accessed=1, transcendentals=0),
        name="score_heads",
    )(pick, rows, weight, *own, *others, bias, count_human, count_mouse)


def head_tile(step, parity, quarter):
    upper = jnp.where(step >= quarter, 1, 0)
    return upper * quarter + parity * quarter + step


def head_grads_kernel(windows, tiles_human, quarter, has_more, pick_ref, *refs):
    grads, rows, out_ref, acc_ref = refs[:windows], refs[windows], refs[-2], refs[-1]
    tile = head_tile(pl.program_id(0), pick_ref[windows], quarter)
    mine = jnp.where(tile < tiles_human, 0, 1)
    acc_ref[...] = refs[windows + 1][...].astype(jnp.float32) if has_more else jnp.zeros_like(acc_ref)
    for window in range(windows):

        @pl.when(pick_ref[window] == mine)
        def _():
            acc_ref[...] += mxu(grads[window][...], rows[window], NN)

    out_ref[...] = acc_ref[...].astype(jnp.bfloat16)


def head_grads(pick, grads, rows, tiles_human, tiles, more=None):
    windows, bins, share = rows.shape
    last = grads[0].shape[0] // TILE - 1

    def tile_of(window):
        def index(t, p):
            tile = head_tile(t, p[windows], tiles // 2)
            kept = jnp.where(p[window] == 0, jnp.minimum(tile, tiles_human - 1), 0)
            kept = jnp.where(p[window] == 1, jnp.maximum(tile, tiles_human), kept)
            return (jnp.minimum(kept, last), 0)

        return index

    extra = [] if more is None else [more]
    return pl.pallas_call(
        lambda *refs: head_grads_kernel(
            windows, tiles_human, tiles // 2, more is not None, *refs
        ),
        grid_spec=pltpu.PrefetchScalarGridSpec(
            num_scalar_prefetch=1,
            grid=(tiles,),
            in_specs=[pl.BlockSpec((TILE, bins), tile_of(w)) for w in range(windows)]
            + [pl.BlockSpec((windows, bins, share), lambda t, p: (0, 0, 0))]
            + [pl.BlockSpec((TILE, share), lambda t, p: (t, 0))] * len(extra),
            out_specs=pl.BlockSpec((TILE, share), lambda t, p: (t, 0)),
            scratch_shapes=[pltpu.VMEM((TILE, share), jnp.float32)],
        ),
        out_shape=jax.ShapeDtypeStruct((tiles * TILE, share), jnp.bfloat16),
        compiler_params=pltpu.CompilerParams(vmem_limit_bytes=40 << 20),
        cost_estimate=pl.CostEstimate(flops=1, bytes_accessed=1, transcendentals=0),
        name="head_grads",
    )(pick, *grads, rows, *extra)


def half_product_kernel(windows, turned, has_more, pick_ref, *refs):
    lefts, rights, out_ref = refs[:windows], refs[windows : 2 * windows], refs[-1]
    total = None
    for left, right in zip(lefts, rights):
        if turned:
            term = mxu(right[...], left[...], NN)
        else:
            term = mxu(left[...], right[...], TN)
        total = term if total is None else total + term
    if turned:
        total = total.T
    if has_more:
        total = total + refs[2 * windows][...].astype(jnp.float32)
    out_ref[...] = total.astype(jnp.bfloat16)


def half_product(half, lefts, rights, slabs, turned, more=None):
    windows = len(lefts)
    rows, width = lefts[0].shape
    slab = width // slabs
    cols = rights[0].shape[0 if turned else 1]
    step = cols
    while step > 768 and step % 256 == 0:
        step //= 2
    left_spec = pl.BlockSpec((rows, slab), lambda u, j, p: (0, 2 * u + p[0]))
    if turned:
        right_spec = pl.BlockSpec((step, rows), lambda u, j, p: (j, 0))
    else:
        right_spec = pl.BlockSpec((rows, step), lambda u, j, p: (0, j))
    out_spec = pl.BlockSpec((slab, step), lambda u, j, p: (u, j))
    extra = [] if more is None else [more]
    return pl.pallas_call(
        lambda *refs: half_product_kernel(windows, turned, more is not None, *refs),
        grid_spec=pltpu.PrefetchScalarGridSpec(
            num_scalar_prefetch=1,
            grid=(slabs // 2, cols // step),
            in_specs=[left_spec] * windows + [right_spec] * windows + [out_spec] * len(extra),
            out_specs=out_spec,
        ),
        out_shape=jax.ShapeDtypeStruct((width // 2, cols), jnp.bfloat16),
        compiler_params=pltpu.CompilerParams(vmem_limit_bytes=48 << 20),
        cost_estimate=pl.CostEstimate(flops=1, bytes_accessed=1, transcendentals=0),
        name="half_product",
    )(half, *lefts, *rights, *extra)


def norm_stats(values):
    mean = jnp.mean(values, axis=-1, keepdims=True)
    centred = values - mean
    inverse = lax.rsqrt(jnp.mean(centred * centred, axis=-1, keepdims=True) + norm_eps)
    return mean, inverse


def norm_backward(grad_output, scaled, inverse, norm_gain):
    grad_scaled = grad_output * norm_gain
    mean_grad = jnp.mean(grad_scaled, axis=-1, keepdims=True)
    mean_proj = jnp.mean(grad_scaled * scaled, axis=-1, keepdims=True)
    grad_input = inverse * (grad_scaled - mean_grad - scaled * mean_proj)
    return (grad_input, jnp.sum(grad_output * scaled, axis=0), jnp.sum(grad_output, axis=0))


def sum_over_model(partial, done, after_line):
    low = done(partial.astype(jnp.bfloat16))
    if lax.axis_size("mp") == 2:
        other = lax.ppermute(low, "mp", [(0, 1), (1, 0)])
        return lambda: low.astype(jnp.float32) + after_line(other).astype(jnp.float32)
    total = lax.psum(low, "mp")
    return lambda: after_line(total).astype(jnp.float32)


def in_model_order(own, dim, after_line):
    if lax.axis_size("mp") == 2:
        first = lax.axis_index("mp") == 0
        other = lax.ppermute(own, "mp", [(0, 1), (1, 0)])

        def ordered():
            got = after_line(other)
            return jnp.concatenate(
                [jnp.where(first, own, got), jnp.where(first, got, own)], axis=dim
            )

        return ordered
    full = lax.all_gather(own, "mp", axis=dim, tiled=True)
    return lambda: after_line(full)


class OtherRows:
    def __init__(self, own, tile, after_line, done):
        self.after_line, self.done = after_line, done
        count = lax.axis_size("dp")
        size = -(-own.shape[0] // tile) * tile // count
        part = None
        for place in range(count - 1, -1, -1):
            piece = own[place * size : (place + 1) * size]
            piece = jnp.pad(piece, [(0, size - piece.shape[0]), (0, 0)])
            here = lax.axis_index("dp") == place
            part = piece if part is None else jnp.where(here, piece, part)
        self.mine = lax.ppermute(done(part), "mp", [(0, 1), (1, 0)])

    def share(self):
        self.full = lax.all_gather(
            self.done(self.after_line(self.mine)), "dp", axis=0, tiled=True
        )

    def finish(self):
        return self.after_line(self.full)


def swap_pairs(axis, step):
    return [(i, i ^ step) for i in range(lax.axis_size(axis))]


class SmallSums:
    def __init__(self, parts, axes, after_line, done):
        self.parts, self.after_line, self.done = parts, after_line, done
        padded = [jnp.pad(x.reshape(-1), (0, -x.size % 128)) for x in parts]
        self.total = jnp.concatenate(padded).reshape(-1, 128)
        self.moves = [
            (axis, 1 << bit)
            for axis in axes
            for bit in range(lax.axis_size(axis).bit_length() - 1)
        ]
        self.got = None
        self.step()

    def step(self):
        if self.got is not None:
            self.total, self.got = self.total + self.after_line(self.got), None
        if self.moves:
            axis, step = self.moves.pop(0)
            self.total = self.done(self.total)
            self.got = lax.ppermute(self.total, axis, swap_pairs(axis, step))

    def finish(self):
        while self.got is not None:
            self.step()
        results, start, total = [], 0, self.total.reshape(-1)
        for x in self.parts:
            results.append(total[start : start + x.size].reshape(x.shape))
            start += -(-x.size // 128) * 128
        return results


class SeqSum:
    def __init__(self, parts, done):
        self.got = lax.all_to_all(done(parts), "seq", split_axis=0, concat_axis=0, tiled=True)

    def arrive(self, after_line):
        self.got = after_line(self.got)

    def finish(self, after_line, done):
        return done(jnp.sum(after_line(self.got).astype(jnp.float32), axis=0))


class ScatterProduct:
    def __init__(self, lefts, rights, after_line, done, turned=False):
        self.after_line, self.done, self.turned = after_line, done, turned
        self.lefts, self.rights = lefts, rights
        lefts = [after_line(lefts[0])] + lefts[1:]
        self.got = lax.ppermute(done(self.half(1, lefts)), "dp", swap_pairs("dp", 1))

    def half(self, other, lefts, more=None):
        pick = jnp.reshape((lax.axis_index("dp") + other) % 2, (1,)).astype(jnp.int32)
        return half_product(pick, lefts, self.rights, lax.axis_size("dp"), self.turned, more)

    def keep(self):
        self.kept = self.done(self.half(0, self.lefts, self.after_line(self.got)))
        return self


class ScatterRest:
    def __init__(self, kept, after_line, done):
        self.after_line, self.done = after_line, done
        size = kept.shape[0] // 2
        upper = lax.axis_index("dp") // 2 == 1
        low, high = kept[:size], kept[size:]
        self.mine = jnp.where(upper, high, low)
        self.got = lax.ppermute(done(jnp.where(upper, low, high)), "dp", swap_pairs("dp", 2))

    def along_seq(self):
        got = self.after_line(self.got).astype(jnp.float32)
        total = (self.mine.astype(jnp.float32) + got).astype(jnp.bfloat16)
        parts = total.reshape(lax.axis_size("seq"), -1, total.shape[1])
        self.sum = SeqSum(parts, self.done)

    def arrive(self):
        self.sum.arrive(self.after_line)

    def finish(self):
        return self.sum.finish(self.after_line, self.done)


def on_device(
    trunk_in,
    norm1_gain,
    norm1_bias,
    w_query,
    w_key,
    w_value,
    w_rel,
    content_bias,
    pos_bias,
    w_out,
    b_out,
    norm2_gain,
    norm2_bias,
    w_in,
    b_in,
    w_hid,
    b_hid,
    head_human,
    bias_human,
    head_mouse,
    bias_mouse,
    species,
    targets_human,
    targets_mouse,
):
    windows, bins, width = trunk_in.shape
    heads = content_bias.shape[0]
    dp_size, seq_size, mp_size = (lax.axis_size(axis) for axis in ("dp", "seq", "mp"))
    seq_index, mp_index = lax.axis_index("seq"), lax.axis_index("mp")
    place = lax.axis_index("dp") * seq_size + seq_index
    places = dp_size * seq_size
    all_bins = bins * seq_size
    query_start = seq_index * bins
    key_scale = KD ** (-0.5)
    loss_scale = 1.0 / math.sqrt(windows * dp_size * CROP)
    crop_start = (all_bins - CROP) // 2
    bf16 = jnp.bfloat16
    me = jnp.reshape(seq_index, (1,)).astype(jnp.int32)

    groups = [[w] for w in range(windows)] if heads % seq_size == 0 else [list(range(windows))]
    group_size = len(groups[0])
    pairs = heads * group_size
    pairs_here = -(-pairs // seq_size)
    block = query_block(all_bins)
    pair_heads = [
        jnp.minimum((seq_index * pairs_here + j) // group_size, heads - 1)
        for j in range(pairs_here)
    ]

    tokens = [jnp.zeros((8, 128), jnp.float32)]

    def after_line(array):
        array, token = lax.optimization_barrier((array, tokens[-1]))
        tokens.append(token)
        return array

    done = after_line

    def exchange(array):
        return lax.all_to_all(array, "seq", split_axis=0, concat_axis=0, tiled=True)

    def spread(array):
        short = seq_size * pairs_here - pairs
        if short:
            array = jnp.pad(array, [(0, short)] + [(0, 0)] * (array.ndim - 1))
        return exchange(array.reshape((seq_size, pairs_here) + array.shape[1:]))

    def regroup(array, size):
        if array.shape[2] == size:
            return array
        depth = array.shape[1]
        array = array.transpose(1, 0, 2).reshape(depth, all_bins // size, size)
        return array.transpose(1, 0, 2)

    def to_owners(arrays):
        return exchange(jnp.stack([regroup(a, bins) for a in arrays], axis=1))

    def by_head(array):
        depth = array.shape[2]
        array = array.reshape(seq_size * pairs_here, depth, bins)[:pairs]
        array = array.reshape(heads, group_size, depth, bins).transpose(0, 2, 1, 3)
        return array.reshape(heads * depth, group_size * bins)

    track_human, track_mouse = head_human.shape[1], head_mouse.shape[1]
    own_heads = (head_human.T, head_mouse.T)
    parts = {}

    def fetch_out(_):
        if mp_size == 2:
            parts["out"] = OtherRows(w_out, w_out.shape[0], after_line, done)

    def fetch_out_share(_):
        if mp_size == 2:
            parts["out"].share()

    def fetch_out_end(_):
        if mp_size != 2:
            parts["w_out"] = lax.all_gather(w_out, "mp", axis=0, tiled=True)
            return
        other, first = parts["out"].finish(), mp_index == 0
        parts["w_out"] = done(
            jnp.concatenate(
                [jnp.where(first, w_out, other), jnp.where(first, other, w_out)], axis=0
            )
        )

    def fetch_heads(_):
        if mp_size == 2:
            parts["heads"] = [OtherRows(own, TILE, after_line, done) for own in own_heads]

    def fetch_human_share(_):
        if mp_size == 2:
            parts["heads"][0].share()

    def fetch_mouse_share(_):
        if mp_size == 2:
            parts["heads"][1].share()

    def fetch_heads_end(_):
        if mp_size == 2:
            parts["others"] = [part.finish() for part in parts["heads"]]
            parts["own"] = own_heads
            return
        full = [lax.all_gather(own, "mp", axis=1, tiled=True) for own in own_heads]
        parts["own"] = [x[:, : width // 2] for x in full]
        parts["others"] = [x[:, width // 2 :] for x in full]

    def of_head(weight, size, h):
        return weight[:, h * size : (h + 1) * size]

    w_packs = [
        jnp.concatenate(
            [of_head(w_value, VD, h), of_head(w_key, KD, h)] + [of_head(w_query, KD, h)] * 2, axis=1
        )
        for h in range(heads)
    ]
    w_grad = jnp.concatenate([w[:, :GRAD_PACK] for w in w_packs], axis=1)
    pack_scale = jnp.concatenate(
        [jnp.ones((VD + KD,), jnp.float32), jnp.full((2 * KD,), key_scale, jnp.float32)]
    )
    pack_biases = [
        jnp.concatenate([jnp.zeros((VD + KD,), jnp.float32), content_bias[h], pos_bias[h]])
        for h in range(heads)
    ]

    basis = jnp.pad(rel_basis(), [(0, 1), (0, 0)])
    w_rel_heads = w_rel.reshape(FEAT, heads, KD)
    rels = [
        mxu(
            basis,
            lax.dynamic_index_in_dim(w_rel_heads, head, 1, keepdims=False).astype(jnp.float32),
            NN,
            exact_mode,
        ).astype(bf16)
        for head in pair_heads
    ]

    count = len(groups)
    many = lambda: [None] * count
    trunk, stats1, normed1, packs, probs, attended = many(), many(), many(), many(), many(), many()
    mids, stats2, normed2, preacts, actives = many(), many(), many(), many(), many()
    trunk_out, grad_trunks, grad_outs, grad_pres = many(), many(), many(), many()
    grad_mids, grad_mid_lows, packed_grads, grad_inputs = many(), many(), many(), many()
    moving, grad_att, own_rows = many(), many(), [None] * windows
    logit_grads, track_sums, losses = [None] * windows, [], []
    sums = [0.0] * 5
    sums1 = [0.0, 0.0]
    drels = [0.0] * pairs_here
    dstats = [0.0] * pairs_here

    def project(g):
        rows = group_size * bins
        values = trunk_in[groups[g][0] : groups[g][-1] + 1].reshape(rows, width).astype(jnp.float32)
        mean, inverse = norm_stats(values)
        normed = ((values - mean) * inverse * norm1_gain + norm1_bias).astype(bf16)
        normed = after_line(normed)
        trunk[g], stats1[g], normed1[g] = values, (mean, inverse), normed
        parts = []
        for h in range(heads):
            pack = (mxu(normed, w_packs[h], NN) * pack_scale + pack_biases[h]).astype(bf16)
            parts.append(pack.reshape(group_size, bins, PACK))
        pack = spread(done(jnp.concatenate(parts, axis=0)))
        packs[g] = pack

    def arrive(g):
        packs[g] = after_line(packs[g])

    def arrive_out(g):
        moving[g] = after_line(moving[g])

    def arrive_grad(g):
        grad_att[g] = after_line(grad_att[g])

    def arrive_packed(g):
        packed_grads[g] = by_head(after_line(packed_grads[g]))

    def attend(g):
        outs, kept = [], []
        pack = after_line(packs[g])
        packs[g] = [pack[:, j].reshape(all_bins, PACK) for j in range(pairs_here)]
        for j in range(pairs_here):
            out, prob = attend_forward(packs[g][j], rels[j])
            outs.append(done(out))
            kept.append(prob)
        probs[g] = kept
        moving[g] = to_owners(outs)

    def attend_swap(g):
        attended[g] = done(by_head(after_line(moving[g])))
        moving[g] = in_model_order(attended[g], 0, after_line)

    def feed_forward(g):
        mid = trunk[g] + mxu(moving[g](), parts["w_out"], TN) + b_out
        mean, inverse = norm_stats(mid)
        normed = ((mid - mean) * inverse * norm2_gain + norm2_bias).astype(bf16)
        preact = mxu(normed, w_in, NN) + b_in
        active = jnp.maximum(preact, 0.0).astype(bf16)
        mids[g], stats2[g], normed2[g], actives[g] = mid, (mean, inverse), normed, active
        moving[g] = sum_over_model(mxu(active, w_hid, NN), done, after_line)

    def score(g):
        out = mids[g] + (moving[g]() + b_hid)
        trunk_out[g] = out
        low = out.astype(bf16)
        grads = []
        for i, window in enumerate(groups[g]):
            rows = low[i * bins : (i + 1) * bins]
            own_rows[window] = lax.dynamic_slice_in_dim(rows, mp_index * share, share, 1)
            pick = jnp.stack([picks[window], jnp.int32(0) + order])
            logit_grads[window], grad_out, track_sum, loss = score_heads(
                window, pick, rows, weight, parts["own"], parts["others"], bias_rows[0], count_human, count_mouse
            )
            track = jnp.sum(track_sum, axis=0)
            scored = jnp.arange(track.size) < tiles_human * TILE
            scored = scored == (picks[window] == 0)
            track_sums.append(jnp.where(scored & (picks[window] < 2), track, 0.0))
            losses.append(jnp.sum(loss))
            grads.append(grad_out)
        grad_trunks[g] = done(jnp.concatenate(grads, axis=0))

    def back_hidden(g):
        grad_out = after_line(grad_trunks[g].astype(bf16))
        grad_preact = jnp.where(actives[g] > 0, mxu(grad_out, w_hid, NT), 0.0)
        grad_pre = grad_preact.astype(bf16)
        grad_outs[g], grad_pres[g] = grad_out, grad_pre
        sums[3] = sums[3] + jnp.sum(grad_trunks[g], axis=0)
        sums[4] = sums[4] + jnp.sum(grad_preact, axis=0)
        moving[g] = sum_over_model(mxu(grad_pre, w_in, NT), done, after_line)

    def back_mid(g):
        mean, inverse = stats2[g]
        grad_normed = moving[g]()
        grad_norm, dgain, dbias = norm_backward(
            grad_normed, (mids[g] - mean) * inverse, inverse, norm2_gain
        )
        grad_mids[g] = grad_trunks[g] + grad_norm
        grad_mid_lows[g] = grad_mids[g].astype(bf16)
        sums[0] = sums[0] + dgain
        sums[1] = sums[1] + dbias
        sums[2] = sums[2] + jnp.sum(grad_mids[g], axis=0)
        grad = done(mxu(w_out, grad_mid_lows[g], NT).astype(bf16))
        grad = grad.reshape(heads, VD, group_size, bins).transpose(0, 2, 1, 3)
        grad_att[g] = spread(grad.reshape(pairs, VD, bins))

    def back_attend(g):
        outs = []
        grad = after_line(grad_att[g])
        for j in range(pairs_here):
            out, drel, stat = attend_backward(
                packs[g][j], rels[j], probs[g][j], regroup(grad[:, j], block)
            )
            outs.append(done(out))
            drels[j] = drels[j] + drel
            dstats[j] = dstats[j] + stat
        packed_grads[g] = to_owners(outs)

    def back_project(g):
        packed_grads[g] = after_line(packed_grads[g])
        product = lax.dot_general(
            packed_grads[g],
            w_grad,
            (((0,), (1,)), ((), ())),
            preferred_element_type=jnp.float32,
        )
        moving[g] = sum_over_model(product, done, after_line)

    def back_input(g):
        mean, inverse = stats1[g]
        grad_norm, dgain, dbias = norm_backward(
            moving[g](), (trunk[g] - mean) * inverse, inverse, norm1_gain
        )
        sums1[0] = sums1[0] + dgain
        sums1[1] = sums1[1] + dbias
        grad_inputs[g] = (grad_mids[g] + grad_norm).reshape(group_size, bins, width)

    bin_place = query_start + jnp.arange(bins)
    in_crop = ((bin_place >= crop_start) & (bin_place < crop_start + CROP)).astype(jnp.float32)
    weight = jnp.broadcast_to((in_crop * loss_scale)[None, :], (8, bins))
    has_crop = (query_start + bins > crop_start) & (query_start < crop_start + CROP)
    picks = jnp.where(has_crop, species, 2)
    count_human = targets_human.transpose(0, 2, 1)
    count_mouse = targets_mouse.transpose(0, 2, 1)
    tiles_human, tiles_mouse = pl.cdiv(track_human, TILE), pl.cdiv(track_mouse, TILE)
    half_tiles = (tiles_human + tiles_mouse) // 2
    bias_all = jnp.concatenate(
        [
            jnp.pad(bias_human, (0, tiles_human * TILE - track_human)),
            jnp.pad(bias_mouse, (0, tiles_mouse * TILE - track_mouse)),
        ]
    )
    bias_rows = []

    def spread_bias(_):
        wide = jnp.broadcast_to(after_line(bias_all)[:, None], (bias_all.size, 128))
        bias_rows.append(done(wide))

    order = mp_index if mp_size == 2 else 0
    share = head_human.shape[0]
    join = lambda arrays: jnp.concatenate(arrays, axis=0)
    results = {}
    width_out = heads * VD

    def pick_half(half):
        return jnp.concatenate([picks, jnp.reshape(half, (1,)).astype(jnp.int32)])

    def grads_heads(_):
        parity = lax.axis_index("dp") % 2
        rows = jnp.stack(own_rows)
        grads = [after_line(logit_grads[0])] + logit_grads[1:]
        sent = head_grads(pick_half(1 - parity), grads, rows, tiles_human, half_tiles)
        got = lax.ppermute(done(sent), "dp", swap_pairs("dp", 1))
        results["heads"] = (grads, rows, got, parity)

    def grads_heads_keep(_):
        grads, rows, got, parity = results["heads"]
        kept = done(
            head_grads(pick_half(parity), grads, rows, tiles_human, half_tiles, after_line(got))
        )
        results["heads"] = ScatterRest(kept, after_line, done)

    def grads_heads_seq(_):
        results["heads"].along_seq()

    def heads_arrive(_):
        results["heads"].arrive()

    def wide_arrive(_):
        results["wide"].arrive()

    def grads_heads_end(_):
        total = results["heads"].finish().astype(bf16)
        results["heads"] = lax.all_gather(total, ("dp", "seq"), axis=0, tiled=True)

    def grads_in(_):
        results["in"] = ScatterProduct(normed2, grad_pres, after_line, done)

    def grads_hid(_):
        results["hid"] = ScatterProduct(grad_outs, actives, after_line, done)

    def grads_in_keep(_):
        results["in"].keep()

    def grads_hid_keep(_):
        results["hid"].keep()
        kept = jnp.concatenate([results["in"].kept, results["hid"].kept], axis=1)
        results["wide"] = ScatterRest(kept, after_line, done)

    def grads_wide_seq(_):
        results["wide"].along_seq()

    def grads_wide_end(_):
        results["wide"] = results["wide"].finish()

    def grads_out(_):
        results["out"] = ScatterProduct(grad_mid_lows, attended, after_line, done, True)

    def grads_out_keep(_):
        results["out"].keep()

    def grads_pack(_):
        results["pack"] = ScatterProduct(normed1, packed_grads, after_line, done, True)

    def grads_pack_keep(_):
        kept = jnp.concatenate([results["out"].kept, results["pack"].keep().kept], axis=1)
        results["late_rows"] = ScatterRest(kept, after_line, done)

    def grads_pack_seq(_):
        results["late_rows"].along_seq()

    def grads_pack_end(_):
        late = results["late_rows"].finish()
        results["out"], results["pack"] = late[:, :width_out], late[:, width_out:]

    def sums_heads(_):
        dw_rel = jnp.zeros((heads, FEAT, KD), jnp.float32)
        dstat = jnp.zeros((heads, 2, KD), jnp.float32)
        for j, head in enumerate(pair_heads):
            part = lax.dot_general(
                basis,
                drels[j],
                (((0,), (1,)), ((), ())),
                precision=exact_mode,
                preferred_element_type=jnp.float32,
            )
            mine = (jnp.arange(heads) == head).astype(jnp.float32)[:, None, None]
            dw_rel = dw_rel + mine * part
            dstat = dstat + mine * dstats[j][None, :2, :KD]
        values = [part, dstats[0]] if heads == seq_size else [dstat, dw_rel]
        axes = ("dp",) if heads == seq_size else ("dp", "seq")
        results["own_head"] = SmallSums(values, axes, after_line, done)

    def sums_late(_):
        values = list(sums1) + list(sums) + [sum(track_sums), sum(losses)[None]]
        results["late"] = SmallSums(values, ("dp", "seq"), after_line, done)

    def step_heads(_):
        results["own_head"].step()

    def step_late(_):
        results["late"].step()

    def heads_out(_):
        full = after_line(results["heads"])
        first = tiles_human * TILE
        results["human"] = done(full[:track_human].astype(jnp.float32))
        results["mouse"] = done(full[first : first + track_mouse].astype(jnp.float32))

    def each(stage):
        return [(stage, g) for g in range(count)]

    def one(*stages):
        return [(stage, -1) for stage in stages]

    if count == 3:
        plan = one(fetch_out) + [(project, 0)] + one(fetch_out_share, fetch_heads)
        plan += [(project, 1), (project, 2)] + one(spread_bias) + [(attend, 0), (attend, 1)]
        plan += one(fetch_human_share) + [(attend_swap, 0)] + one(fetch_out_end)
        plan += [(feed_forward, 0)] + one(fetch_mouse_share) + [(attend, 2), (attend_swap, 1)]
        plan += [(feed_forward, 1), (attend_swap, 2)] + one(fetch_heads_end)
        plan += [(score, 0), (feed_forward, 2), (back_hidden, 0)]
        plan += [(score, 1), (back_hidden, 1), (back_mid, 0), (score, 2), (arrive_grad, 0)]
        plan += one(grads_heads) + [(back_attend, 0), (back_hidden, 2)] + one(grads_heads_keep)
        plan += [(back_mid, 1), (arrive_packed, 0), (back_project, 0)] + one(grads_in)
        plan += [(back_mid, 2), (arrive_grad, 1), (back_attend, 1)] + one(grads_hid, grads_in_keep)
        plan += [(arrive_grad, 2)] + one(grads_heads_seq) + [(back_attend, 2)]
        plan += one(grads_hid_keep) + [(back_input, 0)] + one(heads_arrive, grads_out)
        plan += one(sums_heads, grads_out_keep) + [(arrive_packed, 1), (back_project, 1)]
        plan += one(grads_wide_seq, step_heads) + [(arrive_packed, 2)] + one(grads_heads_end)
        plan += one(grads_pack) + [(back_project, 2)] + one(grads_pack_keep)
        plan += [(back_input, 1)] + one(wide_arrive, step_heads) + [(back_input, 2)]
        plan += one(sums_late, grads_pack_seq, step_late, grads_wide_end, step_late)
        plan += one(heads_out, step_late, grads_pack_end, step_late)
    else:
        plan = one(fetch_out, fetch_out_share, fetch_out_end, spread_bias)
        plan += one(fetch_heads, fetch_human_share, fetch_mouse_share, fetch_heads_end)
        plan += each(project) + each(attend) + each(attend_swap) + each(feed_forward) + each(score)
        plan += each(back_hidden) + each(back_mid)
        plan += one(grads_heads, grads_heads_keep, grads_heads_seq, grads_heads_end)
        plan += each(back_attend) + one(grads_in, grads_in_keep, grads_hid, grads_hid_keep)
        plan += one(grads_wide_seq, grads_wide_end, grads_out, grads_out_keep)
        plan += each(arrive_packed) + each(back_project) + one(grads_pack, grads_pack_keep)
        plan += one(grads_pack_seq, grads_pack_end) + each(back_input)
        plan += one(sums_heads, sums_late, heads_out)
    for stage, g in plan:
        stage(g)
    summed = results["late"].finish()
    dgain1, dbias1, dgain2, dbias2, db_out, db_hid, db_in, dtracks, loss = summed
    mids_sum = results["own_head"].finish()
    if heads == seq_size:
        share_rel, share_stat = FEAT // places, KD // places
        own_rel = mids_sum[0].reshape(dp_size, seq_size, share_rel * KD)
        own_stat = mids_sum[1][:2, :KD].reshape(2, dp_size, seq_size, share_stat)
        dp_here = lax.axis_index("dp")
        own_rel = lax.dynamic_index_in_dim(own_rel, dp_here, 0, keepdims=False)
        own_stat = lax.dynamic_index_in_dim(own_stat, dp_here, 1, keepdims=False)
        own_stat = own_stat.transpose(1, 0, 2).reshape(seq_size, 2 * share_stat)
        small = jnp.concatenate([own_rel, own_stat], axis=1)
        small = jnp.pad(small, [(0, 0), (0, -small.shape[1] % 128)])
        small = lax.all_to_all(small[:, None], "seq", split_axis=0, concat_axis=0, tiled=True)[:, 0]
        rel_rows = small[:, : share_rel * KD].reshape(heads, share_rel, KD)
        rel_rows = rel_rows.transpose(1, 0, 2).reshape(share_rel, heads * KD)
        stats = small[:, share_rel * KD : share_rel * KD + 2 * share_stat]
        dstat = stats.reshape(heads, 2, share_stat)
        dcontent, dposition = dstat[:, 0], dstat[:, 1]
    else:
        dstat, dw_rel = mids_sum
    dw_out = results["out"]
    dw_in, dw_hid = jnp.split(results["wide"], 2, axis=1)
    pack_summed = results["pack"].reshape(-1, heads, GRAD_PACK)
    def own(array, dim=0):
        size = array.shape[dim] // places
        return lax.dynamic_slice_in_dim(array, place * size, size, dim)

    if heads != seq_size:
        rel_rows = own(dw_rel, 1).transpose(1, 0, 2).reshape(-1, heads * KD)
        dcontent, dposition = own(dstat[:, 0], 1), own(dstat[:, 1], 1)
    pack_rows = pack_summed.shape[0]
    mouse_start = tiles_human * TILE
    shape3 = (windows, bins, width)
    return (
        join(trunk_out).reshape(shape3),
        loss[0] + tokens[-1][0, 0],
        join(grad_inputs).reshape(shape3),
        own(dgain1),
        own(dbias1),
        pack_summed[:, :, VD + KD :].reshape(pack_rows, heads * KD),
        pack_summed[:, :, VD : VD + KD].reshape(pack_rows, heads * KD),
        pack_summed[:, :, :VD].reshape(pack_rows, heads * VD),
        rel_rows,
        dcontent,
        dposition,
        dw_out.T,
        own(db_out),
        own(dgain2),
        own(dbias2),
        dw_in,
        db_in,
        dw_hid.T,
        own(db_hid),
        results["human"].T,
        dtracks[:track_human],
        results["mouse"].T,
        dtracks[mouse_start : mouse_start + track_mouse],
    )


def solution(mesh):
    in_specs = (
        P("dp", "seq", None),
        P(),
        P(),
        P(None, "mp"),
        P(None, "mp"),
        P(None, "mp"),
        P(None, "mp"),
        P("mp", None),
        P("mp", None),
        P("mp", None),
        P(),
        P(),
        P(),
        P(None, "mp"),
        P("mp"),
        P("mp", None),
        P(),
        P("mp", None),
        P(),
        P("mp", None),
        P(),
        P("dp"),
        P("dp", "seq", None),
        P("dp", "seq", None),
    )
    out_specs = (
        P("dp", "seq", None),
        P(),
        P("dp", "seq", None),
        P(("dp", "seq")),
        P(("dp", "seq")),
        P(("dp", "seq"), "mp"),
        P(("dp", "seq"), "mp"),
        P(("dp", "seq"), "mp"),
        P(("dp", "seq"), "mp"),
        P("mp", ("dp", "seq")),
        P("mp", ("dp", "seq")),
        P("mp", ("dp", "seq")),
        P(("dp", "seq")),
        P(("dp", "seq")),
        P(("dp", "seq")),
        P(("dp", "seq"), "mp"),
        P("mp"),
        P("mp", ("dp", "seq")),
        P(("dp", "seq")),
        P("mp", None),
        P(),
        P("mp", None),
        P(),
    )
    return jax.shard_map(
        on_device, mesh=mesh, in_specs=in_specs, out_specs=out_specs, check_vma=False
    )
```

```python
import math

import jax
import jax.numpy as jnp
from jax import lax
from jax.experimental import pallas as pl
from jax.experimental.pallas import tpu as pltpu
from jax.sharding import PartitionSpec as P

KD = 64
VD = 192
FEAT = 192
BINS = 1536
CROP = 896


norm_eps = 1e-05
log_eps = 1e-07
exact_mode = lax.Precision.HIGHEST


def rel_basis():
    per_class = FEAT // 6
    distance = jnp.arange(-(BINS - 1), BINS).astype(jnp.float32)
    magnitude = jnp.abs(distance)[:, None]
    half_life = (2.0 ** jnp.linspace(3.0, math.log2(BINS), per_class)).astype(jnp.float32)
    decays = jnp.exp(-math.log(2.0) / half_life[None, :] * magnitude)
    widths = (2.0 ** jnp.arange(1, per_class + 1)).astype(jnp.float32) - 1.0
    central = (widths[None, :] > magnitude).astype(jnp.float32)
    spread = BINS / (2.0 * per_class)
    centre = jnp.linspace(BINS / per_class, BINS, per_class).astype(jnp.float32)
    concentration = (centre / spread) ** 2
    rate_param = centre / spread**2
    peak_at = (concentration - 1.0) / rate_param
    log_ratio = (concentration - 1.0) * (
        jnp.log(jnp.maximum(magnitude, 1e-20)) - jnp.log(peak_at)
    ) - rate_param * (magnitude - peak_at)
    density = jnp.exp(log_ratio)
    gammas = density / jnp.max(density, axis=0, keepdims=True)
    symmetric = jnp.concatenate([decays, central, gammas], axis=1)
    return jnp.concatenate([symmetric, jnp.sign(distance)[:, None] * symmetric], axis=1)


PACK = VD + 3 * KD
GRAD_PACK = VD + 2 * KD
TILE = 896
NN = (((1,), (0,)), ((), ()))
NT = (((1,), (1,)), ((), ()))
TN = (((0,), (0,)), ((), ()))


def mxu(left_arr, right_arr, dims, precision=None):
    return lax.dot_general(
        left_arr, right_arr, dims, precision=precision, preferred_element_type=jnp.float32
    )


def query_block(bins):
    for block in (384, 256, 128):
        if bins % block == 0:
            return block
    return bins


def attend_forward_kernel(block, bins, pack_ref, rel_ref, out_ref, probs_ref):
    step = pl.program_id(0)
    span = bins + block
    query = pack_ref[pl.ds(pl.multiple_of(step * block, block), block), VD + KD :]
    base = pl.multiple_of(bins - block - step * block, block)
    content = mxu(query[:, :KD], pack_ref[:, VD : VD + KD], NT)
    position = mxu(query[:, KD:], rel_ref[pl.ds(base, span), :], NT)
    position = pltpu.roll(position, span - (block - 1), 1, stride=1, stride_axis=0)
    scores = content + position[:, :bins]
    exps = jnp.exp(scores - jnp.max(scores, axis=1, keepdims=True))
    probs = (exps * (1.0 / jnp.sum(exps, axis=1, keepdims=True))).astype(jnp.bfloat16)
    probs_ref[...] = probs
    out_ref[0] = mxu(probs, pack_ref[:, :VD], NN).T.astype(jnp.bfloat16)


def attend_forward(pack, rel):
    bins = pack.shape[0]
    block = query_block(bins)
    steps = bins // block
    return pl.pallas_call(
        lambda *refs: attend_forward_kernel(block, bins, *refs),
        grid=(steps,),
        in_specs=[
            pl.BlockSpec((bins, PACK), lambda i: (0, 0)),
            pl.BlockSpec((2 * bins, KD), lambda i: (0, 0)),
        ],
        out_specs=[
            pl.BlockSpec((1, VD, block), lambda i: (i, 0, 0)),
            pl.BlockSpec((block, bins), lambda i: (i, 0)),
        ],
        out_shape=[
            jax.ShapeDtypeStruct((steps, VD, block), jnp.bfloat16),
            jax.ShapeDtypeStruct((bins, bins), jnp.bfloat16),
        ],
        compiler_params=pltpu.CompilerParams(vmem_limit_bytes=48 << 20),
        cost_estimate=pl.CostEstimate(flops=1, bytes_accessed=1, transcendentals=0),
        name="attend_forward",
    )(pack, rel)


def attend_backward_kernel(
    block, bins, pack_ref, rel_ref, probs_ref, grad_ref, out_ref, drel_ref, stat_ref, acc_ref
):
    step = pl.program_id(0)
    steps = bins // block
    span = bins + block

    @pl.when(step == 0)
    def _():
        acc_ref[...] = jnp.zeros_like(acc_ref)
        drel_ref[...] = jnp.zeros_like(drel_ref)
        stat_ref[...] = jnp.zeros_like(stat_ref)

    query = pack_ref[pl.ds(pl.multiple_of(step * block, block), block), VD + KD :]
    base = pl.multiple_of(bins - block - step * block, block)
    grad_t = grad_ref[0]
    probs = probs_ref[...]
    acc_ref[:VD, :] += mxu(grad_t, probs, NN)
    grad_probs = mxu(grad_t.T, pack_ref[:, :VD], NT)
    wide = probs.astype(jnp.float32)
    scaled = wide * grad_probs
    delta = jnp.sum(scaled, axis=1, keepdims=True)
    grad_scores = (scaled - wide * delta).astype(jnp.bfloat16)
    grad_qc = mxu(grad_scores, pack_ref[:, VD : VD + KD], NN)
    query_t = query.T
    acc_ref[VD:, :] += mxu(query_t[:KD], grad_scores, NN)
    row = lax.broadcasted_iota(jnp.int32, (block, block), 0)
    col = lax.broadcasted_iota(jnp.int32, (block, block), 1)
    flip = (row + col == block - 1).astype(jnp.bfloat16)
    turned = mxu(flip, grad_scores, NN)
    turned = jnp.concatenate([turned, jnp.zeros((block, block), jnp.float32)], axis=1)
    turned = pltpu.roll(turned, 0, 1, stride=1, stride_axis=0).astype(jnp.bfloat16)
    grad_qp = mxu(
        flip.astype(jnp.float32),
        mxu(turned, rel_ref[pl.ds(base, span), :], NN),
        NN,
        exact_mode,
    )
    pos_turned = mxu(query_t[KD:], flip, NN).astype(jnp.bfloat16)
    drel_ref[:, pl.ds(base, span)] += mxu(pos_turned, turned, NN)
    stat_ref[0:1, :KD] += jnp.sum(grad_qc, axis=0, keepdims=True)
    stat_ref[1:2, :KD] += jnp.sum(grad_qp, axis=0, keepdims=True)
    out_ref[pl.ds(step, 1), VD + KD :, :] = (
        ((grad_qc + grad_qp) * (KD**-0.5)).T.astype(jnp.bfloat16)[None]
    )

    @pl.when(step == steps - 1)
    def _():
        for part in range(steps):
            out_ref[part, : VD + KD, :] = acc_ref[:, part * block : (part + 1) * block].astype(
                jnp.bfloat16
            )


def attend_backward(pack, rel, probs, grad):
    bins = pack.shape[0]
    block = query_block(bins)
    steps = bins // block
    return pl.pallas_call(
        lambda *refs: attend_backward_kernel(block, bins, *refs),
        grid=(steps,),
        in_specs=[
            pl.BlockSpec((bins, PACK), lambda i: (0, 0)),
            pl.BlockSpec((2 * bins, KD), lambda i: (0, 0)),
            pl.BlockSpec((block, bins), lambda i: (i, 0)),
            pl.BlockSpec((1, VD, block), lambda i: (i, 0, 0)),
        ],
        out_specs=[
            pl.BlockSpec((steps, GRAD_PACK, block), lambda i: (0, 0, 0)),
            pl.BlockSpec((KD, 2 * bins), lambda i: (0, 0)),
            pl.BlockSpec((8, 128), lambda i: (0, 0)),
        ],
        out_shape=[
            jax.ShapeDtypeStruct((steps, GRAD_PACK, block), jnp.bfloat16),
            jax.ShapeDtypeStruct((KD, 2 * bins), jnp.float32),
            jax.ShapeDtypeStruct((8, 128), jnp.float32),
        ],
        scratch_shapes=[pltpu.VMEM((VD + KD, bins), jnp.float32)],
        compiler_params=pltpu.CompilerParams(vmem_limit_bytes=48 << 20),
        cost_estimate=pl.CostEstimate(flops=1, bytes_accessed=1, transcendentals=0),
        name="attend_backward",
    )(pack, rel, probs, grad)


def heads_kernel(
    track_human,
    track_mouse,
    pick_ref,
    rows_ref,
    weight_ref,
    human_ref,
    mouse_ref,
    human_other_ref,
    mouse_other_ref,
    bias_ref,
    count_human_ref,
    count_mouse_ref,
    grad_ref,
    dtrunk_ref,
    dbias_ref,
    loss_ref,
):
    step = pl.program_id(0)
    kind, swapped = pick_ref[0], pick_ref[1] == 1

    @pl.when(step == 0)
    def _():
        dtrunk_ref[...] = jnp.zeros_like(dtrunk_ref)
        loss_ref[...] = jnp.zeros_like(loss_ref)

    def score(own_ref, other_ref, count_ref, tracks):
        valid = lax.broadcasted_iota(jnp.int32, (TILE, 1), 0) + step * TILE < tracks
        own = jnp.where(valid, own_ref[...], 0.0).astype(jnp.bfloat16)
        oth = jnp.where(valid, other_ref[...], 0.0).astype(jnp.bfloat16)
        head = jnp.concatenate(
            [jnp.where(swapped, oth, own), jnp.where(swapped, own, oth)], axis=1
        )
        logits = mxu(head, rows_ref[...], NT) + bias_ref[:, 0:1]
        counts = count_ref[0].astype(jnp.float32)
        small = jnp.exp(-jnp.abs(logits))
        inverse = 1.0 / (1.0 + small)
        predicted = jnp.maximum(logits, 0.0) + jnp.log1p(small)
        shifted = predicted + log_eps
        sigma = jnp.where(logits >= 0.0, 1.0, small) * inverse
        weight = jnp.where(valid, weight_ref[0:1, :], 0.0)
        rows_loss = weight * (predicted - counts * jnp.log(shifted))
        grad = weight * (sigma - counts * sigma / shifted)
        loss_ref[...] += jnp.sum(rows_loss.reshape(TILE // 8, 8, -1), axis=0)
        bins = grad.shape[1]
        if bins % 128 == 0:
            folded = sum(grad[:, i : i + 128] for i in range(0, bins, 128))
        else:
            folded = jnp.broadcast_to(jnp.sum(grad, axis=1, keepdims=True) / 128, (TILE, 128))
        dbias_ref[...] = jnp.sum(folded.T.reshape(16, 8, TILE), axis=0)
        grad_low = grad.astype(jnp.bfloat16)
        grad_ref[...] = grad_low
        dtrunk_ref[...] += mxu(grad_low.T, head, NN)

    @pl.when(jnp.logical_and(kind == 0, step < pl.cdiv(track_human, TILE)))
    def _():
        score(human_ref, human_other_ref, count_human_ref, track_human)

    @pl.when(jnp.logical_and(kind == 1, step < pl.cdiv(track_mouse, TILE)))
    def _():
        score(mouse_ref, mouse_other_ref, count_mouse_ref, track_mouse)


def score_heads(window, pick, rows, weight, own, others, bias, count_human, count_mouse):
    bins, width = rows.shape
    share = own[0].shape[1]
    rest = width - share
    track_human, track_mouse = count_human.shape[1], count_mouse.shape[1]
    tiles_human, tiles_mouse = pl.cdiv(track_human, TILE), pl.cdiv(track_mouse, TILE)

    def tile(kind, tiles):
        return lambda t, p: jnp.where(p[0] == kind, jnp.minimum(t, tiles - 1), 0)

    human_tile, mouse_tile = tile(0, tiles_human), tile(1, tiles_mouse)

    def out_tile(t, p):
        mine = jnp.where(p[0] == 0, jnp.minimum(t, tiles_human - 1), 0)
        return jnp.where(p[0] == 1, tiles_human + jnp.minimum(t, tiles_mouse - 1), mine)

    whole = lambda t, p: (0, 0)
    tracks = (tiles_human + tiles_mouse) * TILE
    return pl.pallas_call(
        lambda *refs: heads_kernel(track_human, track_mouse, *refs),
        grid_spec=pltpu.PrefetchScalarGridSpec(
            num_scalar_prefetch=1,
            grid=(max(tiles_human, tiles_mouse),),
            in_specs=[
                pl.BlockSpec((bins, width), whole),
                pl.BlockSpec((8, bins), whole),
                pl.BlockSpec((TILE, share), lambda t, p: (human_tile(t, p), 0)),
                pl.BlockSpec((TILE, share), lambda t, p: (mouse_tile(t, p), 0)),
                pl.BlockSpec((TILE, rest), lambda t, p: (human_tile(t, p), 0)),
                pl.BlockSpec((TILE, rest), lambda t, p: (mouse_tile(t, p), 0)),
                pl.BlockSpec((TILE, 128), lambda t, p: (out_tile(t, p), 0)),
                pl.BlockSpec((1, TILE, bins), lambda t, p: (window, human_tile(t, p), 0)),
                pl.BlockSpec((1, TILE, bins), lambda t, p: (window, mouse_tile(t, p), 0)),
            ],
            out_specs=[
                pl.BlockSpec((TILE, bins), lambda t, p: (out_tile(t, p), 0)),
                pl.BlockSpec((bins, width), whole),
                pl.BlockSpec((8, TILE), lambda t, p: (0, out_tile(t, p))),
                pl.BlockSpec((8, bins), whole),
            ],
        ),
        out_shape=[
            jax.ShapeDtypeStruct((tracks, bins), jnp.bfloat16),
            jax.ShapeDtypeStruct((bins, width), jnp.float32),
            jax.ShapeDtypeStruct((8, tracks), jnp.float32),
            jax.ShapeDtypeStruct((8, bins), jnp.float32),
        ],
        compiler_params=pltpu.CompilerParams(vmem_limit_bytes=56 << 20),
        cost_estimate=pl.CostEstimate(flops=1, bytes_accessed=1, transcendentals=0),
        name="score_heads",
    )(pick, rows, weight, *own, *others, bias, count_human, count_mouse)


def head_tile(step, parity, quarter):
    upper = jnp.where(step >= quarter, 1, 0)
    return upper * quarter + parity * quarter + step


def head_grads_kernel(windows, tiles_human, quarter, has_more, pick_ref, *refs):
    grads, rows, out_ref, acc_ref = refs[:windows], refs[windows], refs[-2], refs[-1]
    tile = head_tile(pl.program_id(0), pick_ref[windows], quarter)
    mine = jnp.where(tile < tiles_human, 0, 1)
    acc_ref[...] = refs[windows + 1][...].astype(jnp.float32) if has_more else jnp.zeros_like(acc_ref)
    for window in range(windows):

        @pl.when(pick_ref[window] == mine)
        def _():
            acc_ref[...] += mxu(grads[window][...], rows[window], NN)

    out_ref[...] = acc_ref[...].astype(jnp.bfloat16)


def head_grads(pick, grads, rows, tiles_human, tiles, more=None):
    windows, bins, share = rows.shape
    last = grads[0].shape[0] // TILE - 1

    def tile_of(window):
        def index(t, p):
            tile = head_tile(t, p[windows], tiles // 2)
            kept = jnp.where(p[window] == 0, jnp.minimum(tile, tiles_human - 1), 0)
            kept = jnp.where(p[window] == 1, jnp.maximum(tile, tiles_human), kept)
            return (jnp.minimum(kept, last), 0)

        return index

    extra = [] if more is None else [more]
    return pl.pallas_call(
        lambda *refs: head_grads_kernel(
            windows, tiles_human, tiles // 2, more is not None, *refs
        ),
        grid_spec=pltpu.PrefetchScalarGridSpec(
            num_scalar_prefetch=1,
            grid=(tiles,),
            in_specs=[pl.BlockSpec((TILE, bins), tile_of(w)) for w in range(windows)]
            + [pl.BlockSpec((windows, bins, share), lambda t, p: (0, 0, 0))]
            + [pl.BlockSpec((TILE, share), lambda t, p: (t, 0))] * len(extra),
            out_specs=pl.BlockSpec((TILE, share), lambda t, p: (t, 0)),
            scratch_shapes=[pltpu.VMEM((TILE, share), jnp.float32)],
        ),
        out_shape=jax.ShapeDtypeStruct((tiles * TILE, share), jnp.bfloat16),
        compiler_params=pltpu.CompilerParams(vmem_limit_bytes=40 << 20),
        cost_estimate=pl.CostEstimate(flops=1, bytes_accessed=1, transcendentals=0),
        name="head_grads",
    )(pick, *grads, rows, *extra)


def half_product_kernel(windows, turned, has_more, pick_ref, *refs):
    lefts, rights, out_ref = refs[:windows], refs[windows : 2 * windows], refs[-1]
    total = None
    for left, right in zip(lefts, rights):
        if turned:
            term = mxu(right[...], left[...], NN)
        else:
            term = mxu(left[...], right[...], TN)
        total = term if total is None else total + term
    if turned:
        total = total.T
    if has_more:
        total = total + refs[2 * windows][...].astype(jnp.float32)
    out_ref[...] = total.astype(jnp.bfloat16)


def half_product(half, lefts, rights, slabs, turned, more=None):
    windows = len(lefts)
    rows, width = lefts[0].shape
    slab = width // slabs
    cols = rights[0].shape[0 if turned else 1]
    step = cols
    while step > 768 and step % 256 == 0:
        step //= 2
    left_spec = pl.BlockSpec((rows, slab), lambda u, j, p: (0, 2 * u + p[0]))
    if turned:
        right_spec = pl.BlockSpec((step, rows), lambda u, j, p: (j, 0))
    else:
        right_spec = pl.BlockSpec((rows, step), lambda u, j, p: (0, j))
    out_spec = pl.BlockSpec((slab, step), lambda u, j, p: (u, j))
    extra = [] if more is None else [more]
    return pl.pallas_call(
        lambda *refs: half_product_kernel(windows, turned, more is not None, *refs),
        grid_spec=pltpu.PrefetchScalarGridSpec(
            num_scalar_prefetch=1,
            grid=(slabs // 2, cols // step),
            in_specs=[left_spec] * windows + [right_spec] * windows + [out_spec] * len(extra),
            out_specs=out_spec,
        ),
        out_shape=jax.ShapeDtypeStruct((width // 2, cols), jnp.bfloat16),
        compiler_params=pltpu.CompilerParams(vmem_limit_bytes=48 << 20),
        cost_estimate=pl.CostEstimate(flops=1, bytes_accessed=1, transcendentals=0),
        name="half_product",
    )(half, *lefts, *rights, *extra)


def norm_stats(values):
    mean = jnp.mean(values, axis=-1, keepdims=True)
    centred = values - mean
    inverse = lax.rsqrt(jnp.mean(centred * centred, axis=-1, keepdims=True) + norm_eps)
    return mean, inverse


def norm_backward(grad_output, scaled, inverse, norm_gain):
    grad_scaled = grad_output * norm_gain
    mean_grad = jnp.mean(grad_scaled, axis=-1, keepdims=True)
    mean_proj = jnp.mean(grad_scaled * scaled, axis=-1, keepdims=True)
    grad_input = inverse * (grad_scaled - mean_grad - scaled * mean_proj)
    return (grad_input, jnp.sum(grad_output * scaled, axis=0), jnp.sum(grad_output, axis=0))


def sum_over_model(partial, done, after_line):
    low = done(partial.astype(jnp.bfloat16))
    if lax.axis_size("mp") == 2:
        other = lax.ppermute(low, "mp", [(0, 1), (1, 0)])
        return lambda: low.astype(jnp.float32) + after_line(other).astype(jnp.float32)
    total = lax.psum(low, "mp")
    return lambda: after_line(total).astype(jnp.float32)


def in_model_order(own, dim, after_line):
    if lax.axis_size("mp") == 2:
        first = lax.axis_index("mp") == 0
        other = lax.ppermute(own, "mp", [(0, 1), (1, 0)])

        def ordered():
            got = after_line(other)
            return jnp.concatenate(
                [jnp.where(first, own, got), jnp.where(first, got, own)], axis=dim
            )

        return ordered
    full = lax.all_gather(own, "mp", axis=dim, tiled=True)
    return lambda: after_line(full)


class OtherRows:
    def __init__(self, own, tile, after_line, done):
        self.after_line, self.done = after_line, done
        count = lax.axis_size("dp")
        size = -(-own.shape[0] // tile) * tile // count
        part = None
        for place in range(count - 1, -1, -1):
            piece = own[place * size : (place + 1) * size]
            piece = jnp.pad(piece, [(0, size - piece.shape[0]), (0, 0)])
            here = lax.axis_index("dp") == place
            part = piece if part is None else jnp.where(here, piece, part)
        self.mine = lax.ppermute(done(part), "mp", [(0, 1), (1, 0)])

    def share(self):
        self.full = lax.all_gather(
            self.done(self.after_line(self.mine)), "dp", axis=0, tiled=True
        )

    def finish(self):
        return self.after_line(self.full)


def swap_pairs(axis, step):
    return [(i, i ^ step) for i in range(lax.axis_size(axis))]


class SmallSums:
    def __init__(self, parts, axes, after_line, done):
        self.parts, self.after_line, self.done = parts, after_line, done
        padded = [jnp.pad(x.reshape(-1), (0, -x.size % 128)) for x in parts]
        self.total = jnp.concatenate(padded).reshape(-1, 128)
        self.moves = [
            (axis, 1 << bit)
            for axis in axes
            for bit in range(lax.axis_size(axis).bit_length() - 1)
        ]
        self.got = None
        self.step()

    def step(self):
        if self.got is not None:
            self.total, self.got = self.total + self.after_line(self.got), None
        if self.moves:
            axis, step = self.moves.pop(0)
            self.total = self.done(self.total)
            self.got = lax.ppermute(self.total, axis, swap_pairs(axis, step))

    def finish(self):
        while self.got is not None:
            self.step()
        results, start, total = [], 0, self.total.reshape(-1)
        for x in self.parts:
            results.append(total[start : start + x.size].reshape(x.shape))
            start += -(-x.size // 128) * 128
        return results


class SeqSum:
    def __init__(self, parts, done):
        self.got = lax.all_to_all(done(parts), "seq", split_axis=0, concat_axis=0, tiled=True)

    def arrive(self, after_line):
        self.got = after_line(self.got)

    def finish(self, after_line, done):
        return done(jnp.sum(after_line(self.got).astype(jnp.float32), axis=0))


class ScatterProduct:
    def __init__(self, lefts, rights, after_line, done, turned=False):
        self.after_line, self.done, self.turned = after_line, done, turned
        self.lefts, self.rights = lefts, rights
        lefts = [after_line(lefts[0])] + lefts[1:]
        self.got = lax.ppermute(done(self.half(1, lefts)), "dp", swap_pairs("dp", 1))

    def half(self, other, lefts, more=None):
        pick = jnp.reshape((lax.axis_index("dp") + other) % 2, (1,)).astype(jnp.int32)
        return half_product(pick, lefts, self.rights, lax.axis_size("dp"), self.turned, more)

    def keep(self):
        self.kept = self.done(self.half(0, self.lefts, self.after_line(self.got)))
        return self


class ScatterRest:
    def __init__(self, kept, after_line, done):
        self.after_line, self.done = after_line, done
        size = kept.shape[0] // 2
        upper = lax.axis_index("dp") // 2 == 1
        low, high = kept[:size], kept[size:]
        self.mine = jnp.where(upper, high, low)
        self.got = lax.ppermute(done(jnp.where(upper, low, high)), "dp", swap_pairs("dp", 2))

    def along_seq(self):
        got = self.after_line(self.got).astype(jnp.float32)
        total = (self.mine.astype(jnp.float32) + got).astype(jnp.bfloat16)
        parts = total.reshape(lax.axis_size("seq"), -1, total.shape[1])
        self.sum = SeqSum(parts, self.done)

    def arrive(self):
        self.sum.arrive(self.after_line)

    def finish(self):
        return self.sum.finish(self.after_line, self.done)


def on_device(
    trunk_in,
    norm1_gain,
    norm1_bias,
    w_query,
    w_key,
    w_value,
    w_rel,
    content_bias,
    pos_bias,
    w_out,
    b_out,
    norm2_gain,
    norm2_bias,
    w_in,
    b_in,
    w_hid,
    b_hid,
    head_human,
    bias_human,
    head_mouse,
    bias_mouse,
    species,
    targets_human,
    targets_mouse,
):
    windows, bins, width = trunk_in.shape
    heads = content_bias.shape[0]
    dp_size, seq_size, mp_size = (lax.axis_size(axis) for axis in ("dp", "seq", "mp"))
    seq_index, mp_index = lax.axis_index("seq"), lax.axis_index("mp")
    place = lax.axis_index("dp") * seq_size + seq_index
    places = dp_size * seq_size
    all_bins = bins * seq_size
    query_start = seq_index * bins
    key_scale = KD ** (-0.5)
    loss_scale = 1.0 / math.sqrt(windows * dp_size * CROP)
    crop_start = (all_bins - CROP) // 2
    bf16 = jnp.bfloat16
    me = jnp.reshape(seq_index, (1,)).astype(jnp.int32)

    groups = [[w] for w in range(windows)] if heads % seq_size == 0 else [list(range(windows))]
    group_size = len(groups[0])
    pairs = heads * group_size
    pairs_here = -(-pairs // seq_size)
    block = query_block(all_bins)
    pair_heads = [
        jnp.minimum((seq_index * pairs_here + j) // group_size, heads - 1)
        for j in range(pairs_here)
    ]

    tokens = [jnp.zeros((8, 128), jnp.float32)]

    def after_line(array):
        array, token = lax.optimization_barrier((array, tokens[-1]))
        tokens.append(token)
        return array

    done = after_line

    def exchange(array):
        return lax.all_to_all(array, "seq", split_axis=0, concat_axis=0, tiled=True)

    def spread(array):
        short = seq_size * pairs_here - pairs
        if short:
            array = jnp.pad(array, [(0, short)] + [(0, 0)] * (array.ndim - 1))
        return exchange(array.reshape((seq_size, pairs_here) + array.shape[1:]))

    def regroup(array, size):
        if array.shape[2] == size:
            return array
        depth = array.shape[1]
        array = array.transpose(1, 0, 2).reshape(depth, all_bins // size, size)
        return array.transpose(1, 0, 2)

    def to_owners(arrays):
        return exchange(jnp.stack([regroup(a, bins) for a in arrays], axis=1))

    def by_head(array):
        depth = array.shape[2]
        array = array.reshape(seq_size * pairs_here, depth, bins)[:pairs]
        array = array.reshape(heads, group_size, depth, bins).transpose(0, 2, 1, 3)
        return array.reshape(heads * depth, group_size * bins)

    track_human, track_mouse = head_human.shape[1], head_mouse.shape[1]
    own_heads = (head_human.T, head_mouse.T)
    parts = {}

    def fetch_out(_):
        if mp_size == 2:
            parts["out"] = OtherRows(w_out, w_out.shape[0], after_line, done)

    def fetch_out_share(_):
        if mp_size == 2:
            parts["out"].share()

    def fetch_out_end(_):
        if mp_size != 2:
            parts["w_out"] = lax.all_gather(w_out, "mp", axis=0, tiled=True)
            return
        other, first = parts["out"].finish(), mp_index == 0
        parts["w_out"] = done(
            jnp.concatenate(
                [jnp.where(first, w_out, other), jnp.where(first, other, w_out)], axis=0
            )
        )

    def fetch_heads(_):
        if mp_size == 2:
            parts["heads"] = [OtherRows(own, TILE, after_line, done) for own in own_heads]

    def fetch_human_share(_):
        if mp_size == 2:
            parts["heads"][0].share()

    def fetch_mouse_share(_):
        if mp_size == 2:
            parts["heads"][1].share()

    def fetch_heads_end(_):
        if mp_size == 2:
            parts["others"] = [part.finish() for part in parts["heads"]]
            parts["own"] = own_heads
            return
        full = [lax.all_gather(own, "mp", axis=1, tiled=True) for own in own_heads]
        parts["own"] = [x[:, : width // 2] for x in full]
        parts["others"] = [x[:, width // 2 :] for x in full]

    def of_head(weight, size, h):
        return weight[:, h * size : (h + 1) * size]

    w_packs = [
        jnp.concatenate(
            [of_head(w_value, VD, h), of_head(w_key, KD, h)] + [of_head(w_query, KD, h)] * 2, axis=1
        )
        for h in range(heads)
    ]

    def grad_weights(_):
        parts["w_grad"] = done(jnp.concatenate([w[:, :GRAD_PACK] for w in w_packs], axis=1))

    pack_scale = jnp.concatenate(
        [jnp.ones((VD + KD,), jnp.float32), jnp.full((2 * KD,), key_scale, jnp.float32)]
    )
    pack_biases = [
        jnp.concatenate([jnp.zeros((VD + KD,), jnp.float32), content_bias[h], pos_bias[h]])
        for h in range(heads)
    ]

    basis = jnp.pad(rel_basis(), [(0, 1), (0, 0)])
    w_rel_heads = w_rel.reshape(FEAT, heads, KD)
    rels = [
        mxu(
            basis,
            lax.dynamic_index_in_dim(w_rel_heads, head, 1, keepdims=False).astype(jnp.float32),
            NN,
            exact_mode,
        ).astype(bf16)
        for head in pair_heads
    ]

    count = len(groups)
    many = lambda: [None] * count
    trunk, stats1, normed1, packs, probs, attended = many(), many(), many(), many(), many(), many()
    mids, stats2, normed2, preacts, actives = many(), many(), many(), many(), many()
    trunk_out, grad_trunks, grad_outs, grad_pres = many(), many(), many(), many()
    grad_mids, grad_mid_lows, packed_grads, grad_inputs = many(), many(), many(), many()
    moving, grad_att, own_rows = many(), many(), [None] * windows
    logit_grads, track_sums, losses = [None] * windows, [], []
    sums = [0.0] * 5
    sums1 = [0.0, 0.0]
    drels = [0.0] * pairs_here
    dstats = [0.0] * pairs_here

    def project(g):
        rows = group_size * bins
        values = trunk_in[groups[g][0] : groups[g][-1] + 1].reshape(rows, width).astype(jnp.float32)
        mean, inverse = norm_stats(values)
        normed = ((values - mean) * inverse * norm1_gain + norm1_bias).astype(bf16)
        normed = after_line(normed)
        trunk[g], stats1[g], normed1[g] = values, (mean, inverse), normed
        parts = []
        for h in range(heads):
            pack = (mxu(normed, w_packs[h], NN) * pack_scale + pack_biases[h]).astype(bf16)
            parts.append(pack.reshape(group_size, bins, PACK))
        pack = spread(done(jnp.concatenate(parts, axis=0)))
        packs[g] = pack

    def arrive(g):
        packs[g] = after_line(packs[g])

    def arrive_out(g):
        moving[g] = after_line(moving[g])

    def arrive_grad(g):
        grad_att[g] = after_line(grad_att[g])

    def arrive_packed(g):
        packed_grads[g] = by_head(after_line(packed_grads[g]))

    def attend(g):
        outs, kept = [], []
        pack = after_line(packs[g])
        packs[g] = [pack[:, j].reshape(all_bins, PACK) for j in range(pairs_here)]
        for j in range(pairs_here):
            out, prob = attend_forward(packs[g][j], rels[j])
            outs.append(done(out))
            kept.append(prob)
        probs[g] = kept
        moving[g] = to_owners(outs)

    def attend_swap(g):
        attended[g] = done(by_head(after_line(moving[g])))
        moving[g] = in_model_order(attended[g], 0, after_line)

    def feed_forward(g):
        mid = trunk[g] + mxu(moving[g](), parts["w_out"], TN) + b_out
        mean, inverse = norm_stats(mid)
        normed = ((mid - mean) * inverse * norm2_gain + norm2_bias).astype(bf16)
        preact = mxu(normed, w_in, NN) + b_in
        active = jnp.maximum(preact, 0.0).astype(bf16)
        mids[g], stats2[g], normed2[g], actives[g] = mid, (mean, inverse), normed, active
        moving[g] = sum_over_model(mxu(active, w_hid, NN), done, after_line)

    def score(g):
        out = mids[g] + (moving[g]() + b_hid)
        trunk_out[g] = out
        low = out.astype(bf16)
        grads = []
        for i, window in enumerate(groups[g]):
            rows = low[i * bins : (i + 1) * bins]
            own_rows[window] = lax.dynamic_slice_in_dim(rows, mp_index * share, share, 1)
            pick = jnp.stack([picks[window], jnp.int32(0) + order])
            logit_grads[window], grad_out, track_sum, loss = score_heads(
                window, pick, rows, weight, parts["own"], parts["others"], bias_rows[0], count_human, count_mouse
            )
            track = jnp.sum(track_sum, axis=0)
            scored = jnp.arange(track.size) < tiles_human * TILE
            scored = scored == (picks[window] == 0)
            track_sums.append(jnp.where(scored & (picks[window] < 2), track, 0.0))
            losses.append(jnp.sum(loss))
            grads.append(grad_out)
        grad_trunks[g] = done(jnp.concatenate(grads, axis=0))

    def back_hidden(g):
        grad_out = after_line(grad_trunks[g].astype(bf16))
        grad_preact = jnp.where(actives[g] > 0, mxu(grad_out, w_hid, NT), 0.0)
        grad_pre = grad_preact.astype(bf16)
        grad_outs[g], grad_pres[g] = grad_out, grad_pre
        sums[3] = sums[3] + jnp.sum(grad_trunks[g], axis=0)
        sums[4] = sums[4] + jnp.sum(grad_preact, axis=0)
        moving[g] = sum_over_model(mxu(grad_pre, w_in, NT), done, after_line)

    def back_mid(g):
        mean, inverse = stats2[g]
        grad_normed = moving[g]()
        grad_norm, dgain, dbias = norm_backward(
            grad_normed, (mids[g] - mean) * inverse, inverse, norm2_gain
        )
        grad_mids[g] = grad_trunks[g] + grad_norm
        grad_mid_lows[g] = grad_mids[g].astype(bf16)
        sums[0] = sums[0] + dgain
        sums[1] = sums[1] + dbias
        sums[2] = sums[2] + jnp.sum(grad_mids[g], axis=0)
        grad = done(mxu(w_out, grad_mid_lows[g], NT).astype(bf16))
        grad = grad.reshape(heads, VD, group_size, bins).transpose(0, 2, 1, 3)
        grad_att[g] = spread(grad.reshape(pairs, VD, bins))

    def back_attend(g):
        outs = []
        grad = after_line(grad_att[g])
        for j in range(pairs_here):
            out, drel, stat = attend_backward(
                packs[g][j], rels[j], probs[g][j], regroup(grad[:, j], block)
            )
            outs.append(done(out))
            drels[j] = drels[j] + drel
            dstats[j] = dstats[j] + stat
        packed_grads[g] = to_owners(outs)

    def back_project(g):
        packed_grads[g] = after_line(packed_grads[g])
        product = lax.dot_general(
            packed_grads[g],
            parts["w_grad"],
            (((0,), (1,)), ((), ())),
            preferred_element_type=jnp.float32,
        )
        moving[g] = sum_over_model(product, done, after_line)

    def back_input(g):
        mean, inverse = stats1[g]
        grad_norm, dgain, dbias = norm_backward(
            moving[g](), (trunk[g] - mean) * inverse, inverse, norm1_gain
        )
        sums1[0] = sums1[0] + dgain
        sums1[1] = sums1[1] + dbias
        grad_inputs[g] = (grad_mids[g] + grad_norm).reshape(group_size, bins, width)

    bin_place = query_start + jnp.arange(bins)
    in_crop = ((bin_place >= crop_start) & (bin_place < crop_start + CROP)).astype(jnp.float32)
    weight = jnp.broadcast_to((in_crop * loss_scale)[None, :], (8, bins))
    has_crop = (query_start + bins > crop_start) & (query_start < crop_start + CROP)
    picks = jnp.where(has_crop, species, 2)
    count_human = targets_human.transpose(0, 2, 1)
    count_mouse = targets_mouse.transpose(0, 2, 1)
    tiles_human, tiles_mouse = pl.cdiv(track_human, TILE), pl.cdiv(track_mouse, TILE)
    half_tiles = (tiles_human + tiles_mouse) // 2
    bias_all = jnp.concatenate(
        [
            jnp.pad(bias_human, (0, tiles_human * TILE - track_human)),
            jnp.pad(bias_mouse, (0, tiles_mouse * TILE - track_mouse)),
        ]
    )
    bias_rows = []

    def spread_bias(_):
        wide = jnp.broadcast_to(after_line(bias_all)[:, None], (bias_all.size, 128))
        bias_rows.append(done(wide))

    order = mp_index if mp_size == 2 else 0
    share = head_human.shape[0]
    join = lambda arrays: jnp.concatenate(arrays, axis=0)
    results = {}
    width_out = heads * VD

    def pick_half(half):
        return jnp.concatenate([picks, jnp.reshape(half, (1,)).astype(jnp.int32)])

    def grads_heads(_):
        parity = lax.axis_index("dp") % 2
        rows = jnp.stack(own_rows)
        grads = [after_line(logit_grads[0])] + logit_grads[1:]
        sent = head_grads(pick_half(1 - parity), grads, rows, tiles_human, half_tiles)
        got = lax.ppermute(done(sent), "dp", swap_pairs("dp", 1))
        results["heads"] = (grads, rows, got, parity)

    def grads_heads_keep(_):
        grads, rows, got, parity = results["heads"]
        kept = done(
            head_grads(pick_half(parity), grads, rows, tiles_human, half_tiles, after_line(got))
        )
        results["heads"] = ScatterRest(kept, after_line, done)

    def grads_heads_seq(_):
        results["heads"].along_seq()

    def heads_arrive(_):
        results["heads"].arrive()

    def wide_arrive(_):
        results["wide"].arrive()

    def grads_heads_end(_):
        total = results["heads"].finish().astype(bf16)
        results["heads"] = lax.all_gather(total, ("dp", "seq"), axis=0, tiled=True)

    def grads_in(_):
        results["in"] = ScatterProduct(normed2, grad_pres, after_line, done)

    def grads_hid(_):
        results["hid"] = ScatterProduct(grad_outs, actives, after_line, done)

    def grads_in_keep(_):
        results["in"].keep()

    def grads_hid_keep(_):
        results["hid"].keep()
        kept = jnp.concatenate([results["in"].kept, results["hid"].kept], axis=1)
        results["wide"] = ScatterRest(kept, after_line, done)

    def grads_wide_seq(_):
        results["wide"].along_seq()

    def grads_wide_end(_):
        results["wide"] = results["wide"].finish()

    def grads_out(_):
        results["out"] = ScatterProduct(grad_mid_lows, attended, after_line, done, True)

    def grads_out_keep(_):
        results["out"].keep()

    def grads_pack(_):
        results["pack"] = ScatterProduct(normed1, packed_grads, after_line, done, True)

    def grads_pack_keep(_):
        kept = jnp.concatenate([results["out"].kept, results["pack"].keep().kept], axis=1)
        results["late_rows"] = ScatterRest(kept, after_line, done)

    def grads_pack_seq(_):
        results["late_rows"].along_seq()

    def grads_pack_end(_):
        late = results["late_rows"].finish()
        results["out"], results["pack"] = late[:, :width_out], late[:, width_out:]

    def sums_heads(_):
        dw_rel = jnp.zeros((heads, FEAT, KD), jnp.float32)
        dstat = jnp.zeros((heads, 2, KD), jnp.float32)
        for j, head in enumerate(pair_heads):
            part = lax.dot_general(
                basis,
                drels[j],
                (((0,), (1,)), ((), ())),
                precision=exact_mode,
                preferred_element_type=jnp.float32,
            )
            mine = (jnp.arange(heads) == head).astype(jnp.float32)[:, None, None]
            dw_rel = dw_rel + mine * part
            dstat = dstat + mine * dstats[j][None, :2, :KD]
        values = [part, dstats[0]] if heads == seq_size else [dstat, dw_rel]
        axes = ("dp",) if heads == seq_size else ("dp", "seq")
        results["own_head"] = SmallSums(values, axes, after_line, done)

    def sums_late(_):
        values = list(sums1) + list(sums) + [sum(track_sums), sum(losses)[None]]
        results["late"] = SmallSums(values, ("dp", "seq"), after_line, done)

    def step_heads(_):
        results["own_head"].step()

    def step_late(_):
        results["late"].step()

    def heads_out(_):
        full = after_line(results["heads"])
        first = tiles_human * TILE
        results["human"] = done(full[:track_human].astype(jnp.float32))
        results["mouse"] = done(full[first : first + track_mouse].astype(jnp.float32))

    def each(stage):
        return [(stage, g) for g in range(count)]

    def one(*stages):
        return [(stage, -1) for stage in stages]

    if count == 3:
        plan = one(fetch_out) + [(project, 0)] + one(fetch_out_share, fetch_heads)
        plan += [(project, 1), (project, 2)] + one(spread_bias) + [(attend, 0), (attend, 1)]
        plan += one(fetch_human_share, grad_weights) + [(attend_swap, 0)] + one(fetch_out_end)
        plan += [(feed_forward, 0)] + one(fetch_mouse_share) + [(attend, 2), (attend_swap, 1)]
        plan += [(feed_forward, 1), (attend_swap, 2)] + one(fetch_heads_end)
        plan += [(score, 0), (feed_forward, 2), (back_hidden, 0)]
        plan += [(score, 1), (back_hidden, 1), (back_mid, 0), (score, 2), (arrive_grad, 0)]
        plan += one(grads_heads) + [(back_attend, 0), (back_hidden, 2)] + one(grads_heads_keep)
        plan += [(back_mid, 1), (arrive_packed, 0), (back_project, 0)] + one(grads_in)
        plan += [(back_mid, 2), (arrive_grad, 1), (back_attend, 1)] + one(grads_hid, grads_in_keep)
        plan += [(arrive_grad, 2)] + one(grads_heads_seq) + [(back_attend, 2)]
        plan += one(grads_hid_keep) + [(back_input, 0)] + one(heads_arrive, grads_out)
        plan += one(sums_heads, grads_out_keep) + [(arrive_packed, 1), (back_project, 1)]
        plan += one(grads_wide_seq, step_heads) + [(arrive_packed, 2)] + one(grads_heads_end)
        plan += one(grads_pack) + [(back_project, 2)] + one(grads_pack_keep)
        plan += [(back_input, 1)] + one(wide_arrive, step_heads) + [(back_input, 2)]
        plan += one(sums_late, grads_pack_seq, step_late, grads_wide_end, step_late)
        plan += one(heads_out, step_late, grads_pack_end, step_late)
    else:
        plan = one(fetch_out, fetch_out_share, fetch_out_end, spread_bias, grad_weights)
        plan += one(fetch_heads, fetch_human_share, fetch_mouse_share, fetch_heads_end)
        plan += each(project) + each(attend) + each(attend_swap) + each(feed_forward) + each(score)
        plan += each(back_hidden) + each(back_mid)
        plan += one(grads_heads, grads_heads_keep, grads_heads_seq, grads_heads_end)
        plan += each(back_attend) + one(grads_in, grads_in_keep, grads_hid, grads_hid_keep)
        plan += one(grads_wide_seq, grads_wide_end, grads_out, grads_out_keep)
        plan += each(arrive_packed) + each(back_project) + one(grads_pack, grads_pack_keep)
        plan += one(grads_pack_seq, grads_pack_end) + each(back_input)
        plan += one(sums_heads, sums_late, heads_out)
    for stage, g in plan:
        stage(g)
    summed = results["late"].finish()
    dgain1, dbias1, dgain2, dbias2, db_out, db_hid, db_in, dtracks, loss = summed
    mids_sum = results["own_head"].finish()
    if heads == seq_size:
        share_rel, share_stat = FEAT // places, KD // places
        own_rel = mids_sum[0].reshape(dp_size, seq_size, share_rel * KD)
        own_stat = mids_sum[1][:2, :KD].reshape(2, dp_size, seq_size, share_stat)
        dp_here = lax.axis_index("dp")
        own_rel = lax.dynamic_index_in_dim(own_rel, dp_here, 0, keepdims=False)
        own_stat = lax.dynamic_index_in_dim(own_stat, dp_here, 1, keepdims=False)
        own_stat = own_stat.transpose(1, 0, 2).reshape(seq_size, 2 * share_stat)
        small = jnp.concatenate([own_rel, own_stat], axis=1)
        small = jnp.pad(small, [(0, 0), (0, -small.shape[1] % 128)])
        small = lax.all_to_all(small[:, None], "seq", split_axis=0, concat_axis=0, tiled=True)[:, 0]
        rel_rows = small[:, : share_rel * KD].reshape(heads, share_rel, KD)
        rel_rows = rel_rows.transpose(1, 0, 2).reshape(share_rel, heads * KD)
        stats = small[:, share_rel * KD : share_rel * KD + 2 * share_stat]
        dstat = stats.reshape(heads, 2, share_stat)
        dcontent, dposition = dstat[:, 0], dstat[:, 1]
    else:
        dstat, dw_rel = mids_sum
    dw_out = results["out"]
    dw_in, dw_hid = jnp.split(results["wide"], 2, axis=1)
    pack_summed = results["pack"].reshape(-1, heads, GRAD_PACK)
    def own(array, dim=0):
        size = array.shape[dim] // places
        return lax.dynamic_slice_in_dim(array, place * size, size, dim)

    if heads != seq_size:
        rel_rows = own(dw_rel, 1).transpose(1, 0, 2).reshape(-1, heads * KD)
        dcontent, dposition = own(dstat[:, 0], 1), own(dstat[:, 1], 1)
    pack_rows = pack_summed.shape[0]
    mouse_start = tiles_human * TILE
    shape3 = (windows, bins, width)
    return (
        join(trunk_out).reshape(shape3),
        loss[0] + tokens[-1][0, 0],
        join(grad_inputs).reshape(shape3),
        own(dgain1),
        own(dbias1),
        pack_summed[:, :, VD + KD :].reshape(pack_rows, heads * KD),
        pack_summed[:, :, VD : VD + KD].reshape(pack_rows, heads * KD),
        pack_summed[:, :, :VD].reshape(pack_rows, heads * VD),
        rel_rows,
        dcontent,
        dposition,
        dw_out.T,
        own(db_out),
        own(dgain2),
        own(dbias2),
        dw_in,
        db_in,
        dw_hid.T,
        own(db_hid),
        results["human"].T,
        dtracks[:track_human],
        results["mouse"].T,
        dtracks[mouse_start : mouse_start + track_mouse],
    )


def solution(mesh):
    in_specs = (
        P("dp", "seq", None),
        P(),
        P(),
        P(None, "mp"),
        P(None, "mp"),
        P(None, "mp"),
        P(None, "mp"),
        P("mp", None),
        P("mp", None),
        P("mp", None),
        P(),
        P(),
        P(),
        P(None, "mp"),
        P("mp"),
        P("mp", None),
        P(),
        P("mp", None),
        P(),
        P("mp", None),
        P(),
        P("dp"),
        P("dp", "seq", None),
        P("dp", "seq", None),
    )
    out_specs = (
        P("dp", "seq", None),
        P(),
        P("dp", "seq", None),
        P(("dp", "seq")),
        P(("dp", "seq")),
        P(("dp", "seq"), "mp"),
        P(("dp", "seq"), "mp"),
        P(("dp", "seq"), "mp"),
        P(("dp", "seq"), "mp"),
        P("mp", ("dp", "seq")),
        P("mp", ("dp", "seq")),
        P("mp", ("dp", "seq")),
        P(("dp", "seq")),
        P(("dp", "seq")),
        P(("dp", "seq")),
        P(("dp", "seq"), "mp"),
        P("mp"),
        P("mp", ("dp", "seq")),
        P(("dp", "seq")),
        P("mp", None),
        P(),
        P("mp", None),
        P(),
    )
    return jax.shard_map(
        on_device, mesh=mesh, in_specs=in_specs, out_specs=out_specs, check_vma=False
    )
```
